32 devices in a mesh: region: 8 (over z, x), chan: 4 (over y, core).
Axes of the slice: x: 2, y: 2, z: 4, core: 2. Of those that a mesh axis runs over, the one named last changes fastest.
Arguments:
- point_feats: bfloat16 [64, 131072], P('chan', 'region'), may hold values from -6 to 6
- destination: int32 [131072], P('region'), may hold values from 0 to 7, as said below
- voxel_slot: int32 [131072], P('region'), may hold values from 0 to 32767, as said below
- adjacency: int32 [512, 26], P('region'), may hold values from 0 to 512, as said below
- active_count: int32 [8], P('region'), may hold values from 4 to 64, as said below
- conv_weight: bfloat16 [64, 64, 3, 3, 3], P('chan'), may hold values from -0.15625 to 0.15625
- down_weight: bfloat16 [128, 64, 2, 2, 2], P(None, 'chan'), may hold values from -0.25 to 0.25
Outputs:
- coarse: bfloat16 [512, 8192], P('region', 'chan')
The draws below stay inside these ranges and needn't reach their ends.
Inputs may be any that keep to these rules, and one draw needn't show every extreme that they name: `destination`: each block of 16384 consecutive points names every region exactly 16384 / 8 times. Every point lies in an active brick of its region: voxel_slot // 512 < active_count[destination]. `adjacency`: entry n of row g names the brick at offset n from g, or 512 where that brick is inactive or off the map; rows of inactive slots hold only 512; the relation is symmetric. A neighbour at dx = 0 lies in g's own region, one at dx = -1 in that region or the previous one, one at dx = +1 in that region or the next one. In every region at most 16 active bricks have a neighbour in the next region and at most 16 in the previous one, and some region reaches 16 for each side. A region's active bricks fill its slots 0 to active_count - 1; some region fills all 64.
All inputs are finite; a program needn't handle non-finite values.
Results may differ from the reference program's by a relative error of at most 0.0053.
Values may be sent and summed in bfloat16 or wider, within the bound.
No kernel may reach another device: no remote copies, remote signals or barrier semaphores. Data moves between devices by JAX's collectives and lax.ppermute only.
A program may use at most 128 MiB of HBM per device.

```python
import jax
import jax.numpy as jnp
from jax import lax

C_IN = 64
C_MID = 64
C_OUT = 128
SPAN_X = 4
SPAN_Y = 4
SPAN_Z = 4
PTS_DEV = 16384
SLOTS = 64
BRICKS_ALL = 512
POINTS = 131072
N_REGION = 8


OFFSETS = [(first, second, third) for first in (-1, 0, 1) for second in (-1, 0, 1) for third in (-1, 0, 1) if (first, second, third) != (0, 0, 0)]


def geometry(key):
    base_key = jax.random.fold_in(key, 7)
    count_key, order_key = jax.random.split(base_key)
    lowest = max(SLOTS // 16, 1)
    spread = max(SLOTS - lowest, 1)
    uniform = jax.random.randint(count_key, (N_REGION,), 0, SLOTS - lowest + 1)
    counts = lowest + uniform * uniform // spread
    counts = counts.at[0].set(SLOTS).at[1].set(SLOTS)
    orders = jax.vmap(lambda single: jax.random.permutation(single, SLOTS))(jax.random.split(order_key, N_REGION)).astype(jnp.int32)
    inverse = jnp.argsort(orders, axis=1).astype(jnp.int32)
    return (counts.astype(jnp.int32), orders, inverse)


def destinations(key):
    per_region = PTS_DEV // N_REGION
    labels = jnp.arange(PTS_DEV, dtype=jnp.int32) // per_region
    region_keys = jax.random.split(jax.random.fold_in(key, 11), N_REGION)
    return jax.vmap(lambda single: jax.random.permutation(single, labels))(region_keys).reshape(-1).astype(jnp.int32)


def draw_destination(key, part):
    return destinations(key)


def draw_voxel_slot(key, part):
    counts, orders, inverse = geometry(key)
    targets = destinations(key)
    slot_key, within_key = jax.random.split(jax.random.fold_in(key, 13))
    bricks = jax.random.randint(slot_key, targets.shape, 0, counts[targets])
    within = jax.random.randint(within_key, targets.shape, 0, 512)
    values = (bricks * 512 + within).astype(jnp.int32)
    top_place = jnp.argmax(targets == 0).astype(jnp.int32)
    low_place = jnp.argmax(targets == 1).astype(jnp.int32)
    values = values.at[top_place].set(SLOTS * 512 - 1).at[low_place].set(0)
    return values.astype(jnp.int32)


def draw_active_count(key, part):
    return geometry(key)[0]


def draw_adjacency(key, part):
    counts, orders, inverse = geometry(key)
    face_cells = SPAN_Y * SPAN_Z
    local_x = orders // face_cells
    local_y = orders // SPAN_Z % SPAN_Y
    local_z = orders % SPAN_Z
    regions = jnp.arange(N_REGION, dtype=jnp.int32)[:, None]
    active = jnp.arange(SLOTS, dtype=jnp.int32)[None, :] < counts[:, None]
    columns = []
    for step_x, step_y, step_z in OFFSETS:
        global_x = regions * SPAN_X + local_x + step_x
        near_y = local_y + step_y
        near_z = local_z + step_z
        inside = (global_x >= 0) & (global_x < N_REGION * SPAN_X) & (near_y >= 0) & (near_y < SPAN_Y) & (near_z >= 0) & (near_z < SPAN_Z)
        clip_x = jnp.clip(global_x, 0, N_REGION * SPAN_X - 1)
        other_region = clip_x // SPAN_X
        cell_index = (clip_x % SPAN_X * SPAN_Y + jnp.clip(near_y, 0, SPAN_Y - 1)) * SPAN_Z + jnp.clip(near_z, 0, SPAN_Z - 1)
        other_slot = inverse[other_region, cell_index]
        linked = inside & active & (other_slot < counts[other_region])
        columns.append(jnp.where(linked, other_region * SLOTS + other_slot, N_REGION * SLOTS))
    return jnp.stack(columns, axis=-1).reshape(N_REGION * SLOTS, 26).astype(jnp.int32)


def level_of(key, dims, shards, smallest, largest):
    gain = 1.0
    for axis_at, shards_of in shards:
        draws = jax.random.uniform(jax.random.fold_in(jax.random.fold_in(key, 6), axis_at), (shards_of,), jnp.float32, smallest / len(shards), largest / len(shards))
        gain = gain * jnp.repeat(jnp.exp(draws), dims[axis_at] // shards_of).reshape((-1,) + (1,) * (len(dims) - 1 - axis_at))
    return gain


def normal_values(key, dims, width, limit, shards=(), held_as=jnp.bfloat16):
    values = jax.random.normal(key, dims, jnp.float32) * width
    if len(shards) > 0:
        values = level_of(key, dims, shards, -0.22, 0.18) * values
    return jnp.clip(values, min=-limit, max=limit).astype(held_as)


def setup_inputs(seed: int = 0) -> dict:
    keys = jax.random.split(jax.random.key(seed), 8)
    point_feats = normal_values(keys[0], (C_IN, POINTS), 1.0, 6.0, ((0, 4), (1, 8)))
    destination = draw_destination(jax.random.fold_in(keys[7], 71), 0)
    voxel_slot = draw_voxel_slot(jax.random.fold_in(keys[7], 71), 0)
    adjacency = draw_adjacency(jax.random.fold_in(keys[7], 71), 0)
    active_count = draw_active_count(jax.random.fold_in(keys[7], 71), 0)
    conv_weight = normal_values(keys[5], (C_MID, C_IN, 3, 3, 3), (27 * C_IN) ** -0.5, 0.15625, ((0, 4),))
    down_weight = normal_values(keys[6], (C_OUT, C_MID, 2, 2, 2), (8 * C_MID) ** -0.5, 0.25, ((1, 4),))
    return dict(point_feats=point_feats, destination=destination, voxel_slot=voxel_slot, adjacency=adjacency, active_count=active_count, conv_weight=conv_weight, down_weight=down_weight)


OFFSETS = [(first, second, third) for first in (-1, 0, 1) for second in (-1, 0, 1) for third in (-1, 0, 1) if (first, second, third) != (0, 0, 0)]
SOURCE = {-1: (7, 8), 0: (0, 8), 1: (0, 1)}
TARGET = {-1: (0, 1), 0: (1, 9), 1: (9, 10)}


def splat(columns, voxel_ids):
    totals = jnp.zeros((C_IN, SLOTS * 512), jnp.float32).at[:, voxel_ids].add(columns.astype(jnp.float32))
    counts = jnp.zeros((SLOTS * 512,), jnp.float32).at[voxel_ids].add(1.0)
    voxel_grid = (totals / jnp.maximum(counts, 1.0)).astype(jnp.bfloat16)
    return voxel_grid.reshape(C_IN, SLOTS, 8, 8, 8).transpose(1, 0, 2, 3, 4)


def convolve(inputs, kernel, stride):
    return lax.conv_general_dilated(inputs.astype(jnp.float32), kernel.astype(jnp.float32), (stride, stride, stride), "VALID", dimension_numbers=("NCDHW", "OIDHW", "NCDHW"), precision=lax.Precision.HIGHEST)


def reference(point_feats, destination, voxel_slot, adjacency, active_count, conv_weight, down_weight):
    per_region = PTS_DEV // N_REGION
    sorted_order = jnp.argsort(destination.reshape(N_REGION, PTS_DEV), axis=1, stable=True).astype(jnp.int32)
    sources = (jnp.arange(N_REGION, dtype=jnp.int32) * PTS_DEV)[:, None]

    def one_grid(region):
        picked = lax.dynamic_slice_in_dim(sorted_order, region * per_region, per_region, 1)
        picked_rows = (sources + picked).reshape(-1).astype(jnp.int32)
        return splat(jnp.take(point_feats, picked_rows, axis=1), jnp.take(voxel_slot, picked_rows))

    voxel_grids = lax.map(one_grid, jnp.arange(N_REGION, dtype=jnp.int32))
    brick_table = jnp.concatenate([voxel_grids.reshape(BRICKS_ALL, C_IN, 8, 8, 8), jnp.zeros((1, C_IN, 8, 8, 8), jnp.bfloat16)], axis=0)
    adjacency_rows = adjacency.reshape(N_REGION, SLOTS, 26)

    def one_region(region):
        neighbours = adjacency_rows[region]
        center = voxel_grids[region]
        padded = jnp.pad(center, ((0, 0), (0, 0), (1, 1), (1, 1), (1, 1)))
        for number, offset in enumerate(OFFSETS):
            fetched = jnp.take(brick_table, neighbours[:, number], axis=0)
            source = tuple(slice(*SOURCE[element]) for element in offset)
            target = tuple(slice(*TARGET[element]) for element in offset)
            padded = padded.at[(slice(None), slice(None)) + target].set(fetched[(slice(None), slice(None)) + source])
        hidden = convolve(padded, conv_weight, 1)
        alive_mask = (jnp.arange(SLOTS, dtype=jnp.int32) < active_count[region]).astype(jnp.float32)[:, None, None, None, None]
        hidden = (jnp.maximum(hidden, 0.0) * alive_mask).astype(jnp.bfloat16)
        lowered = convolve(hidden, down_weight, 2)
        return jnp.maximum(lowered, 0.0).astype(jnp.bfloat16).reshape(SLOTS, C_OUT * 64)

    return lax.map(one_region, jnp.arange(N_REGION, dtype=jnp.int32)).reshape(BRICKS_ALL, C_OUT * 64)
```

```python
import functools

import jax
import jax.numpy as jnp
import numpy as np
from jax import lax
from jax.experimental import pallas as pl
from jax.experimental.pallas import tpu as pltpu
from jax.sharding import PartitionSpec as P

OFFSETS = [
    (first, second, third)
    for first in (-1, 0, 1)
    for second in (-1, 0, 1)
    for third in (-1, 0, 1)
    if (first, second, third) != (0, 0, 0)
]
LANES = 128
REACH = 16
F32 = jnp.float32
BF16 = jnp.bfloat16
NT = (((1,), (1,)), ((), ()))
VMEM = pl.BlockSpec(memory_space=pltpu.VMEM)
SMEM = pl.BlockSpec(memory_space=pltpu.SMEM)


def mm(a, b):
    return jnp.dot(a, b, preferred_element_type=F32)


def params():
    return pltpu.CompilerParams(vmem_limit_bytes=48 * 1024 * 1024)


def permute_kernel(depth, feats, order, out, stack):
    channels, points = feats.shape
    high = points // depth
    for part in range(high):
        stack[part * channels : (part + 1) * channels, :] = feats[:, part * depth : (part + 1) * depth]
    blocks = out.shape[1]
    pairs = order.shape[0] // 2

    def step(at, _):
        wanted = order[pl.ds(at * 2, 2), :]
        wanted = jnp.concatenate([wanted[0:1], wanted[1:2]], axis=1)
        low = wanted & (depth - 1)
        top = wanted // depth
        hot = (lax.broadcasted_iota(jnp.int32, (depth, 2 * LANES), 0) == low).astype(BF16)
        found = mm(stack[...], hot)
        picked = jnp.zeros((channels, 2 * LANES), F32)
        for part in range(high):
            picked = jnp.where(top == part, found[part * channels : (part + 1) * channels], picked)
        picked = picked.astype(BF16)
        for half in range(2):
            tile = at * 2 + half
            out[tile // blocks, tile % blocks] = picked[:, half * LANES : (half + 1) * LANES]
        return 0

    lax.fori_loop(0, pairs, step, 0)


def permute(feats, order, regions):
    channels, points = feats.shape
    depth = 512
    return pl.pallas_call(
        functools.partial(permute_kernel, depth),
        out_shape=jax.ShapeDtypeStruct((regions, points // regions // LANES, channels, LANES), BF16),
        in_specs=[VMEM, VMEM],
        out_specs=VMEM,
        scratch_shapes=[pltpu.VMEM((points // depth * channels, depth), BF16)],
        compiler_params=params(),
        name="permute",
    )(feats, order)


WINDOW = 256
GROUP = 8


def voxel_kernel(slots, feats, ids, first, last, hops, send_pos, out, faces, acc):
    chunks, blocks, channels, _ = feats.shape
    groups = chunks // GROUP
    windows = slots * 64 // WINDOW
    per_plane = slots * 8 // WINDOW
    devices = out.shape[0]

    def window(number):
        acc[...] = jnp.zeros_like(acc)

        def one_group(group, _):
            def step(at, _):
                sides = []
                rows = []
                for member in range(GROUP):
                    chunk = group * GROUP + member
                    block = first[number, chunk] + at
                    valid = block < last[number, chunk]
                    block = jnp.minimum(block, blocks - 1)
                    code = ids[chunk, pl.ds(block, 1), :]
                    cell = code & 7
                    rows.append(jnp.where(valid, code >> 3, -1))
                    values = feats[chunk, block].astype(F32)
                    mask = [cell == k for k in range(8)]
                    side = [jnp.where(m, values, 0.0).astype(BF16) for m in mask]
                    side += [jnp.broadcast_to(jnp.where(m, 1.0, 0.0), (channels, LANES)).astype(BF16) for m in mask]
                    sides.append(jnp.concatenate(side, axis=0))
                side = jnp.concatenate(sides, axis=1)
                row = jnp.concatenate(rows, axis=1)
                hot = lax.broadcasted_iota(jnp.int32, (WINDOW, GROUP * LANES), 0) + number * WINDOW == row
                acc[...] += lax.dot_general(hot.astype(BF16), side, NT, preferred_element_type=F32)
                return 0

            lax.fori_loop(0, hops[number, group], step, 0)
            return 0

        if groups == 1:
            one_group(0, 0)
        else:
            lax.fori_loop(0, groups, one_group, 0)
        mean = (acc[:, :LANES] / jnp.maximum(acc[:, LANES:], 1.0)).astype(BF16)
        plane = number // per_plane
        begin = (number % per_plane) * WINDOW
        owner = plane // 2
        out[owner, 1 + plane % 2, begin : begin + WINDOW, :] = mean
        if plane % 2 == 0:
            out[(owner - 1) % devices, 3, begin : begin + WINDOW, :] = mean
        else:
            out[(owner + 1) % devices, 0, begin : begin + WINDOW, :] = mean

    for number in range(windows):
        window(number)
    for side in range(2):
        hot = lax.broadcasted_iota(jnp.int32, (REACH, slots), 0) == send_pos[side : side + 1, :]
        hot = jnp.where(hot, 1.0, 0.0).astype(BF16)
        for j in range(8):
            if side == 0:
                plane = out[devices - 1, 2, j * slots : (j + 1) * slots, :]
            else:
                plane = out[0, 1, j * slots : (j + 1) * slots, :]
            faces[side, j] = mm(hot, plane).astype(BF16)


def voxels(feats, ids, send_pos, slots, devices):
    chunks, blocks, channels, _ = feats.shape
    windows = slots * 64 // WINDOW
    bounds = (jnp.arange(windows + 1, dtype=jnp.int32) * (WINDOW * 8))[:, None, None, None]
    before = jnp.sum((ids[None] < bounds).astype(jnp.int32), axis=(2, 3))
    first = before[:-1] // LANES
    last = (before[1:] + LANES - 1) // LANES
    hops = jnp.max((last - first).reshape(windows, chunks // GROUP, GROUP), axis=2)
    return pl.pallas_call(
        functools.partial(voxel_kernel, slots),
        out_shape=(
            jax.ShapeDtypeStruct((devices, 4, 8 * slots, LANES), BF16),
            jax.ShapeDtypeStruct((2, 8, REACH, LANES), BF16),
        ),
        in_specs=[VMEM, VMEM, SMEM, SMEM, SMEM, VMEM],
        out_specs=(VMEM, VMEM),
        scratch_shapes=[pltpu.VMEM((WINDOW, 2 * LANES), F32)],
        compiler_params=params(),
        name="voxels",
    )(feats, ids, first, last, hops, send_pos)


def spread_matrix():
    spread = np.zeros((4, 384, 192), np.float32)
    for k in range(4):
        for e in range(3):
            cell = k + e
            for channel in range(64):
                source, inner = divmod(channel, 16)
                if 1 <= cell <= 4:
                    row = source * 64 + (cell - 1) * 16 + inner
                else:
                    row = 256 + (cell // 5) * 64 + source * 16 + inner
                spread[k, row, e * 64 + channel] = 1
    return spread


def weight_kernel(spread, weights, out):
    for ab in range(9):
        for k in range(4):
            out[ab, :, k * 64 : (k + 1) * 64] = lax.dot_general(
                spread[k], weights[ab], NT, preferred_element_type=F32
            ).astype(BF16)


def banded(weights):
    return pl.pallas_call(
        weight_kernel,
        out_shape=jax.ShapeDtypeStruct((9, 384, 256), BF16),
        in_specs=[VMEM, VMEM],
        out_specs=VMEM,
        compiler_params=params(),
        name="banded",
    )(jnp.asarray(spread_matrix(), BF16), weights)


def halo_matrix():
    pick = np.zeros((512, 256), np.float32)
    for group, cell in enumerate((7, 0, 3, 4)):
        for source in range(4):
            for inner in range(16):
                pick[source * 128 + cell * 16 + inner, group * 64 + source * 16 + inner] = 1
    return pick


def conv_kernel(slots, active, grid, remote, hot, pick, weights, down, out, table, padded, stacked):
    rows = slots * 8
    extra = REACH
    total = slots + extra
    low = lax.broadcasted_iota(jnp.int32, (slots, LANES), 1) < 64

    def arrange(parts, plane, j, at, count):
        for half in range(2):
            cut = slice(half * 64, half * 64 + 64)
            for pair in range(2):
                both = jnp.concatenate([parts[2 * pair][:, cut], parts[2 * pair + 1][:, cut]], axis=1)
                table[plane, j, at : at + count, half * 384 + pair * 128 : half * 384 + pair * 128 + 128] = both

    for plane in range(4):
        whole = jnp.concatenate([grid[source, plane] for source in range(4)], axis=1)
        edge = mm(whole, pick[...]).astype(BF16)
        for j in range(8):
            arrange([grid[s, plane, j * slots : (j + 1) * slots, :] for s in range(4)], plane, j, 0, slots)
            table[plane, j, 0:slots, 256:384] = edge[j * slots : (j + 1) * slots, :128]
            table[plane, j, 0:slots, 640:768] = edge[j * slots : (j + 1) * slots, 128:]
    for plane in (0, 3):
        for j in range(8):
            parts = [remote[s, j] for s in range(4)]
            arrange(parts, plane, j, slots, extra)
            edge = mm(jnp.concatenate(parts, axis=1), pick[...]).astype(BF16)
            table[plane, j, slots:total, 256:384] = edge[:, :128]
            table[plane, j, slots:total, 640:768] = edge[:, 128:]

    for plane in range(4):
        base = (0, 9, 9, 18)[plane]
        used = total if plane in (0, 3) else slots
        for jj in range(10):
            dy, j = ((-1, 7) if jj == 0 else (1, 0) if jj == 9 else (0, jj - 1))
            at = base + (dy + 1) * 3
            source = table[plane, j, 0:used, :]
            if plane in (1, 2) and dy == 0:
                own = source
            else:
                own = mm(hot[at + 1, :, 0:used], source).astype(BF16)
            near = source[:, 256:384]
            down_edge = mm(hot[at, :, 0:used], near).astype(BF16)
            up_edge = mm(hot[at + 2, :, 0:used], near).astype(BF16)
            kept = own[:, 640:768]
            padded[plane, jj, :, 0:256] = own[:, 0:256]
            padded[plane, jj, :, 256:384] = jnp.where(low, down_edge, kept)
            padded[plane, jj, :, 384:640] = own[:, 384:640]
            padded[plane, jj, :, 640:768] = jnp.where(low, kept, up_edge)

    alive = lax.broadcasted_iota(jnp.int32, (slots, 256), 0) < active[0]
    for half in range(2):
        for a_out in range(2):
            total_sum = jnp.zeros((rows, 256), F32)
            for a in range(3):
                for b in range(3):
                    left = padded[a_out + a, b : b + 8, :, half * 384 : half * 384 + 384].reshape(rows, 384)
                    total_sum += mm(left, weights[a * 3 + b])
            for j in range(8):
                block = jnp.where(alive, jnp.maximum(total_sum[j * slots : (j + 1) * slots], 0.0), 0.0).astype(BF16)
                for kk in range(2):
                    begin = ((j // 2) * 4 + half * 2 + kk) * slots
                    place = (a_out * 2 + j % 2) * 128
                    stacked[begin : begin + slots, place : place + 128] = block[:, kk * 128 : kk * 128 + 128]

    result = lax.dot_general(down[...], stacked[...], NT, preferred_element_type=F32)
    result = jnp.maximum(result, 0.0).astype(BF16)
    devices = out.shape[0]
    width = out.shape[1]
    for device in range(devices):
        out[device] = result[device * width : (device + 1) * width]


def convolve(active, grid, remote, hot, weights, down):
    devices = grid.shape[0]
    slots = grid.shape[2] // 8
    outputs = down.shape[0]
    return pl.pallas_call(
        functools.partial(conv_kernel, slots),
        out_shape=jax.ShapeDtypeStruct((devices, outputs // devices, 16 * slots), BF16),
        in_specs=[SMEM] + [VMEM] * 6,
        out_specs=VMEM,
        scratch_shapes=[
            pltpu.VMEM((4, 8, slots + REACH, 768), BF16),
            pltpu.VMEM((4, 10, slots, 768), BF16),
            pltpu.VMEM((16 * slots, 512), BF16),
        ],
        compiler_params=params(),
        name="convolve",
    )(active, grid, remote, hot, jnp.asarray(halo_matrix(), BF16), weights, down)


def final_kernel(slots, data, out, turned):
    planes, outputs, _ = data.shape
    for plane in range(planes):
        for cell in range(16):
            turned[pl.ds(plane * 16 + cell, outputs, stride=64), :] = data[
                plane, :, cell * slots : (cell + 1) * slots
            ].astype(F32)
    for tile in range(out.shape[1] // LANES):
        out[:, tile * LANES : (tile + 1) * LANES] = turned[tile * LANES : (tile + 1) * LANES, :].T.astype(BF16)


def finish(data, slots):
    outputs = data.shape[1]
    return pl.pallas_call(
        functools.partial(final_kernel, slots),
        out_shape=jax.ShapeDtypeStruct((slots, outputs * 64), BF16),
        in_specs=[VMEM],
        out_specs=VMEM,
        scratch_shapes=[pltpu.VMEM((outputs * 64, slots), F32)],
        compiler_params=params(),
        name="finish",
    )(data)


def links(adjacency, region, regions, chan, devices):
    slots = adjacency.shape[0]
    named = adjacency.T
    linked = named < slots * regions
    owner = jnp.where(linked, named // slots, regions + 7)
    slot = named % slots
    every = jnp.arange(slots, dtype=jnp.int32)
    steps = np.array([offset[0] for offset in OFFSETS])
    send_pos = []
    place = {}
    for step in (1, -1):
        rows = np.nonzero(steps == step)[0]
        owns = owner[rows[0] : rows[-1] + 1] == region + step
        sends = jnp.any(owns, axis=0)
        rank = jnp.sum((sends[None, :] & (every[None, :] < every[:, None])).astype(jnp.int32), axis=1)
        send_pos.append(jnp.where(sends, rank, -1))
        there = slot[rows[0] : rows[-1] + 1]
        member = jnp.any(owns[:, :, None] & (there[:, :, None] == every), axis=(0, 1))
        below = jnp.sum(
            (member[None, None, :] & (every < there[:, :, None])).astype(jnp.int32), axis=2
        )
        place[step] = jnp.where(owns, slots + below, -1)
    own = jnp.where(owner == region, slot, -1)
    same = jnp.concatenate([own[9:13], every[None, :], own[13:17]], axis=0)
    left = jnp.where(owner[0:9] == region, slot[0:9], place[-1])
    right = jnp.where(owner[17:26] == region, slot[17:26], place[1])
    first = jnp.where(chan == 0, left, same)
    last = jnp.where(chan == devices - 1, right, same)
    pos = jnp.concatenate([first, same, last], axis=0)
    hot = (pos[:, :, None] == jnp.arange(slots + REACH, dtype=jnp.int32)).astype(BF16)
    return jnp.stack(send_pos), hot


def send_faces(faces, chan, regions, devices):
    got = []
    for source in range(devices):
        other = (source + devices // 2) % devices
        pairs = [(r * devices + source, (r + 1) * devices) for r in range(regions - 1)]
        pairs += [(r * devices + other, r * devices - 1) for r in range(1, regions)]
        got.append(lax.ppermute(jnp.where(chan == source, faces[0], faces[1]), ("region", "chan"), pairs))
    swapped = got[devices // 2 :] + got[: devices // 2]
    return jnp.where(chan == devices - 1, jnp.stack(swapped), jnp.stack(got))


def body(point_feats, destination, voxel_slot, adjacency, active_count, conv_weight, down_weight):
    regions = lax.axis_size("region")
    region = lax.axis_index("region")
    devices = lax.axis_size("chan")
    chan = lax.axis_index("chan")
    slots = adjacency.shape[0]
    points = point_feats.shape[1]
    cells = slots * 512
    per = points // regions

    slot = voxel_slot // 512
    inside = voxel_slot % 512
    code = ((inside // 8) * slots + slot) * 8 + inside % 8
    key, order = lax.sort(
        (destination * cells + code, jnp.arange(points, dtype=jnp.int32)), num_keys=1, is_stable=False
    )
    ids = lax.all_to_all((key % cells).reshape(regions, per // LANES, LANES), "region", 0, 0, tiled=True)
    moved = permute(point_feats, order.reshape(points // LANES, LANES), regions)
    moved = lax.all_to_all(moved, "region", 0, 0, tiled=True)

    taps = conv_weight.transpose(2, 3, 4, 0, 1).reshape(9, 3, conv_weight.shape[0], -1)
    taps = lax.all_gather(taps, "chan", axis=2, tiled=True)
    weights = banded(taps.transpose(0, 2, 1, 3).reshape(9, taps.shape[2], -1))
    down = lax.all_gather(down_weight, "chan", axis=1, tiled=True)
    down = down.transpose(0, 2, 3, 4, 1).reshape(down.shape[0], -1)

    send_pos, hot = links(adjacency, region, regions, chan, devices)
    planes, faces = voxels(moved, ids, send_pos, slots, devices)
    remote = send_faces(faces, chan, regions, devices)
    grid = lax.all_to_all(planes, "chan", 0, 0, tiled=True)
    coarse = convolve(active_count, grid, remote, hot, weights, down)
    coarse = lax.all_to_all(coarse, "chan", 0, 0, tiled=True)
    return finish(coarse, slots)


def solution(mesh):
    return jax.shard_map(
        body,
        mesh=mesh,
        in_specs=(
            P("chan", "region"),
            P("region"),
            P("region"),
            P("region", None),
            P("region"),
            P("chan", None, None, None, None),
            P(None, "chan", None, None, None),
        ),
        out_specs=P("region", "chan"),
        check_vma=False,
    )
```

```python
import functools

import jax
import jax.numpy as jnp
import numpy as np
from jax import lax
from jax.experimental import pallas as pl
from jax.experimental.pallas import tpu as pltpu
from jax.sharding import PartitionSpec as P

OFFSETS = [
    (first, second, third)
    for first in (-1, 0, 1)
    for second in (-1, 0, 1)
    for third in (-1, 0, 1)
    if (first, second, third) != (0, 0, 0)
]
LANES = 128
REACH = 16
F32 = jnp.float32
BF16 = jnp.bfloat16
NT = (((1,), (1,)), ((), ()))
VMEM = pl.BlockSpec(memory_space=pltpu.VMEM)
SMEM = pl.BlockSpec(memory_space=pltpu.SMEM)


def mm(a, b):
    return jnp.dot(a, b, preferred_element_type=F32)


def params():
    return pltpu.CompilerParams(vmem_limit_bytes=48 * 1024 * 1024)


ID_ROWS = 16


def permute_kernel(depth, width, cells, feats, order, keys, ready, out, stack):
    channels, points = feats.shape
    high = points // depth
    for part in range(high):
        stack[part * channels : (part + 1) * channels, :] = feats[:, part * depth : (part + 1) * depth]
    regions = out.shape[0]
    blocks = points // regions // LANES
    tiles = (out.shape[1] - blocks) // 2
    count = width // LANES

    def step(at, _):
        wanted = order[pl.ds(at * count, count), :]
        wanted = jnp.concatenate([wanted[i : i + 1] for i in range(count)], axis=1)
        low = (wanted & (depth - 1)).astype(jnp.int16)
        top = wanted // depth
        hot = lax.broadcasted_iota(jnp.int16, (depth, width), 0) == low
        hot = jnp.where(hot, jnp.ones((), BF16), jnp.zeros((), BF16))
        found = mm(stack[...], hot)
        picked = jnp.zeros((channels, width), F32)
        for part in range(high):
            picked = jnp.where(top == part, found[part * channels : (part + 1) * channels], picked)
        picked = picked.astype(BF16)
        for part in range(count):
            tile = at * count + part
            out[tile // blocks, tile % blocks] = picked[:, part * LANES : (part + 1) * LANES]
        return 0

    lax.fori_loop(0, points // width, step, 0)
    for target in range(regions):
        for tile in range(tiles):
            begin = target * blocks + tile * ID_ROWS
            rows = min(ID_ROWS, blocks - tile * ID_ROWS)
            code = lax.rem(keys[begin : begin + rows, :], cells)
            if rows < ID_ROWS:
                code = jnp.concatenate([code, jnp.zeros((ID_ROWS - rows, LANES), jnp.int32)], axis=0)
            out[target, blocks + tile] = (code >> 8).astype(F32).astype(BF16)
            out[target, blocks + tiles + tile] = (code & 255).astype(F32).astype(BF16)


def permute(feats, order, keys, ready, regions, cells):
    channels, points = feats.shape
    depth, width = 512, 1024
    blocks = points // regions // LANES
    tiles = -(-blocks // ID_ROWS)
    return pl.pallas_call(
        functools.partial(permute_kernel, depth, width, cells),
        out_shape=jax.ShapeDtypeStruct((regions, blocks + 2 * tiles, channels, LANES), BF16),
        in_specs=[VMEM, VMEM, VMEM, pl.BlockSpec(memory_space=pl.ANY)],
        out_specs=VMEM,
        scratch_shapes=[pltpu.VMEM((points // depth * channels, depth), BF16)],
        compiler_params=params(),
        name="permute",
    )(feats, order, keys, ready)


WINDOW = 256
GROUP = 8
STATIC = 2


def decode(feats, ids):
    chunks, total, _, _ = feats.shape
    tiles = ids.shape[1] // ID_ROWS
    blocks = total - 2 * tiles
    for chunk in range(chunks):
        for tile in range(tiles):
            upper = feats[chunk, blocks + tile].astype(F32)
            lower = feats[chunk, blocks + tiles + tile].astype(F32)
            ids[chunk, tile * ID_ROWS : (tile + 1) * ID_ROWS, :] = (upper * 256.0 + lower).astype(jnp.int32)


def window_mean(number, feats, ids, first, last, hops, acc):
    chunks, total, channels, _ = feats.shape
    groups = chunks // GROUP
    blocks = total - 2 * (ids.shape[1] // ID_ROWS)

    def product(group, steps):
        sides = []
        rows = []
        for at in steps:
            for member in range(GROUP):
                chunk = group * GROUP + member
                block = first[number, chunk] + at
                valid = block < last[number, chunk]
                block = jnp.minimum(block, blocks - 1)
                code = ids[chunk, pl.ds(block, 1), :]
                cell = code & 7
                rows.append(jnp.where(valid, (code >> 3) - number * WINDOW, -1))
                values = feats[chunk, block].astype(F32)
                mask = [cell == k for k in range(8)]
                side = [jnp.where(m, values, 0.0).astype(BF16) for m in mask]
                side += [jnp.broadcast_to(jnp.where(m, 1.0, 0.0), (channels, LANES)).astype(BF16) for m in mask]
                sides.append(jnp.concatenate(side, axis=0))
        side = jnp.concatenate(sides, axis=1)
        row = jnp.concatenate(rows, axis=1).astype(jnp.int16)
        hot = lax.broadcasted_iota(jnp.int16, (WINDOW, len(steps) * GROUP * LANES), 0) == row
        hot = jnp.where(hot, jnp.ones((), BF16), jnp.zeros((), BF16))
        return lax.dot_general(hot, side, NT, preferred_element_type=F32)

    def one_group(group, start):
        def step(at, _):
            acc[...] += product(group, [at])
            return 0

        lax.fori_loop(start, hops[number, group], step, 0)

    if groups == 1:
        acc[...] = product(0, list(range(STATIC)))
        one_group(0, STATIC)
    else:
        acc[...] = jnp.zeros_like(acc)

        def each(group, _):
            one_group(group, 0)
            return 0

        lax.fori_loop(0, groups, each, 0)
    return (acc[:, :LANES] / jnp.maximum(acc[:, LANES:], 1.0)).astype(BF16)


def far_kernel(chan, feats, first, last, hops, out, ids, acc):
    decode(feats, ids)
    begin = 2 * (chan[0] ^ 2) + 7
    parts = out.shape[1] // WINDOW
    for plane in range(4):
        for part in range(parts):
            number = lax.rem(begin + plane, 8) * parts + part
            out[plane, part * WINDOW : (part + 1) * WINDOW, :] = window_mean(number, feats, ids, first, last, hops, acc)


def near_kernel(slots, chan, feats, first, last, hops, far, send_pos, out, faces, ids, acc, planes):
    decode(feats, ids)
    partner = chan[0] ^ 2
    begin = 2 * partner + 7
    parts = far.shape[1] // WINDOW
    planes[0:4] = far[...]
    for plane in range(4, 8):
        for part in range(parts):
            number = lax.rem(begin + plane, 8) * parts + part
            planes[plane, part * WINDOW : (part + 1) * WINDOW, :] = window_mean(
                number, feats, ids, first, last, hops, acc
            )
    for place, flip in enumerate((3, 1, 0)):
        shift = 2 * ((chan[0] ^ flip) - partner) + 8
        for plane in range(4):
            out[place, plane] = planes[lax.rem(shift + plane, 8)]
    for side in range(2):
        hot = lax.broadcasted_iota(jnp.int32, (REACH, slots), 0) == send_pos[side : side + 1, :]
        hot = jnp.where(hot, 1.0, 0.0).astype(BF16)
        face = planes.at[lax.rem((7, 8)[side] - begin + 16, 8)]
        for j in range(8):
            faces[side, j] = mm(hot, face[j * slots : (j + 1) * slots, :]).astype(BF16)


def ranges(moved, tiles, slots):
    chunks, total, _, _ = moved.shape
    blocks = total - 2 * tiles
    ends = moved[:, blocks:, :, :: LANES - 1].astype(F32)
    ends = ends[:, :tiles] * 256.0 + ends[:, tiles:]
    ends = ends.reshape(chunks, tiles * ID_ROWS, 2)[:, :blocks].astype(jnp.int32)
    windows = slots * 64 // WINDOW
    bounds = (jnp.arange(windows, dtype=jnp.int32) * (WINDOW * 8))[:, None, None]
    first = jnp.sum((ends[None, :, :, 1] < bounds).astype(jnp.int32), axis=2)
    last = jnp.sum((ends[None, :, :, 0] < bounds + WINDOW * 8).astype(jnp.int32), axis=2)
    hops = jnp.max((last - first).reshape(windows, chunks // GROUP, GROUP), axis=2)
    return first, last, hops


def far_voxels(chan, moved, bounds, slots, tiles):
    return pl.pallas_call(
        far_kernel,
        out_shape=jax.ShapeDtypeStruct((4, 8 * slots, LANES), BF16),
        in_specs=[SMEM, VMEM, SMEM, SMEM, SMEM],
        out_specs=VMEM,
        scratch_shapes=[
            pltpu.VMEM((moved.shape[0], tiles * ID_ROWS, LANES), jnp.int32),
            pltpu.VMEM((WINDOW, 2 * LANES), F32),
        ],
        compiler_params=params(),
        cost_estimate=pl.CostEstimate(flops=4_000_000_000, bytes_accessed=1_200_000, transcendentals=0),
        name="far_voxels",
    )(chan, moved, *bounds)


def near_voxels(chan, moved, bounds, far, send_pos, slots, tiles):
    return pl.pallas_call(
        functools.partial(near_kernel, slots),
        out_shape=(
            jax.ShapeDtypeStruct((3, 4, 8 * slots, LANES), BF16),
            jax.ShapeDtypeStruct((2, 8, REACH, LANES), BF16),
        ),
        in_specs=[SMEM, VMEM, SMEM, SMEM, SMEM, VMEM, VMEM],
        out_specs=(VMEM, VMEM),
        scratch_shapes=[
            pltpu.VMEM((moved.shape[0], tiles * ID_ROWS, LANES), jnp.int32),
            pltpu.VMEM((WINDOW, 2 * LANES), F32),
            pltpu.VMEM((8, 8 * slots, LANES), BF16),
        ],
        compiler_params=params(),
        cost_estimate=pl.CostEstimate(flops=4_000_000_000, bytes_accessed=3_000_000, transcendentals=0),
        name="near_voxels",
    )(chan, moved, *bounds, far, send_pos)


def spread_matrix():
    spread = np.zeros((4, 384, 192), np.float32)
    for k in range(4):
        for e in range(3):
            cell = k + e
            for channel in range(64):
                source, inner = divmod(channel, 16)
                if 1 <= cell <= 4:
                    row = source * 64 + (cell - 1) * 16 + inner
                else:
                    row = 256 + (cell // 5) * 64 + source * 16 + inner
                spread[k, row, e * 64 + channel] = 1
    return spread


def weight_kernel(chan, spread, own, one, two, three, out, down):
    every = (own, one, two, three)
    columns = lax.broadcasted_iota(jnp.int32, (192, 192), 1) ^ (chan[0] * 16)
    turn = jnp.where(lax.broadcasted_iota(jnp.int32, (192, 192), 0) == columns, 1.0, 0.0).astype(BF16)
    for ab in range(9):
        taps = jnp.concatenate([ref[ab] for ref in every], axis=0)
        taps = mm(taps, turn).astype(BF16)
        for k in range(4):
            out[ab, :, k * 64 : (k + 1) * 64] = lax.dot_general(
                spread[k], taps, NT, preferred_element_type=F32
            ).astype(BF16)
    outputs = down.shape[0]
    total = jnp.zeros((outputs, 512), F32)
    rows = lax.broadcasted_iota(jnp.int32, (128, 512), 0)
    place = (rows >> 4) * 64 + (rows & 15)
    for source, ref in enumerate(every):
        part = ref[9:, :, 0:128].reshape(outputs, 128)
        move = lax.broadcasted_iota(jnp.int32, (128, 512), 1) == place + source * 16
        total += mm(part, jnp.where(move, 1.0, 0.0).astype(BF16))
    down[...] = total.astype(BF16)


def prepare(chan, own, others, outputs):
    return pl.pallas_call(
        weight_kernel,
        out_shape=(
            jax.ShapeDtypeStruct((9, 384, 256), BF16),
            jax.ShapeDtypeStruct((outputs, 512), BF16),
        ),
        in_specs=[SMEM] + [VMEM] * 5,
        out_specs=(VMEM, VMEM),
        compiler_params=params(),
        cost_estimate=pl.CostEstimate(flops=2_000_000_000, bytes_accessed=3_000_000, transcendentals=0),
        name="prepare",
    )(chan, jnp.asarray(spread_matrix(), BF16), own, *others)


def halo_matrix():
    pick = np.zeros((512, 256), np.float32)
    for group, cell in enumerate((7, 0, 3, 4)):
        for source in range(4):
            for inner in range(16):
                pick[source * 128 + cell * 16 + inner, group * 64 + source * 16 + inner] = 1
    return pick


def conv_kernel(slots, chan, active, near, one, two, three, r0, r1, r2, r3, hot, pick, weights, down, *rest):
    grid = (near.at[2], one, two, three)
    remote = (r0, r1, r2, r3)
    out, table, padded, stacked, answer = rest
    rows = slots * 8
    extra = REACH
    total = slots + extra
    low = lax.broadcasted_iota(jnp.int32, (slots, LANES), 1) < 64

    def arrange(parts, plane, j, at, count):
        for half in range(2):
            cut = slice(half * 64, half * 64 + 64)
            for pair in range(2):
                both = jnp.concatenate([parts[2 * pair][:, cut], parts[2 * pair + 1][:, cut]], axis=1)
                table[plane, j, at : at + count, half * 384 + pair * 128 : half * 384 + pair * 128 + 128] = both

    for plane in range(4):
        whole = jnp.concatenate([grid[source][plane] for source in range(4)], axis=1)
        edge = mm(whole, pick[...]).astype(BF16)
        for j in range(8):
            arrange([grid[s][plane, j * slots : (j + 1) * slots, :] for s in range(4)], plane, j, 0, slots)
            table[plane, j, 0:slots, 256:384] = edge[j * slots : (j + 1) * slots, :128]
            table[plane, j, 0:slots, 640:768] = edge[j * slots : (j + 1) * slots, 128:]
    for plane in (0, 3):
        for j in range(8):
            parts = [remote[s][j] for s in range(4)]
            arrange(parts, plane, j, slots, extra)
            edge = mm(jnp.concatenate(parts, axis=1), pick[...]).astype(BF16)
            table[plane, j, slots:total, 256:384] = edge[:, :128]
            table[plane, j, slots:total, 640:768] = edge[:, 128:]

    for plane in range(4):
        base = (0, 9, 9, 18)[plane]
        used = total if plane in (0, 3) else slots
        for jj in range(10):
            dy, j = ((-1, 7) if jj == 0 else (1, 0) if jj == 9 else (0, jj - 1))
            at = base + (dy + 1) * 3
            source = table[plane, j, 0:used, :]
            if plane in (1, 2) and dy == 0:
                own = source
            else:
                own = mm(hot[at + 1, :, 0:used], source).astype(BF16)
            near = source[:, 256:384]
            down_edge = mm(hot[at, :, 0:used], near).astype(BF16)
            up_edge = mm(hot[at + 2, :, 0:used], near).astype(BF16)
            kept = own[:, 640:768]
            padded[plane, jj, :, 0:256] = own[:, 0:256]
            padded[plane, jj, :, 256:384] = jnp.where(low, down_edge, kept)
            padded[plane, jj, :, 384:640] = own[:, 384:640]
            padded[plane, jj, :, 640:768] = jnp.where(low, kept, up_edge)

    alive = lax.broadcasted_iota(jnp.int32, (slots, 256), 0) < active[0]
    for half in range(2):
        for a_out in range(2):
            total_sum = jnp.zeros((rows, 256), F32)
            for a in range(3):
                for b in range(3):
                    left = padded[a_out + a, b : b + 8, :, half * 384 : half * 384 + 384].reshape(rows, 384)
                    total_sum += mm(left, weights[a * 3 + b])
            for j in range(8):
                block = jnp.where(alive, jnp.maximum(total_sum[j * slots : (j + 1) * slots], 0.0), 0.0).astype(BF16)
                for kk in range(2):
                    begin = ((j // 2) * 4 + half * 2 + kk) * slots
                    place = (a_out * 2 + j % 2) * 128
                    stacked[begin : begin + slots, place : place + 128] = block[:, kk * 128 : kk * 128 + 128]

    result = lax.dot_general(down[...], stacked[...], NT, preferred_element_type=F32)
    result = jnp.maximum(result, 0.0).astype(BF16)
    devices, width, _ = out.shape
    answer[...] = result
    for flip in range(devices):
        out[flip] = answer[pl.ds(pl.multiple_of((chan[0] ^ flip) * width, width), width), :]


def convolve(chan, active, near, others, remote, hot, weights, down):
    devices = 4
    slots = near.shape[2] // 8
    outputs = down.shape[0]
    return pl.pallas_call(
        functools.partial(conv_kernel, slots),
        out_shape=jax.ShapeDtypeStruct((devices, outputs // devices, 16 * slots), BF16),
        in_specs=[SMEM] * 2 + [VMEM] * 12,
        out_specs=VMEM,
        scratch_shapes=[
            pltpu.VMEM((4, 8, slots + REACH, 768), BF16),
            pltpu.VMEM((4, 10, slots, 768), BF16),
            pltpu.VMEM((16 * slots, 512), BF16),
            pltpu.VMEM((outputs, 16 * slots), BF16),
        ],
        compiler_params=params(),
        cost_estimate=pl.CostEstimate(flops=6_000_000_000, bytes_accessed=5_000_000, transcendentals=0),
        name="convolve",
    )(chan, active, near, *others, *remote, hot, jnp.asarray(halo_matrix(), BF16), weights, down)


def final_kernel(slots, chan, own, one, two, three, out, turned):
    _, outputs, _ = own.shape
    for flip, ref in enumerate((own.at[0], one, two, three)):
        plane = chan[0] ^ flip
        for cell in range(16):
            turned[pl.ds(plane * 16 + cell, outputs, stride=64), :] = ref[
                :, cell * slots : (cell + 1) * slots
            ].astype(F32)
    for tile in range(out.shape[1] // LANES):
        out[:, tile * LANES : (tile + 1) * LANES] = turned[tile * LANES : (tile + 1) * LANES, :].T.astype(BF16)


def finish(chan, coarse, others, slots):
    outputs = coarse.shape[1]
    return pl.pallas_call(
        functools.partial(final_kernel, slots),
        out_shape=jax.ShapeDtypeStruct((slots, outputs * 64), BF16),
        in_specs=[SMEM] + [VMEM] * 4,
        out_specs=VMEM,
        scratch_shapes=[pltpu.VMEM((outputs * 64, slots), F32)],
        compiler_params=params(),
        name="finish",
    )(chan, coarse, *others)


def links(adjacency, region, regions, chan, devices):
    slots = adjacency.shape[0]
    named = adjacency.T
    linked = named < slots * regions
    owner = jnp.where(linked, named // slots, regions + 7)
    slot = named % slots
    every = jnp.arange(slots, dtype=jnp.int32)
    steps = np.array([offset[0] for offset in OFFSETS])
    send_pos = []
    place = {}
    for step in (1, -1):
        rows = np.nonzero(steps == step)[0]
        owns = owner[rows[0] : rows[-1] + 1] == region + step
        sends = jnp.any(owns, axis=0)
        rank = jnp.sum((sends[None, :] & (every[None, :] < every[:, None])).astype(jnp.int32), axis=1)
        send_pos.append(jnp.where(sends, rank, -1))
        there = slot[rows[0] : rows[-1] + 1]
        member = jnp.any(owns[:, :, None] & (there[:, :, None] == every), axis=(0, 1))
        below = jnp.sum(
            (member[None, None, :] & (every < there[:, :, None])).astype(jnp.int32), axis=2
        )
        place[step] = jnp.where(owns, slots + below, -1)
    own = jnp.where(owner == region, slot, -1)
    same = jnp.concatenate([own[9:13], every[None, :], own[13:17]], axis=0)
    left = jnp.where(owner[0:9] == region, slot[0:9], place[-1])
    right = jnp.where(owner[17:26] == region, slot[17:26], place[1])
    first = jnp.where(chan == 0, left, same)
    last = jnp.where(chan == devices - 1, right, same)
    pos = jnp.concatenate([first, same, last], axis=0)
    hot = (pos[:, :, None] == jnp.arange(slots + REACH, dtype=jnp.int32)).astype(BF16)
    return jnp.stack(send_pos), hot


def send_faces(faces, chan, regions, devices):
    got = []
    for flip in range(devices):
        other = (devices - 1) ^ flip
        pairs = [(r * devices + flip, (r + 1) * devices) for r in range(regions - 1)]
        pairs += [(r * devices + other, r * devices - 1) for r in range(1, regions)]
        got.append(lax.ppermute(jnp.where(chan == flip, faces[0], faces[1]), ("region", "chan"), pairs))
    return got


def swap(value, flip, devices):
    return lax.ppermute(value, "chan", [(source, source ^ flip) for source in range(devices)])


def body(point_feats, destination, voxel_slot, adjacency, active_count, conv_weight, down_weight):
    regions = lax.axis_size("region")
    region = lax.axis_index("region")
    devices = lax.axis_size("chan")
    chan = lax.axis_index("chan")
    me = chan.reshape(1)
    slots = adjacency.shape[0]
    points = point_feats.shape[1]
    cells = slots * 512
    tiles = -(-(points // regions // LANES) // ID_ROWS)

    taps = conv_weight.transpose(2, 3, 0, 4, 1).reshape(9, conv_weight.shape[0], 192)
    down = down_weight.transpose(0, 2, 3, 4, 1).reshape(-1, conv_weight.shape[0], 128)
    mine = jnp.concatenate([taps, jnp.pad(down, ((0, 0), (0, 0), (0, 64)))], axis=0)
    theirs = [swap(mine, flip, devices) for flip in (1, 2, 3)]
    weights, down = prepare(me, mine, theirs, down_weight.shape[0])

    slot = voxel_slot // 512
    inside = voxel_slot % 512
    code = ((inside // 8) * slots + slot) * 8 + inside % 8
    keys, order = lax.sort(
        (destination * cells + code, jnp.arange(points, dtype=jnp.int32)), num_keys=1, is_stable=False
    )
    square = (points // LANES, LANES)
    moved = permute(point_feats, order.reshape(square), keys.reshape(square), theirs[-1], regions, cells)
    moved = lax.all_to_all(moved, "region", 0, 0, tiled=True)

    send_pos, hot = links(adjacency, region, regions, chan, devices)
    bounds = ranges(moved, tiles, slots)
    far = far_voxels(me, moved, bounds, slots, tiles)
    from_two = swap(far, 2, devices)
    near, faces = near_voxels(me, moved, bounds, far, send_pos, slots, tiles)
    from_three = swap(near[0], 3, devices)
    from_one = swap(near[1], 1, devices)
    remote = send_faces(faces, chan, regions, devices)
    coarse = convolve(me, active_count, near, (from_one, from_two, from_three), remote, hot, weights, down)
    back = [swap(coarse[flip], flip, devices) for flip in (1, 2, 3)]
    return finish(me, coarse, back, slots)


def solution(mesh):
    return jax.shard_map(
        body,
        mesh=mesh,
        in_specs=(
            P("chan", "region"),
            P("region"),
            P("region"),
            P("region", None),
            P("region"),
            P("chan", None, None, None, None),
            P(None, "chan", None, None, None),
        ),
        out_specs=P("region", "chan"),
        check_vma=False,
    )
```

```python
import functools

import jax
import jax.numpy as jnp
import numpy as np
from jax import lax
from jax.experimental import pallas as pl
from jax.experimental.pallas import tpu as pltpu
from jax.sharding import PartitionSpec as P

OFFSETS = [
    (first, second, third)
    for first in (-1, 0, 1)
    for second in (-1, 0, 1)
    for third in (-1, 0, 1)
    if (first, second, third) != (0, 0, 0)
]
LANES = 128
REACH = 16
F32 = jnp.float32
BF16 = jnp.bfloat16
NT = (((1,), (1,)), ((), ()))
VMEM = pl.BlockSpec(memory_space=pltpu.VMEM)
SMEM = pl.BlockSpec(memory_space=pltpu.SMEM)


def mm(a, b):
    return jnp.dot(a, b, preferred_element_type=F32)


def params():
    return pltpu.CompilerParams(vmem_limit_bytes=24 * 1024 * 1024)


ID_ROWS = 16
GROUP = 8


def one_hot_columns(depth, stack, wanted, channels=16):
    count = wanted.shape[0]
    width = count * LANES
    wanted = jnp.concatenate([wanted[i : i + 1] for i in range(count)], axis=1)
    low = (wanted & (depth - 1)).astype(jnp.int16)
    top = wanted // depth
    hot = lax.broadcasted_iota(jnp.int16, (depth, width), 0) == low
    hot = jnp.where(hot, jnp.ones((), BF16), jnp.zeros((), BF16))
    found = mm(stack[...], hot)
    picked = jnp.zeros((channels, width), F32)
    for part in range(stack.shape[0] // channels):
        picked = jnp.where(top == part, found[part * channels : (part + 1) * channels], picked)
    return picked.astype(BF16)


def fill_stack(depth, feats, stack):
    channels, points = feats.shape
    for part in range(points // depth):
        stack[part * channels : (part + 1) * channels, :] = feats[:, part * depth : (part + 1) * depth]


def put_codes(out, blocks, tiles, tile, rows):
    if rows.shape[0] < ID_ROWS:
        rows = jnp.concatenate([rows, jnp.zeros((ID_ROWS - rows.shape[0], LANES), jnp.int32)], axis=0)
    out[blocks + tile] = (rows >> 8).astype(F32).astype(BF16)
    out[blocks + tiles + tile] = (rows & 255).astype(F32).astype(BF16)


def permute_kernel(depth, width, cells, feats, order, keys, out, stack):
    channels, points = feats.shape
    fill_stack(depth, feats, stack)
    regions = out.shape[0]
    blocks = points // regions // LANES
    tiles = (out.shape[1] - blocks) // 2
    count = width // LANES

    def step(at, _):
        picked = one_hot_columns(depth, stack, order[pl.ds(at * count, count), :])
        for part in range(count):
            tile = at * count + part
            out[tile // blocks, tile % blocks] = picked[:, part * LANES : (part + 1) * LANES]
        return 0

    lax.fori_loop(0, points // width, step, 0)
    for target in range(regions):
        for tile in range(tiles):
            begin = target * blocks + tile * ID_ROWS
            rows = min(ID_ROWS, blocks - tile * ID_ROWS)
            put_codes(out.at[target], blocks, tiles, tile, lax.rem(keys[begin : begin + rows, :], cells))


def permute(feats, order, keys, regions, cells):
    channels, points = feats.shape
    depth, width = 512, 1024
    blocks = points // regions // LANES
    tiles = -(-blocks // ID_ROWS)
    return pl.pallas_call(
        functools.partial(permute_kernel, depth, width, cells),
        out_shape=jax.ShapeDtypeStruct((regions, blocks + 2 * tiles, channels, LANES), BF16),
        in_specs=[VMEM] * 3,
        out_specs=VMEM,
        scratch_shapes=[pltpu.VMEM((points // depth * channels, depth), BF16)],
        compiler_params=params(),
        name="permute",
    )(feats, order, keys)


def piece_kernel(depth, cells, flips, region, feats, order, keys, *rest):
    outs = rest[-1 - len(flips) : -1]
    stack = rest[-1]
    fill_stack(depth, feats, stack)
    tiles = 1
    blocks = outs[0].shape[0] - 2 * tiles
    count = 8
    for flip, out in zip(flips, outs):
        begin = pl.multiple_of((region[0] ^ flip) * blocks, 8)
        for step in range(blocks // count):
            picked = one_hot_columns(depth, stack, order[pl.ds(begin + step * count, count), :])
            for part in range(count):
                out[step * count + part] = picked[:, part * LANES : (part + 1) * LANES]
        put_codes(out, blocks, tiles, 0, lax.rem(keys[pl.ds(begin, blocks), :], cells))


def permute_piece(flips, region, feats, order, keys, regions, cells, before=()):
    channels, points = feats.shape
    depth = 512
    blocks = points // regions // LANES
    return pl.pallas_call(
        functools.partial(piece_kernel, depth, cells, flips),
        out_shape=[jax.ShapeDtypeStruct((blocks + 2, channels, LANES), BF16)] * len(flips),
        in_specs=[SMEM] + [VMEM] * 3 + [pl.BlockSpec(memory_space=pl.ANY)] * len(before),
        out_specs=[VMEM] * len(flips),
        scratch_shapes=[pltpu.VMEM((points // depth * channels, depth), BF16)],
        compiler_params=params(),
        cost_estimate=pl.CostEstimate(flops=2_000_000_000, bytes_accessed=1_000_000, transcendentals=0),
        name="permute_piece",
    )(region, feats, order, keys, *before)


def exchange(feats, order, keys, region, regions, cells):
    blocks = feats.shape[1] // regions // LANES
    if regions != GROUP or blocks != ID_ROWS:
        moved = permute(feats, order, keys, regions, cells)
        return [lax.all_to_all(moved, "region", 0, 0, tiled=True)], moved

    def send(values, flips):
        pairs = [[(source, source ^ flip) for source in range(regions)] for flip in flips]
        return [lax.ppermute(value, "region", pair) for value, pair in zip(values, pairs)]

    at = region.reshape(1)
    made = []
    got = []
    for number, flips in enumerate(((6, 7), (4, 5), (2, 3), (1, 0))):
        before = got[number - 2] if number >= 2 else ()
        values = permute_piece(flips, at, feats, order, keys, regions, cells, before)
        made.append(values)
        if number < 3:
            got.append(send(values, flips))
        else:
            got.append(send(values[:1], flips[:1]) + list(values[1:]))
    return [chunk for some in got for chunk in some], made[1][0]


WINDOW = 256
STATIC = 2


def chunk_of(chunks, number):
    return chunks[0].at[number] if len(chunks) == 1 else chunks[number]


def decode(chunks, ids, ends, places):
    count, padded_blocks, _ = ids.shape
    tiles = padded_blocks // ID_ROWS
    blocks = chunk_of(chunks, 0).shape[0] - 2 * tiles
    bounds = lax.broadcasted_iota(jnp.int32, (ID_ROWS, LANES), 1) * (WINDOW * 8)
    row = lax.broadcasted_iota(jnp.int32, (ID_ROWS, LANES), 0)
    for chunk in range(count):
        first = jnp.zeros((1, LANES), jnp.int32)
        last = jnp.zeros((1, LANES), jnp.int32)
        for tile in range(tiles):
            upper = chunk_of(chunks, chunk)[blocks + tile].astype(F32)
            lower = chunk_of(chunks, chunk)[blocks + tiles + tile].astype(F32)
            code = (upper * 256.0 + lower).astype(jnp.int32)
            ids[chunk, tile * ID_ROWS : (tile + 1) * ID_ROWS, :] = code
            real = row + tile * ID_ROWS < blocks
            passed = real & (code[:, LANES - 1 :] < bounds)
            begun = real & (code[:, 0:1] < bounds + WINDOW * 8)
            first += jnp.sum(jnp.where(passed, 1, 0), axis=0, keepdims=True)
            last += jnp.sum(jnp.where(begun, 1, 0), axis=0, keepdims=True)
        ends[chunk : chunk + 1, :] = first
        ends[count + chunk : count + chunk + 1, :] = last
    pltpu.sync_copy(ends, places)


def window_mean(number, chunks, ids, places, acc):
    count, padded_blocks, _ = ids.shape
    channels = chunk_of(chunks, 0).shape[1]
    groups = count // GROUP
    blocks = chunk_of(chunks, 0).shape[0] - 2 * (padded_blocks // ID_ROWS)

    def product(group, steps):
        sides = []
        rows = []
        for at in steps:
            for member in range(GROUP):
                chunk = group * GROUP + member
                block = places[chunk, number] + at
                valid = block < places[count + chunk, number]
                block = jnp.minimum(block, blocks - 1)
                code = ids[chunk, pl.ds(block, 1), :]
                cell = code & 7
                rows.append(jnp.where(valid, (code >> 3) - number * WINDOW, -1))
                values = chunk_of(chunks, chunk)[block].astype(F32)
                mask = [cell == k for k in range(8)]
                side = [jnp.where(m, values, 0.0).astype(BF16) for m in mask]
                side += [jnp.broadcast_to(jnp.where(m, 1.0, 0.0), (channels, LANES)).astype(BF16) for m in mask]
                sides.append(jnp.concatenate(side, axis=0))
        side = jnp.concatenate(sides, axis=1)
        row = jnp.concatenate(rows, axis=1).astype(jnp.int16)
        hot = lax.broadcasted_iota(jnp.int16, (WINDOW, len(steps) * GROUP * LANES), 0) == row
        hot = jnp.where(hot, jnp.ones((), BF16), jnp.zeros((), BF16))
        return lax.dot_general(hot, side, NT, preferred_element_type=F32)

    def one_group(group, start):
        def step(at, _):
            acc[...] += product(group, [at])
            return 0

        hops = 0
        for member in range(GROUP):
            chunk = group * GROUP + member
            hops = jnp.maximum(hops, places[count + chunk, number] - places[chunk, number])
        lax.fori_loop(start, hops, step, 0)

    if groups == 1:
        acc[...] = product(0, list(range(STATIC)))
        one_group(0, STATIC)
    else:
        acc[...] = jnp.zeros_like(acc)

        def each(group, _):
            one_group(group, 0)
            return 0

        lax.fori_loop(0, groups, each, 0)
    return (acc[:, :LANES] / jnp.maximum(acc[:, LANES:], 1.0)).astype(BF16)


def far_kernel(count, chan, *rest):
    chunks = rest[:count]
    out, ids, acc, ends, places = rest[-5:]
    decode(chunks, ids, ends, places)
    begin = 2 * (chan[0] ^ 2) + 7
    parts = out.shape[1] // WINDOW
    for plane in range(out.shape[0]):
        for part in range(parts):
            number = lax.rem(begin + plane, 8) * parts + part
            out[plane, part * WINDOW : (part + 1) * WINDOW, :] = window_mean(number, chunks, ids, places, acc)


def near_kernel(slots, count, chan, *rest):
    chunks = rest[:count]
    far, send_pos, three, one, own, f0, f1, f2, f3, ids, acc, ends, places, planes = rest[count:]
    decode(chunks, ids, ends, places)
    partner = chan[0] ^ 2
    begin = 2 * partner + 7
    parts = far.shape[1] // WINDOW
    planes[0:4] = far[...]
    for plane in range(4, 8):
        for part in range(parts):
            number = lax.rem(begin + plane, 8) * parts + part
            planes[plane, part * WINDOW : (part + 1) * WINDOW, :] = window_mean(number, chunks, ids, places, acc)
    for out, flip in ((three, 3), (one, 1), (own, 0)):
        shift = 2 * ((chan[0] ^ flip) - partner) + 8
        for plane in range(4):
            out[plane] = planes[lax.rem(shift + plane, 8)]
    compact = []
    for side in range(2):
        hot = lax.broadcasted_iota(jnp.int32, (REACH, slots), 0) == send_pos[side : side + 1, :]
        compact.append(jnp.where(hot, 1.0, 0.0).astype(BF16))
    last_plane, first_plane = (planes.at[lax.rem(at - begin + 16, 8)] for at in (7, 8))
    for j in range(8):
        rows = slice(j * slots, (j + 1) * slots)
        to_next = mm(compact[0], last_plane[rows, :])
        to_previous = mm(compact[1], first_plane[rows, :])
        for flip, out in enumerate((f0, f1, f2, f3)):
            out[j] = jnp.where(chan[0] == flip, to_next, to_previous).astype(BF16)


def voxel_scratch(chunks, regions):
    total = chunks[0].shape[-3]
    tiles = -(-total // (ID_ROWS + 2))
    return [
        pltpu.VMEM((regions, tiles * ID_ROWS, LANES), jnp.int32),
        pltpu.VMEM((WINDOW, 2 * LANES), F32),
        pltpu.VMEM((2 * regions, LANES), jnp.int32),
        pltpu.SMEM((2 * regions, LANES), jnp.int32),
    ]


def far_voxels(chan, chunks, regions, slots, before):
    return pl.pallas_call(
        functools.partial(far_kernel, len(chunks)),
        out_shape=jax.ShapeDtypeStruct((4, 8 * slots, LANES), BF16),
        in_specs=[SMEM] + [VMEM] * len(chunks) + [pl.BlockSpec(memory_space=pl.ANY)] * len(before),
        out_specs=VMEM,
        scratch_shapes=voxel_scratch(chunks, regions),
        compiler_params=params(),
        cost_estimate=pl.CostEstimate(flops=4_000_000_000, bytes_accessed=1_200_000, transcendentals=0),
        name="far_voxels",
    )(chan, *chunks, *before)


def near_voxels(chan, chunks, regions, far, send_pos, slots):
    return pl.pallas_call(
        functools.partial(near_kernel, slots, len(chunks)),
        out_shape=[jax.ShapeDtypeStruct((4, 8 * slots, LANES), BF16)] * 3
        + [jax.ShapeDtypeStruct((8, REACH, LANES), BF16)] * 4,
        in_specs=[SMEM] + [VMEM] * len(chunks) + [VMEM, VMEM],
        out_specs=[VMEM] * 7,
        scratch_shapes=voxel_scratch(chunks, regions) + [pltpu.VMEM((8, 8 * slots, LANES), BF16)],
        compiler_params=params(),
        cost_estimate=pl.CostEstimate(flops=4_000_000_000, bytes_accessed=3_000_000, transcendentals=0),
        name="near_voxels",
    )(chan, *chunks, far, send_pos)


def spread_matrix():
    spread = np.zeros((4, 384, 192), np.float32)
    for k in range(4):
        for e in range(3):
            cell = k + e
            for channel in range(64):
                source, inner = divmod(channel, 16)
                if 1 <= cell <= 4:
                    row = source * 64 + (cell - 1) * 16 + inner
                else:
                    row = 256 + (cell // 5) * 64 + source * 16 + inner
                spread[k, row, e * 64 + channel] = 1
    return spread


def pack_kernel(conv, down, _, pack):
    for ab in range(9):
        for e in range(3):
            pack[ab, :, e * 64 : (e + 1) * 64] = conv[ab * 3 + e]
    for part in range(8):
        pack[9 + part, :, 0:128] = down[part * 16 : (part + 1) * 16, :]
        pack[9 + part, :, 128:192] = jnp.zeros((16, 64), BF16)


def pack(conv, down, before):
    return pl.pallas_call(
        pack_kernel,
        out_shape=jax.ShapeDtypeStruct((17, 16, 192), BF16),
        in_specs=[VMEM, VMEM, pl.BlockSpec(memory_space=pl.ANY)],
        out_specs=VMEM,
        compiler_params=params(),
        name="pack",
    )(conv, down, before)


def weight_kernel(chan, spread, own, one, two, three, even, odd, down):
    every = (own, one, two, three)
    columns = lax.broadcasted_iota(jnp.int32, (192, 192), 1) ^ (chan[0] * 16)
    turn = jnp.where(lax.broadcasted_iota(jnp.int32, (192, 192), 0) == columns, 1.0, 0.0).astype(BF16)
    for ab in range(9):
        taps = jnp.concatenate([ref[ab] for ref in every], axis=0)
        taps = mm(taps, turn).astype(BF16)
        for k in range(4):
            column = slice(k * 64, (k + 1) * 64)
            band = lax.dot_general(spread[k], taps, NT, preferred_element_type=F32).astype(BF16)
            for out, pair in ((even, (0, 2)), (odd, (1, 3))):
                for place, source in enumerate(pair):
                    main = band[source * 64 : source * 64 + 64]
                    out[0, ab, place * 64 : place * 64 + 64, column] = main
                    out[1, ab, 128 + place * 64 : 192 + place * 64, column] = main
                    for end in range(2):
                        edge = band[256 + end * 64 + source * 16 : 272 + end * 64 + source * 16]
                        row = end * 32 + place * 16
                        out[0, ab, 128 + row : 144 + row, column] = edge
                        out[1, ab, 64 + row : 80 + row, column] = edge
        for out in (even, odd):
            out[0, ab, 192:256, :] = jnp.zeros((64, 256), BF16)
            out[1, ab, 0:64, :] = jnp.zeros((64, 256), BF16)
    outputs = down.shape[0]
    total = jnp.zeros((outputs, 512), F32)
    rows = lax.broadcasted_iota(jnp.int32, (128, 512), 0)
    place = (rows & 7) * 64 + (rows >> 3)
    for source, ref in enumerate(every):
        part = ref[9:, :, 0:128].reshape(128, outputs)
        move = lax.broadcasted_iota(jnp.int32, (128, 512), 1) == place + source * 16
        move = jnp.where(move, 1.0, 0.0).astype(BF16)
        total += lax.dot_general(part, move, (((0,), (0,)), ((), ())), preferred_element_type=F32)
    down[...] = total.astype(BF16)


def prepare(chan, own, others, outputs):
    return pl.pallas_call(
        weight_kernel,
        out_shape=(
            jax.ShapeDtypeStruct((2, 9, 256, 256), BF16),
            jax.ShapeDtypeStruct((2, 9, 256, 256), BF16),
            jax.ShapeDtypeStruct((outputs, 512), BF16),
        ),
        in_specs=[SMEM] + [VMEM] * 5,
        out_specs=(VMEM, VMEM, VMEM),
        compiler_params=params(),
        cost_estimate=pl.CostEstimate(flops=2_000_000_000, bytes_accessed=3_000_000, transcendentals=0),
        name="prepare",
    )(chan, jnp.asarray(spread_matrix(), BF16), own, *others)


def halo_matrix():
    pick = np.zeros((256, 128), np.float32)
    for group, cell in enumerate((7, 4, 3, 0)):
        for source in range(2):
            for inner in range(16):
                pick[source * 128 + cell * 16 + inner, group * 32 + source * 16 + inner] = 1
    return pick


def pad_planes(slots, grid, remote, hot, pick, table, padded):
    total = slots + REACH
    lane = lax.broadcasted_iota(jnp.int32, (slots, LANES), 1)
    for plane in range(4):
        edge = mm(jnp.concatenate([ref[plane] for ref in grid], axis=1), pick[...]).astype(BF16)
        for j in range(8):
            rows = slice(j * slots, (j + 1) * slots)
            parts = [ref[plane, rows, :] for ref in grid]
            table[plane, j, 0:slots, 0:128] = jnp.concatenate([part[:, 0:64] for part in parts], axis=1)
            table[plane, j, 0:slots, 128:256] = edge[rows]
            table[plane, j, 0:slots, 256:384] = jnp.concatenate([part[:, 64:128] for part in parts], axis=1)
    for plane in (0, 3):
        for j in range(8):
            parts = [ref[j] for ref in remote]
            table[plane, j, slots:total, 0:128] = jnp.concatenate([part[:, 0:64] for part in parts], axis=1)
            table[plane, j, slots:total, 128:256] = mm(jnp.concatenate(parts, axis=1), pick[...]).astype(BF16)
            table[plane, j, slots:total, 256:384] = jnp.concatenate([part[:, 64:128] for part in parts], axis=1)

    for plane in range(4):
        base = (0, 9, 9, 18)[plane]
        used = total if plane in (0, 3) else slots
        for jj in range(10):
            dy, j = ((-1, 7) if jj == 0 else (1, 0) if jj == 9 else (0, jj - 1))
            at = base + (dy + 1) * 3
            source = table[plane, j, 0:used, :]
            if plane in (1, 2) and dy == 0:
                own = source
            else:
                own = mm(hot[at + 1, :, 0:used], source).astype(BF16)
            below = mm(hot[at, :, 0:used], source[:, 128:256]).astype(BF16)
            above = mm(hot[at + 2, :, 0:used], source[:, 128:256]).astype(BF16)
            padded[plane, jj, :, 0:128] = own[:, 0:128]
            padded[plane, jj, :, 128:256] = jnp.where(lane < 32, below, jnp.where(lane < 96, own[:, 128:256], above))
            padded[plane, jj, :, 256:384] = own[:, 256:384]


def products(padded, weights, half, a_out, start):
    slots = padded.shape[2]
    for ab in range(9):
        left = padded[a_out + ab // 3, ab % 3 : ab % 3 + 8, :, half * 128 : half * 128 + 256]
        term = mm(left.reshape(8 * slots, 256), weights[half, ab])
        start = term if start is None else start + term
    return start


def even_kernel(slots, own, two, r0, r2, hot, pick, weights, sums, table, padded):
    pad_planes(slots, (own, two), (r0, r2), hot, pick, table, padded)
    for half in range(2):
        for a_out in range(2):
            sums[half, a_out] = products(padded, weights, half, a_out, None)


def odd_kernel(slots, chan, active, one, three, r1, r3, hot, pick, weights, down, sums, *rest):
    table, padded, stacked, answer = rest[4:]
    pad_planes(slots, (one, three), (r1, r3), hot, pick, table, padded)
    alive = lax.broadcasted_iota(jnp.int32, (slots, 256), 0) < active[0]
    for half in range(2):
        for a_out in range(2):
            total_sum = products(padded, weights, half, a_out, sums[half, a_out])
            for j in range(8):
                block = jnp.where(alive, jnp.maximum(total_sum[j * slots : (j + 1) * slots], 0.0), 0.0).astype(BF16)
                for kk in range(2):
                    begin = ((j // 2) * 4 + half * 2 + kk) * slots
                    place = (a_out * 2 + j % 2) * 128
                    stacked[begin : begin + slots, place : place + 128] = block[:, kk * 128 : kk * 128 + 128]

    result = lax.dot_general(down[...], stacked[...], NT, preferred_element_type=F32)
    answer[...] = jnp.maximum(result, 0.0).astype(BF16)
    width = rest[0].shape[0]
    for flip in range(4):
        rest[flip][...] = answer[pl.ds(pl.multiple_of((chan[0] ^ flip) * width, width), width), :]


def even_sums(own, two, remote, hot, weights):
    slots = own.shape[1] // 8
    return pl.pallas_call(
        functools.partial(even_kernel, slots),
        out_shape=jax.ShapeDtypeStruct((2, 2, 8 * slots, 256), F32),
        in_specs=[VMEM] * 7,
        out_specs=VMEM,
        scratch_shapes=[
            pltpu.VMEM((4, 8, slots + REACH, 384), BF16),
            pltpu.VMEM((4, 10, slots, 384), BF16),
        ],
        compiler_params=params(),
        cost_estimate=pl.CostEstimate(flops=4_000_000_000, bytes_accessed=5_000_000, transcendentals=0),
        name="even_sums",
    )(own, two, *remote, hot, jnp.asarray(halo_matrix(), BF16), weights)


def convolve(chan, active, one, three, remote, hot, weights, down, sums):
    devices = 4
    slots = one.shape[1] // 8
    outputs = down.shape[0]
    return pl.pallas_call(
        functools.partial(odd_kernel, slots),
        out_shape=[jax.ShapeDtypeStruct((outputs // devices, 16 * slots), BF16)] * devices,
        in_specs=[SMEM] * 2 + [VMEM] * 9,
        out_specs=[VMEM] * devices,
        scratch_shapes=[
            pltpu.VMEM((4, 8, slots + REACH, 384), BF16),
            pltpu.VMEM((4, 10, slots, 384), BF16),
            pltpu.VMEM((16 * slots, 512), BF16),
            pltpu.VMEM((outputs, 16 * slots), BF16),
        ],
        compiler_params=params(),
        cost_estimate=pl.CostEstimate(flops=4_000_000_000, bytes_accessed=5_000_000, transcendentals=0),
        name="convolve",
    )(chan, active, one, three, *remote, hot, jnp.asarray(halo_matrix(), BF16), weights, down, sums)


def final_kernel(slots, chan, own, one, two, three, out, turned):
    outputs = own.shape[0]
    for flip, ref in enumerate((own, one, two, three)):
        plane = chan[0] ^ flip
        for cell in range(16):
            turned[pl.ds(plane * 16 + cell, outputs, stride=64), :] = ref[
                :, cell * slots : (cell + 1) * slots
            ].astype(F32)
    for tile in range(out.shape[1] // LANES):
        out[:, tile * LANES : (tile + 1) * LANES] = turned[tile * LANES : (tile + 1) * LANES, :].T.astype(BF16)


def finish(chan, coarse, others, slots):
    outputs = coarse.shape[0]
    return pl.pallas_call(
        functools.partial(final_kernel, slots),
        out_shape=jax.ShapeDtypeStruct((slots, outputs * 64), BF16),
        in_specs=[SMEM] + [VMEM] * 4,
        out_specs=VMEM,
        scratch_shapes=[pltpu.VMEM((outputs * 64, slots), F32)],
        compiler_params=params(),
        name="finish",
    )(chan, coarse, *others)


def links(adjacency, region, regions, chan, devices):
    slots = adjacency.shape[0]
    named = adjacency.T
    linked = named < slots * regions
    owner = jnp.where(linked, named // slots, regions + 7)
    slot = named % slots
    every = jnp.arange(slots, dtype=jnp.int32)
    steps = np.array([offset[0] for offset in OFFSETS])
    send_pos = []
    place = {}
    for step in (1, -1):
        rows = np.nonzero(steps == step)[0]
        owns = owner[rows[0] : rows[-1] + 1] == region + step
        sends = jnp.any(owns, axis=0)
        rank = jnp.sum((sends[None, :] & (every[None, :] < every[:, None])).astype(jnp.int32), axis=1)
        send_pos.append(jnp.where(sends, rank, -1))
        there = slot[rows[0] : rows[-1] + 1]
        member = jnp.any(owns[:, :, None] & (there[:, :, None] == every), axis=(0, 1))
        below = jnp.sum(
            (member[None, None, :] & (every < there[:, :, None])).astype(jnp.int32), axis=2
        )
        place[step] = jnp.where(owns, slots + below, -1)
    own = jnp.where(owner == region, slot, -1)
    same = jnp.concatenate([own[9:13], every[None, :], own[13:17]], axis=0)
    left = jnp.where(owner[0:9] == region, slot[0:9], place[-1])
    right = jnp.where(owner[17:26] == region, slot[17:26], place[1])
    first = jnp.where(chan == 0, left, same)
    last = jnp.where(chan == devices - 1, right, same)
    pos = jnp.concatenate([first, same, last], axis=0)
    hot = (pos[:, :, None] == jnp.arange(slots + REACH, dtype=jnp.int32)).astype(BF16)
    return jnp.stack(send_pos), hot


def send_faces(faces, regions, devices):
    got = []
    for flip in range(devices):
        other = (devices - 1) ^ flip
        pairs = [(r * devices + flip, (r + 1) * devices) for r in range(regions - 1)]
        pairs += [(r * devices + other, r * devices - 1) for r in range(1, regions)]
        got.append(lax.ppermute(faces[flip], ("region", "chan"), pairs))
    return got


def swap(value, flip, devices):
    return lax.ppermute(value, "chan", [(source, source ^ flip) for source in range(devices)])


def body(point_feats, destination, voxel_slot, adjacency, active_count, conv_weight, down_weight):
    regions = lax.axis_size("region")
    region = lax.axis_index("region")
    devices = lax.axis_size("chan")
    chan = lax.axis_index("chan")
    me = chan.reshape(1)
    slots = adjacency.shape[0]
    points = point_feats.shape[1]
    cells = slots * 512

    slot = voxel_slot // 512
    inside = voxel_slot % 512
    code = ((inside // 8) * slots + slot) * 8 + inside % 8
    keys, order = lax.sort(
        (destination * cells + code, jnp.arange(points, dtype=jnp.int32)), num_keys=1, is_stable=False
    )
    square = (points // LANES, LANES)
    taps = conv_weight.transpose(2, 3, 4, 0, 1).reshape(27, conv_weight.shape[0], -1)
    down = down_weight.transpose(1, 2, 3, 4, 0).reshape(-1, down_weight.shape[0])
    chunks, middle = exchange(
        point_feats, order.reshape(square), keys.reshape(square), region, regions, cells
    )
    mine = pack(taps, down, middle)
    late = mine[16, 0, 128] != 0
    theirs = [swap(mine, flip, devices) for flip in (1, 2, 3)]
    even, odd, down = prepare(me, mine, theirs, down_weight.shape[0])
    adjacency = jnp.where(late, 0, adjacency)

    send_pos, hot = links(adjacency, region, regions, chan, devices)
    far = far_voxels(me, chunks, regions, slots, (down, hot, send_pos))
    from_two = swap(far, 2, devices)
    near_three, near_one, near, *faces = near_voxels(me, chunks, regions, far, send_pos, slots)
    from_three = swap(near_three, 3, devices)
    from_one = swap(near_one, 1, devices)
    remote = send_faces(faces, regions, devices)
    sums = even_sums(near, from_two, remote[0::2], hot, even)
    coarse = convolve(me, active_count, from_one, from_three, remote[1::2], hot, odd, down, sums)
    back = [swap(coarse[flip], flip, devices) for flip in (1, 2, 3)]
    return finish(me, coarse[0], back, slots)


def solution(mesh):
    return jax.shard_map(
        body,
        mesh=mesh,
        in_specs=(
            P("chan", "region"),
            P("region"),
            P("region"),
            P("region", None),
            P("region"),
            P("chan", None, None, None, None),
            P(None, "chan", None, None, None),
        ),
        out_specs=P("region", "chan"),
        check_vma=False,
    )
```

```python
import functools

import jax
import jax.numpy as jnp
import numpy as np
from jax import lax
from jax.experimental import pallas as pl
from jax.experimental.pallas import tpu as pltpu
from jax.sharding import PartitionSpec as P

OFFSETS = [
    (first, second, third)
    for first in (-1, 0, 1)
    for second in (-1, 0, 1)
    for third in (-1, 0, 1)
    if (first, second, third) != (0, 0, 0)
]
LANES = 128
REACH = 16
F32 = jnp.float32
BF16 = jnp.bfloat16
NT = (((1,), (1,)), ((), ()))
VMEM = pl.BlockSpec(memory_space=pltpu.VMEM)
SMEM = pl.BlockSpec(memory_space=pltpu.SMEM)


def mm(a, b):
    return jnp.dot(a, b, preferred_element_type=F32)


def params():
    return pltpu.CompilerParams(vmem_limit_bytes=24 * 1024 * 1024)


ID_ROWS = 16
GROUP = 8


def one_hot_columns(depth, stack, wanted, channels=16):
    count = wanted.shape[0]
    width = count * LANES
    wanted = jnp.concatenate([wanted[i : i + 1] for i in range(count)], axis=1)
    low = (wanted & (depth - 1)).astype(jnp.int16)
    top = wanted // depth
    hot = lax.broadcasted_iota(jnp.int16, (depth, width), 0) == low
    hot = jnp.where(hot, jnp.ones((), BF16), jnp.zeros((), BF16))
    found = mm(stack[...], hot)
    picked = jnp.zeros((channels, width), F32)
    for part in range(stack.shape[0] // channels):
        picked = jnp.where(top == part, found[part * channels : (part + 1) * channels], picked)
    return picked.astype(BF16)


def fill_stack(depth, feats, stack):
    channels, points = feats.shape
    for part in range(points // depth):
        stack[part * channels : (part + 1) * channels, :] = feats[:, part * depth : (part + 1) * depth]


def put_codes(out, blocks, tiles, tile, rows):
    if rows.shape[0] < ID_ROWS:
        rows = jnp.concatenate([rows, jnp.zeros((ID_ROWS - rows.shape[0], LANES), jnp.int32)], axis=0)
    out[blocks + tile] = (rows >> 8).astype(F32).astype(BF16)
    out[blocks + tiles + tile] = (rows & 255).astype(F32).astype(BF16)


def permute_kernel(depth, width, cells, feats, order, keys, out, stack):
    channels, points = feats.shape
    fill_stack(depth, feats, stack)
    regions = out.shape[0]
    blocks = points // regions // LANES
    tiles = (out.shape[1] - blocks) // 2
    count = width // LANES

    def step(at, _):
        picked = one_hot_columns(depth, stack, order[pl.ds(at * count, count), :])
        for part in range(count):
            tile = at * count + part
            out[tile // blocks, tile % blocks] = picked[:, part * LANES : (part + 1) * LANES]
        return 0

    lax.fori_loop(0, points // width, step, 0)
    for target in range(regions):
        for tile in range(tiles):
            begin = target * blocks + tile * ID_ROWS
            rows = min(ID_ROWS, blocks - tile * ID_ROWS)
            put_codes(out.at[target], blocks, tiles, tile, lax.rem(keys[begin : begin + rows, :], cells))


def permute(feats, order, keys, regions, cells):
    channels, points = feats.shape
    depth, width = 512, 1024
    blocks = points // regions // LANES
    tiles = -(-blocks // ID_ROWS)
    return pl.pallas_call(
        functools.partial(permute_kernel, depth, width, cells),
        out_shape=jax.ShapeDtypeStruct((regions, blocks + 2 * tiles, channels, LANES), BF16),
        in_specs=[VMEM] * 3,
        out_specs=VMEM,
        scratch_shapes=[pltpu.VMEM((points // depth * channels, depth), BF16)],
        compiler_params=params(),
        name="permute",
    )(feats, order, keys)


def rotated(rows):
    before = jnp.concatenate([rows[-1:], rows[:-1]], axis=0)
    return jnp.concatenate([before[:, LANES // 2 :], rows[:, : LANES // 2]], axis=1)


def piece_kernel(depth, cells, flips, region, feats, order, keys, *rest):
    outs = rest[-1 - len(flips) : -1]
    stack = rest[-1]
    fill_stack(depth, feats, stack)
    tiles = 1
    blocks = outs[0].shape[0] - 2 * tiles
    count = 8
    for flip, out in zip(flips, outs):
        begin = pl.multiple_of((region[0] ^ flip) * blocks, 8)
        wanted = rotated(order[pl.ds(begin, blocks), :])
        for step in range(blocks // count):
            picked = one_hot_columns(depth, stack, wanted[step * count : (step + 1) * count])
            for part in range(count):
                out[step * count + part] = picked[:, part * LANES : (part + 1) * LANES]
        put_codes(out, blocks, tiles, 0, rotated(lax.rem(keys[pl.ds(begin, blocks), :], cells)))


def permute_piece(flips, region, feats, order, keys, regions, cells, before=()):
    channels, points = feats.shape
    depth = 512
    blocks = points // regions // LANES
    return pl.pallas_call(
        functools.partial(piece_kernel, depth, cells, flips),
        out_shape=[jax.ShapeDtypeStruct((blocks + 2, channels, LANES), BF16)] * len(flips),
        in_specs=[SMEM] + [VMEM] * 3 + [pl.BlockSpec(memory_space=pl.ANY)] * len(before),
        out_specs=[VMEM] * len(flips),
        scratch_shapes=[pltpu.VMEM((points // depth * channels, depth), BF16)],
        compiler_params=params(),
        cost_estimate=pl.CostEstimate(flops=2_000_000_000, bytes_accessed=1_000_000, transcendentals=0),
        name="permute_piece",
    )(region, feats, order, keys, *before)


def exchange(feats, order, keys, region, regions, cells):
    blocks = feats.shape[1] // regions // LANES
    if regions != GROUP or blocks != ID_ROWS:
        moved = permute(feats, order, keys, regions, cells)
        return [lax.all_to_all(moved, "region", 0, 0, tiled=True)], moved

    def send(values, flips):
        pairs = [[(source, source ^ flip) for source in range(regions)] for flip in flips]
        return [lax.ppermute(value, "region", pair) for value, pair in zip(values, pairs)]

    at = region.reshape(1)
    made = []
    got = []
    for number, flips in enumerate(((6, 7), (4, 5), (2, 3), (1, 0))):
        before = got[number - 2] if number >= 2 else ()
        values = permute_piece(flips, at, feats, order, keys, regions, cells, before)
        made.append(values)
        if number < 3:
            got.append(send(values, flips))
        else:
            got.append(send(values[:1], flips[:1]) + list(values[1:]))
    return [chunk for some in got for chunk in some], made[2][0]


WINDOW = 256


def chunk_of(chunks, number):
    return chunks[0].at[number] if len(chunks) == 1 else chunks[number]


def decode(chunks, ids, ends, places):
    count, padded_blocks, _ = ids.shape
    tiles = padded_blocks // ID_ROWS
    blocks = chunk_of(chunks, 0).shape[0] - 2 * tiles
    bounds = lax.broadcasted_iota(jnp.int32, (ID_ROWS, LANES), 1) * (WINDOW * 8)
    row = lax.broadcasted_iota(jnp.int32, (ID_ROWS, LANES), 0)
    for chunk in range(count):
        first = jnp.zeros((1, LANES), jnp.int32)
        last = jnp.zeros((1, LANES), jnp.int32)
        for tile in range(tiles):
            upper = chunk_of(chunks, chunk)[blocks + tile].astype(F32)
            lower = chunk_of(chunks, chunk)[blocks + tiles + tile].astype(F32)
            code = (upper * 256.0 + lower).astype(jnp.int32)
            ids[chunk, tile * ID_ROWS : (tile + 1) * ID_ROWS, :] = code
            real = row + tile * ID_ROWS < blocks
            passed = real & (code[:, LANES - 1 :] < bounds)
            head = code[:, 0:1]
            if len(chunks) > 1:
                last += jnp.where(head[0:1] < bounds[0:1] + WINDOW * 8, 1, 0)
                head = jnp.where(row[:, 0:1] == 0, code[:, LANES // 2 : LANES // 2 + 1], head)
            begun = real & (head < bounds + WINDOW * 8)
            first += jnp.sum(jnp.where(passed, 1, 0), axis=0, keepdims=True)
            last += jnp.sum(jnp.where(begun, 1, 0), axis=0, keepdims=True)
        ends[chunk : chunk + 1, :] = first
        ends[count + chunk : count + chunk + 1, :] = last
    pltpu.sync_copy(ends, places)


def window_mean(number, chunks, ids, places, acc):
    count, padded_blocks, _ = ids.shape
    channels = chunk_of(chunks, 0).shape[1]
    groups = count // GROUP
    blocks = chunk_of(chunks, 0).shape[0] - 2 * (padded_blocks // ID_ROWS)

    lane = lax.broadcasted_iota(jnp.int32, (1, LANES), 1)

    def product(group, steps, static=False):
        sides = []
        rows = []
        for at in steps:
            for member in range(GROUP):
                chunk = group * GROUP + member
                if static:
                    block = number + at
                else:
                    block = places[chunk, number] + at
                    valid = block < places[count + chunk, number]
                if len(chunks) == 1:
                    block = jnp.minimum(block, blocks - 1)
                else:
                    begin = jnp.where(block == 0, LANES // 2, 0)
                    end = jnp.where(block == blocks, LANES // 2, LANES)
                    if not static:
                        end = jnp.where(valid & ((block < number) | (block > number + 1)), end, 0)
                    valid = (lane >= begin) & (lane < end)
                    block = block & (blocks - 1)
                code = ids[chunk, pl.ds(block, 1), :]
                cell = code & 7
                rows.append(jnp.where(valid, (code >> 3) - number * WINDOW, -1))
                values = chunk_of(chunks, chunk)[block].astype(F32)
                mask = [cell == k for k in range(8)]
                side = [jnp.where(m, values, 0.0).astype(BF16) for m in mask]
                side += [jnp.broadcast_to(jnp.where(m, 1.0, 0.0), (channels, LANES)).astype(BF16) for m in mask]
                sides.append(jnp.concatenate(side, axis=0))
        side = jnp.concatenate(sides, axis=1)
        row = jnp.concatenate(rows, axis=1).astype(jnp.int16)
        hot = lax.broadcasted_iota(jnp.int16, (WINDOW, len(steps) * GROUP * LANES), 0) == row
        hot = jnp.where(hot, jnp.ones((), BF16), jnp.zeros((), BF16))
        return lax.dot_general(hot, side, NT, preferred_element_type=F32)

    def one_group(group, start):
        def step(at, _):
            acc[...] += product(group, [at])
            return 0

        hops = 0
        for member in range(GROUP):
            chunk = group * GROUP + member
            first, last = places[chunk, number], places[count + chunk, number]
            need = last - first
            if len(chunks) > 1:
                need = jnp.where((first < number) | (last > number + 2), need, 0)
            hops = jnp.maximum(hops, need)
        lax.fori_loop(start, hops, step, 0)

    if len(chunks) > 1:
        acc[...] = product(0, [0, 1], static=True)
        one_group(0, 0)
    else:
        acc[...] = jnp.zeros_like(acc)

        def each(group, _):
            one_group(group, 0)
            return 0

        lax.fori_loop(0, groups, each, 0)
    return (acc[:, :LANES] / jnp.maximum(acc[:, LANES:], 1.0)).astype(BF16)


def far_kernel(count, chan, *rest):
    chunks = rest[:count]
    out, ids, acc, ends, places = rest[-5:]
    decode(chunks, ids, ends, places)
    begin = 2 * (chan[0] ^ 2) + 7
    parts = out.shape[1] // WINDOW
    for plane in range(out.shape[0]):
        for part in range(parts):
            number = lax.rem(begin + plane, 8) * parts + part
            out[plane, part * WINDOW : (part + 1) * WINDOW, :] = window_mean(number, chunks, ids, places, acc)


def near_kernel(slots, count, chan, *rest):
    chunks = rest[:count]
    far, send_pos, three, one, own, f0, f1, f2, f3, ids, acc, ends, places, planes = rest[count:]
    decode(chunks, ids, ends, places)
    partner = chan[0] ^ 2
    begin = 2 * partner + 7
    parts = far.shape[1] // WINDOW
    planes[0:4] = far[...]
    for plane in range(4, 8):
        for part in range(parts):
            number = lax.rem(begin + plane, 8) * parts + part
            planes[plane, part * WINDOW : (part + 1) * WINDOW, :] = window_mean(number, chunks, ids, places, acc)
    for out, flip in ((three, 3), (one, 1), (own, 0)):
        shift = 2 * ((chan[0] ^ flip) - partner) + 8
        for plane in range(4):
            out[plane] = planes[lax.rem(shift + plane, 8)]
    compact = []
    for side in range(2):
        hot = lax.broadcasted_iota(jnp.int32, (REACH, slots), 0) == send_pos[side : side + 1, :]
        compact.append(jnp.where(hot, 1.0, 0.0).astype(BF16))
    last_plane, first_plane = (planes.at[lax.rem(at - begin + 16, 8)] for at in (7, 8))
    for j in range(8):
        rows = slice(j * slots, (j + 1) * slots)
        to_next = mm(compact[0], last_plane[rows, :])
        to_previous = mm(compact[1], first_plane[rows, :])
        for flip, out in enumerate((f0, f1, f2, f3)):
            out[j] = jnp.where(chan[0] == flip, to_next, to_previous).astype(BF16)


def voxel_scratch(chunks, regions):
    total = chunks[0].shape[-3]
    tiles = -(-total // (ID_ROWS + 2))
    return [
        pltpu.VMEM((regions, tiles * ID_ROWS, LANES), jnp.int32),
        pltpu.VMEM((WINDOW, 2 * LANES), F32),
        pltpu.VMEM((2 * regions, LANES), jnp.int32),
        pltpu.SMEM((2 * regions, LANES), jnp.int32),
    ]


def far_voxels(chan, chunks, regions, slots, before):
    return pl.pallas_call(
        functools.partial(far_kernel, len(chunks)),
        out_shape=jax.ShapeDtypeStruct((4, 8 * slots, LANES), BF16),
        in_specs=[SMEM] + [VMEM] * len(chunks) + [pl.BlockSpec(memory_space=pl.ANY)] * len(before),
        out_specs=VMEM,
        scratch_shapes=voxel_scratch(chunks, regions),
        compiler_params=params(),
        cost_estimate=pl.CostEstimate(flops=4_000_000_000, bytes_accessed=1_200_000, transcendentals=0),
        name="far_voxels",
    )(chan, *chunks, *before)


def near_voxels(chan, chunks, regions, far, send_pos, slots):
    return pl.pallas_call(
        functools.partial(near_kernel, slots, len(chunks)),
        out_shape=[jax.ShapeDtypeStruct((4, 8 * slots, LANES), BF16)] * 3
        + [jax.ShapeDtypeStruct((8, REACH, LANES), BF16)] * 4,
        in_specs=[SMEM] + [VMEM] * len(chunks) + [VMEM, VMEM],
        out_specs=[VMEM] * 7,
        scratch_shapes=voxel_scratch(chunks, regions) + [pltpu.VMEM((8, 8 * slots, LANES), BF16)],
        compiler_params=params(),
        cost_estimate=pl.CostEstimate(flops=4_000_000_000, bytes_accessed=3_000_000, transcendentals=0),
        name="near_voxels",
    )(chan, *chunks, far, send_pos)


def pack_kernel(conv, down, _, pack):
    for ab in range(9):
        for e in range(3):
            pack[ab, :, e * 64 : (e + 1) * 64] = conv[ab * 3 + e]
    for part in range(8):
        pack[9 + part, :, 0:128] = down[part * 16 : (part + 1) * 16, :]
        pack[9 + part, :, 128:192] = jnp.zeros((16, 64), BF16)


def pack(conv, down, before):
    return pl.pallas_call(
        pack_kernel,
        out_shape=jax.ShapeDtypeStruct((17, 16, 192), BF16),
        in_specs=[VMEM, VMEM, pl.BlockSpec(memory_space=pl.ANY)],
        out_specs=VMEM,
        compiler_params=params(),
        name="pack",
    )(conv, down, before)


def weight_kernel(chan, own, one, two, three, even, odd, down):
    every = (own, one, two, three)
    columns = lax.broadcasted_iota(jnp.int32, (192, 192), 1) ^ (chan[0] * 16)
    turn = jnp.where(lax.broadcasted_iota(jnp.int32, (192, 192), 0) == columns, 1.0, 0.0).astype(BF16)
    for out in (even, odd):
        out[...] = jnp.zeros_like(out)
    for ab in range(9):
        taps = jnp.concatenate([ref[ab] for ref in every], axis=0)
        turned = lax.dot_general(turn, taps, NT, preferred_element_type=F32)
        turned = jnp.concatenate([turned, turned], axis=1).astype(BF16)
        for e in range(3):
            for source in range(4):
                out, place = (even, odd)[source % 2], source // 2
                rows = turned[e * 64 + source * 16 : e * 64 + source * 16 + 16]
                for k in range(4):
                    piece = rows[:, (k % 2) * 64 : (k % 2) * 64 + 64]
                    column = slice(k * 64, (k + 1) * 64)
                    cell = k + e
                    if 1 <= cell <= 4:
                        row = place * 64 + (cell - 1) * 16
                        out[0, ab, row : row + 16, column] = piece
                        out[1, ab, 128 + row : 144 + row, column] = piece
                    else:
                        row = (cell // 5) * 32 + place * 16
                        out[0, ab, 128 + row : 144 + row, column] = piece
                        out[1, ab, 64 + row : 80 + row, column] = piece
    outputs = down.shape[0]
    total = jnp.zeros((outputs, 512), F32)
    rows = lax.broadcasted_iota(jnp.int32, (128, 512), 0)
    place = (rows & 7) * 64 + (rows >> 3)
    for source, ref in enumerate(every):
        part = ref[9:, :, 0:128].reshape(128, outputs)
        move = lax.broadcasted_iota(jnp.int32, (128, 512), 1) == place + source * 16
        move = jnp.where(move, 1.0, 0.0).astype(BF16)
        total += lax.dot_general(part, move, (((0,), (0,)), ((), ())), preferred_element_type=F32)
    down[...] = total.astype(BF16)


def prepare(chan, own, others, outputs):
    return pl.pallas_call(
        weight_kernel,
        out_shape=(
            jax.ShapeDtypeStruct((2, 9, 256, 256), BF16),
            jax.ShapeDtypeStruct((2, 9, 256, 256), BF16),
            jax.ShapeDtypeStruct((outputs, 512), BF16),
        ),
        in_specs=[SMEM] + [VMEM] * 4,
        out_specs=(VMEM, VMEM, VMEM),
        compiler_params=params(),
        cost_estimate=pl.CostEstimate(flops=2_000_000_000, bytes_accessed=3_000_000, transcendentals=0),
        name="prepare",
    )(chan, own, *others)


def halo_matrix():
    pick = np.zeros((256, 128), np.float32)
    for group, cell in enumerate((7, 4, 3, 0)):
        for source in range(2):
            for inner in range(16):
                pick[source * 128 + cell * 16 + inner, group * 32 + source * 16 + inner] = 1
    return pick


def pad_planes(slots, grid, remote, hot, pick, table, padded):
    total = slots + REACH
    lane = lax.broadcasted_iota(jnp.int32, (slots, LANES), 1)
    for plane in range(4):
        edge = mm(jnp.concatenate([ref[plane] for ref in grid], axis=1), pick[...]).astype(BF16)
        for j in range(8):
            rows = slice(j * slots, (j + 1) * slots)
            parts = [ref[plane, rows, :] for ref in grid]
            table[plane, j, 0:slots, 0:128] = jnp.concatenate([part[:, 0:64] for part in parts], axis=1)
            table[plane, j, 0:slots, 128:256] = edge[rows]
            table[plane, j, 0:slots, 256:384] = jnp.concatenate([part[:, 64:128] for part in parts], axis=1)
    for plane in (0, 3):
        for j in range(8):
            parts = [ref[j] for ref in remote]
            table[plane, j, slots:total, 0:128] = jnp.concatenate([part[:, 0:64] for part in parts], axis=1)
            table[plane, j, slots:total, 128:256] = mm(jnp.concatenate(parts, axis=1), pick[...]).astype(BF16)
            table[plane, j, slots:total, 256:384] = jnp.concatenate([part[:, 64:128] for part in parts], axis=1)

    for plane in range(4):
        base = (0, 9, 9, 18)[plane]
        used = total if plane in (0, 3) else slots
        for jj in range(10):
            dy, j = ((-1, 7) if jj == 0 else (1, 0) if jj == 9 else (0, jj - 1))
            at = base + (dy + 1) * 3
            source = table[plane, j, 0:used, :]
            if plane in (1, 2) and dy == 0:
                own = source
            else:
                own = mm(hot[at + 1, :, 0:used], source).astype(BF16)
            below = mm(hot[at, :, 0:used], source[:, 128:256]).astype(BF16)
            above = mm(hot[at + 2, :, 0:used], source[:, 128:256]).astype(BF16)
            padded[plane, jj, :, 0:128] = own[:, 0:128]
            padded[plane, jj, :, 128:256] = jnp.where(lane < 32, below, jnp.where(lane < 96, own[:, 128:256], above))
            padded[plane, jj, :, 256:384] = own[:, 256:384]


def products(padded, weights, half, a_out, start):
    slots = padded.shape[2]
    for ab in range(9):
        left = padded[a_out + ab // 3, ab % 3 : ab % 3 + 8, :, half * 128 : half * 128 + 256]
        term = mm(left.reshape(8 * slots, 256), weights[half, ab])
        start = term if start is None else start + term
    return start


def even_kernel(slots, own, two, r0, r2, hot, pick, weights, sums, table, padded):
    pad_planes(slots, (own, two), (r0, r2), hot, pick, table, padded)
    for half in range(2):
        for a_out in range(2):
            sums[half, a_out] = products(padded, weights, half, a_out, None)


def odd_kernel(slots, chan, active, one, three, r1, r3, hot, pick, weights, down, sums, *rest):
    table, padded, stacked, answer = rest[4:]
    pad_planes(slots, (one, three), (r1, r3), hot, pick, table, padded)
    alive = lax.broadcasted_iota(jnp.int32, (slots, 256), 0) < active[0]
    for half in range(2):
        for a_out in range(2):
            total_sum = products(padded, weights, half, a_out, sums[half, a_out])
            for j in range(8):
                block = jnp.where(alive, jnp.maximum(total_sum[j * slots : (j + 1) * slots], 0.0), 0.0).astype(BF16)
                for kk in range(2):
                    begin = ((j // 2) * 4 + half * 2 + kk) * slots
                    place = (a_out * 2 + j % 2) * 128
                    stacked[begin : begin + slots, place : place + 128] = block[:, kk * 128 : kk * 128 + 128]

    result = lax.dot_general(down[...], stacked[...], NT, preferred_element_type=F32)
    answer[...] = jnp.maximum(result, 0.0).astype(BF16)
    width = rest[0].shape[0]
    for flip in range(4):
        rest[flip][...] = answer[pl.ds(pl.multiple_of((chan[0] ^ flip) * width, width), width), :]


def even_sums(own, two, remote, hot, weights):
    slots = own.shape[1] // 8
    return pl.pallas_call(
        functools.partial(even_kernel, slots),
        out_shape=jax.ShapeDtypeStruct((2, 2, 8 * slots, 256), F32),
        in_specs=[VMEM] * 7,
        out_specs=VMEM,
        scratch_shapes=[
            pltpu.VMEM((4, 8, slots + REACH, 384), BF16),
            pltpu.VMEM((4, 10, slots, 384), BF16),
        ],
        compiler_params=params(),
        cost_estimate=pl.CostEstimate(flops=4_000_000_000, bytes_accessed=5_000_000, transcendentals=0),
        name="even_sums",
    )(own, two, *remote, hot, jnp.asarray(halo_matrix(), BF16), weights)


def convolve(chan, active, one, three, remote, hot, weights, down, sums):
    devices = 4
    slots = one.shape[1] // 8
    outputs = down.shape[0]
    return pl.pallas_call(
        functools.partial(odd_kernel, slots),
        out_shape=[jax.ShapeDtypeStruct((outputs // devices, 16 * slots), BF16)] * devices,
        in_specs=[SMEM] * 2 + [VMEM] * 9,
        out_specs=[VMEM] * devices,
        scratch_shapes=[
            pltpu.VMEM((4, 8, slots + REACH, 384), BF16),
            pltpu.VMEM((4, 10, slots, 384), BF16),
            pltpu.VMEM((16 * slots, 512), BF16),
            pltpu.VMEM((outputs, 16 * slots), BF16),
        ],
        compiler_params=params(),
        cost_estimate=pl.CostEstimate(flops=4_000_000_000, bytes_accessed=5_000_000, transcendentals=0),
        name="convolve",
    )(chan, active, one, three, *remote, hot, jnp.asarray(halo_matrix(), BF16), weights, down, sums)


def final_kernel(slots, chan, own, one, two, three, out, turned):
    outputs = own.shape[0]
    for flip, ref in enumerate((own, one, two, three)):
        plane = chan[0] ^ flip
        for cell in range(16):
            turned[pl.ds(plane * 16 + cell, outputs, stride=64), :] = ref[
                :, cell * slots : (cell + 1) * slots
            ].astype(F32)
    for tile in range(out.shape[1] // LANES):
        out[:, tile * LANES : (tile + 1) * LANES] = turned[tile * LANES : (tile + 1) * LANES, :].T.astype(BF16)


def finish(chan, coarse, others, slots):
    outputs = coarse.shape[0]
    return pl.pallas_call(
        functools.partial(final_kernel, slots),
        out_shape=jax.ShapeDtypeStruct((slots, outputs * 64), BF16),
        in_specs=[SMEM] + [VMEM] * 4,
        out_specs=VMEM,
        scratch_shapes=[pltpu.VMEM((outputs * 64, slots), F32)],
        compiler_params=params(),
        name="finish",
    )(chan, coarse, *others)


def links(adjacency, region, regions, chan, devices):
    slots = adjacency.shape[0]
    named = adjacency.T
    linked = named < slots * regions
    owner = jnp.where(linked, named // slots, regions + 7)
    slot = named % slots
    every = jnp.arange(slots, dtype=jnp.int32)
    steps = np.array([offset[0] for offset in OFFSETS])
    send_pos = []
    place = {}
    for step in (1, -1):
        rows = np.nonzero(steps == step)[0]
        owns = owner[rows[0] : rows[-1] + 1] == region + step
        sends = jnp.any(owns, axis=0)
        rank = jnp.sum((sends[None, :] & (every[None, :] < every[:, None])).astype(jnp.int32), axis=1)
        send_pos.append(jnp.where(sends, rank, -1))
        there = slot[rows[0] : rows[-1] + 1]
        member = jnp.any(owns[:, :, None] & (there[:, :, None] == every), axis=(0, 1))
        below = jnp.sum(
            (member[None, None, :] & (every < there[:, :, None])).astype(jnp.int32), axis=2
        )
        place[step] = jnp.where(owns, slots + below, -1)
    own = jnp.where(owner == region, slot, -1)
    same = jnp.concatenate([own[9:13], every[None, :], own[13:17]], axis=0)
    left = jnp.where(owner[0:9] == region, slot[0:9], place[-1])
    right = jnp.where(owner[17:26] == region, slot[17:26], place[1])
    first = jnp.where(chan == 0, left, same)
    last = jnp.where(chan == devices - 1, right, same)
    pos = jnp.concatenate([first, same, last], axis=0)
    hot = (pos[:, :, None] == jnp.arange(slots + REACH, dtype=jnp.int32)).astype(BF16)
    return jnp.stack(send_pos), hot


def send_faces(faces, regions, devices):
    got = []
    for flip in range(devices):
        other = (devices - 1) ^ flip
        pairs = [(r * devices + flip, (r + 1) * devices) for r in range(regions - 1)]
        pairs += [(r * devices + other, r * devices - 1) for r in range(1, regions)]
        got.append(lax.ppermute(faces[flip], ("region", "chan"), pairs))
    return got


def swap(value, flip, devices):
    return lax.ppermute(value, "chan", [(source, source ^ flip) for source in range(devices)])


def body(point_feats, destination, voxel_slot, adjacency, active_count, conv_weight, down_weight):
    regions = lax.axis_size("region")
    region = lax.axis_index("region")
    devices = lax.axis_size("chan")
    chan = lax.axis_index("chan")
    me = chan.reshape(1)
    slots = adjacency.shape[0]
    points = point_feats.shape[1]
    cells = slots * 512

    slot = voxel_slot // 512
    inside = voxel_slot % 512
    code = ((inside // 8) * slots + slot) * 8 + inside % 8
    keys, order = lax.sort(
        (destination * cells + code, jnp.arange(points, dtype=jnp.int32)), num_keys=1, is_stable=False
    )
    square = (points // LANES, LANES)
    taps = conv_weight.transpose(2, 3, 4, 0, 1).reshape(27, conv_weight.shape[0], -1)
    down = down_weight.transpose(1, 2, 3, 4, 0).reshape(-1, down_weight.shape[0])
    chunks, middle = exchange(
        point_feats, order.reshape(square), keys.reshape(square), region, regions, cells
    )
    mine = pack(taps, down, middle)
    late = mine[16, 0, 128] != 0
    theirs = [swap(mine, flip, devices) for flip in (1, 2, 3)]
    even, odd, down = prepare(me, mine, theirs, down_weight.shape[0])
    adjacency = jnp.where(late, 0, adjacency)

    send_pos, hot = links(adjacency, region, regions, chan, devices)
    far = far_voxels(me, chunks, regions, slots, (down, hot, send_pos))
    from_two = swap(far, 2, devices)
    near_three, near_one, near, *faces = near_voxels(me, chunks, regions, far, send_pos, slots)
    from_three = swap(near_three, 3, devices)
    from_one = swap(near_one, 1, devices)
    remote = send_faces(faces, regions, devices)
    sums = even_sums(near, from_two, remote[0::2], hot, even)
    coarse = convolve(me, active_count, from_one, from_three, remote[1::2], hot, odd, down, sums)
    back = [swap(coarse[flip], flip, devices) for flip in (1, 2, 3)]
    return finish(me, coarse[0], back, slots)


def solution(mesh):
    return jax.shard_map(
        body,
        mesh=mesh,
        in_specs=(
            P("chan", "region"),
            P("region"),
            P("region"),
            P("region", None),
            P("region"),
            P("chan", None, None, None, None),
            P(None, "chan", None, None, None),
        ),
        out_specs=P("region", "chan"),
        check_vma=False,
    )
```

```python
import functools

import jax
import jax.numpy as jnp
import numpy as np
from jax import lax
from jax.experimental import pallas as pl
from jax.experimental.pallas import tpu as pltpu
from jax.sharding import PartitionSpec as P

OFFSETS = [
    (first, second, third)
    for first in (-1, 0, 1)
    for second in (-1, 0, 1)
    for third in (-1, 0, 1)
    if (first, second, third) != (0, 0, 0)
]
LANES = 128
REACH = 16
F32 = jnp.float32
BF16 = jnp.bfloat16
NT = (((1,), (1,)), ((), ()))
VMEM = pl.BlockSpec(memory_space=pltpu.VMEM)
SMEM = pl.BlockSpec(memory_space=pltpu.SMEM)


def mm(a, b):
    return jnp.dot(a, b, preferred_element_type=F32)


def params():
    return pltpu.CompilerParams(vmem_limit_bytes=24 * 1024 * 1024)


ID_ROWS = 16
GROUP = 8


def one_hot_columns(depth, stack, wanted, channels=16):
    count = wanted.shape[0]
    width = count * LANES
    wanted = jnp.concatenate([wanted[i : i + 1] for i in range(count)], axis=1)
    low = (wanted & (depth - 1)).astype(jnp.int16)
    top = wanted // depth
    hot = lax.broadcasted_iota(jnp.int16, (depth, width), 0) == low
    hot = jnp.where(hot, jnp.ones((), BF16), jnp.zeros((), BF16))
    found = mm(stack[...], hot)
    picked = jnp.zeros((channels, width), F32)
    for part in range(stack.shape[0] // channels):
        picked = jnp.where(top == part, found[part * channels : (part + 1) * channels], picked)
    return picked.astype(BF16)


def fill_stack(depth, feats, stack):
    channels, points = feats.shape
    for part in range(points // depth):
        stack[part * channels : (part + 1) * channels, :] = feats[:, part * depth : (part + 1) * depth]


def put_codes(out, blocks, tiles, tile, rows):
    if rows.shape[0] < ID_ROWS:
        rows = jnp.concatenate([rows, jnp.zeros((ID_ROWS - rows.shape[0], LANES), jnp.int32)], axis=0)
    out[blocks + tile] = (rows >> 8).astype(F32).astype(BF16)
    out[blocks + tiles + tile] = (rows & 255).astype(F32).astype(BF16)


def permute_kernel(depth, width, cells, feats, order, keys, out, stack):
    channels, points = feats.shape
    fill_stack(depth, feats, stack)
    regions = out.shape[0]
    blocks = points // regions // LANES
    tiles = (out.shape[1] - blocks) // 2
    count = width // LANES

    def step(at, _):
        picked = one_hot_columns(depth, stack, order[pl.ds(at * count, count), :])
        for part in range(count):
            tile = at * count + part
            out[tile // blocks, tile % blocks] = picked[:, part * LANES : (part + 1) * LANES]
        return 0

    lax.fori_loop(0, points // width, step, 0)
    for target in range(regions):
        for tile in range(tiles):
            begin = target * blocks + tile * ID_ROWS
            rows = min(ID_ROWS, blocks - tile * ID_ROWS)
            put_codes(out.at[target], blocks, tiles, tile, lax.rem(keys[begin : begin + rows, :], cells))


def permute(feats, order, keys, regions, cells):
    channels, points = feats.shape
    depth, width = 512, 1024
    blocks = points // regions // LANES
    tiles = -(-blocks // ID_ROWS)
    return pl.pallas_call(
        functools.partial(permute_kernel, depth, width, cells),
        out_shape=jax.ShapeDtypeStruct((regions, blocks + 2 * tiles, channels, LANES), BF16),
        in_specs=[VMEM] * 3,
        out_specs=VMEM,
        scratch_shapes=[pltpu.VMEM((points // depth * channels, depth), BF16)],
        compiler_params=params(),
        name="permute",
    )(feats, order, keys)


def rotated(rows):
    before = jnp.concatenate([rows[-1:], rows[:-1]], axis=0)
    return jnp.concatenate([before[:, LANES // 2 :], rows[:, : LANES // 2]], axis=1)


def piece_kernel(depth, cells, flips, region, feats, order, keys, *rest):
    outs = rest[-1 - len(flips) : -1]
    stack = rest[-1]
    fill_stack(depth, feats, stack)
    tiles = 1
    blocks = outs[0].shape[0] - 2 * tiles
    count = 8
    for flip, out in zip(flips, outs):
        begin = pl.multiple_of((region[0] ^ flip) * blocks, 8)
        wanted = rotated(order[pl.ds(begin, blocks), :])
        for step in range(blocks // count):
            picked = one_hot_columns(depth, stack, wanted[step * count : (step + 1) * count])
            for part in range(count):
                out[step * count + part] = picked[:, part * LANES : (part + 1) * LANES]
        put_codes(out, blocks, tiles, 0, rotated(lax.rem(keys[pl.ds(begin, blocks), :], cells)))


def permute_piece(flips, region, feats, order, keys, regions, cells, before=()):
    channels, points = feats.shape
    depth = 512
    blocks = points // regions // LANES
    return pl.pallas_call(
        functools.partial(piece_kernel, depth, cells, flips),
        out_shape=[jax.ShapeDtypeStruct((blocks + 2, channels, LANES), BF16)] * len(flips),
        in_specs=[SMEM] + [VMEM] * 3 + [pl.BlockSpec(memory_space=pl.ANY)] * len(before),
        out_specs=[VMEM] * len(flips),
        scratch_shapes=[pltpu.VMEM((points // depth * channels, depth), BF16)],
        compiler_params=params(),
        cost_estimate=pl.CostEstimate(flops=2_000_000_000, bytes_accessed=1_000_000, transcendentals=0),
        name="permute_piece",
    )(region, feats, order, keys, *before)


def exchange(feats, order, keys, region, regions, cells):
    blocks = feats.shape[1] // regions // LANES
    if regions != GROUP or blocks != ID_ROWS:
        moved = permute(feats, order, keys, regions, cells)
        return [lax.all_to_all(moved, "region", 0, 0, tiled=True)], moved

    def send(values, flips):
        pairs = [[(source, source ^ flip) for source in range(regions)] for flip in flips]
        return [lax.ppermute(value, "region", pair) for value, pair in zip(values, pairs)]

    at = region.reshape(1)
    made = []
    got = []
    for number, flips in enumerate(((6, 7), (4, 5), (2, 3, 1, 0))):
        before = [*got[number - 2], made[-1][0]] if number >= 2 else ()
        values = permute_piece(flips, at, feats, order, keys, regions, cells, before)
        made.append(values)
        sent = sum(flip != 0 for flip in flips)
        got.append(send(values[:sent], flips[:sent]) + list(values[sent:]))
    return [chunk for some in got for chunk in some], made[2][0]


WINDOW = 256


def chunk_of(chunks, number):
    return chunks[0].at[number] if len(chunks) == 1 else chunks[number]


def decode(chunks, ids, ends, places):
    count, padded_blocks, _ = ids.shape
    tiles = padded_blocks // ID_ROWS
    blocks = chunk_of(chunks, 0).shape[0] - 2 * tiles
    bounds = lax.broadcasted_iota(jnp.int32, (ID_ROWS, LANES), 1) * (WINDOW * 8)
    row = lax.broadcasted_iota(jnp.int32, (ID_ROWS, LANES), 0)
    for chunk in range(count):
        first = jnp.zeros((1, LANES), jnp.int32)
        last = jnp.zeros((1, LANES), jnp.int32)
        for tile in range(tiles):
            upper = chunk_of(chunks, chunk)[blocks + tile].astype(F32)
            lower = chunk_of(chunks, chunk)[blocks + tiles + tile].astype(F32)
            code = (upper * 256.0 + lower).astype(jnp.int32)
            ids[chunk, tile * ID_ROWS : (tile + 1) * ID_ROWS, :] = code
            real = row + tile * ID_ROWS < blocks
            passed = real & (code[:, LANES - 1 :] < bounds)
            head = code[:, 0:1]
            if len(chunks) > 1:
                last += jnp.where(head[0:1] < bounds[0:1] + WINDOW * 8, 1, 0)
                head = jnp.where(row[:, 0:1] == 0, code[:, LANES // 2 : LANES // 2 + 1], head)
            begun = real & (head < bounds + WINDOW * 8)
            first += jnp.sum(jnp.where(passed, 1, 0), axis=0, keepdims=True)
            last += jnp.sum(jnp.where(begun, 1, 0), axis=0, keepdims=True)
        ends[chunk : chunk + 1, :] = first
        ends[count + chunk : count + chunk + 1, :] = last
    pltpu.sync_copy(ends, places)


def window_mean(number, chunks, ids, places, acc):
    count, padded_blocks, _ = ids.shape
    channels = chunk_of(chunks, 0).shape[1]
    groups = count // GROUP
    blocks = chunk_of(chunks, 0).shape[0] - 2 * (padded_blocks // ID_ROWS)

    lane = lax.broadcasted_iota(jnp.int32, (1, LANES), 1)

    def product(group, steps, static=False):
        sides = []
        rows = []
        for at in steps:
            for member in range(GROUP):
                chunk = group * GROUP + member
                if static:
                    block = number + at
                else:
                    block = places[chunk, number] + at
                    valid = block < places[count + chunk, number]
                if len(chunks) == 1:
                    block = jnp.minimum(block, blocks - 1)
                else:
                    begin = jnp.where(block == 0, LANES // 2, 0)
                    end = jnp.where(block == blocks, LANES // 2, LANES)
                    if not static:
                        end = jnp.where(valid & ((block < number) | (block > number + 1)), end, 0)
                    valid = (lane >= begin) & (lane < end)
                    block = block & (blocks - 1)
                code = ids[chunk, pl.ds(block, 1), :]
                cell = code & 7
                rows.append(jnp.where(valid, (code >> 3) - number * WINDOW, -1))
                values = chunk_of(chunks, chunk)[block].astype(F32)
                mask = [cell == k for k in range(8)]
                side = [jnp.where(m, values, 0.0).astype(BF16) for m in mask]
                side += [jnp.broadcast_to(jnp.where(m, 1.0, 0.0), (channels, LANES)).astype(BF16) for m in mask]
                sides.append(jnp.concatenate(side, axis=0))
        side = jnp.concatenate(sides, axis=1)
        row = jnp.concatenate(rows, axis=1).astype(jnp.int16)
        hot = lax.broadcasted_iota(jnp.int16, (WINDOW, len(steps) * GROUP * LANES), 0) == row
        hot = jnp.where(hot, jnp.ones((), BF16), jnp.zeros((), BF16))
        return lax.dot_general(hot, side, NT, preferred_element_type=F32)

    def one_group(group, start):
        def step(at, _):
            acc[...] += product(group, [at])
            return 0

        hops = 0
        for member in range(GROUP):
            chunk = group * GROUP + member
            first, last = places[chunk, number], places[count + chunk, number]
            need = last - first
            if len(chunks) > 1:
                need = jnp.where((first < number) | (last > number + 2), need, 0)
            hops = jnp.maximum(hops, need)
        lax.fori_loop(start, hops, step, 0)

    if len(chunks) > 1:
        acc[...] = product(0, [0, 1], static=True)
        one_group(0, 0)
    else:
        acc[...] = jnp.zeros_like(acc)

        def each(group, _):
            one_group(group, 0)
            return 0

        lax.fori_loop(0, groups, each, 0)
    return (acc[:, :LANES] / jnp.maximum(acc[:, LANES:], 1.0)).astype(BF16)


def far_kernel(count, chan, *rest):
    chunks = rest[:count]
    out, ids, acc, ends, places = rest[-5:]
    decode(chunks, ids, ends, places)
    begin = 2 * (chan[0] ^ 2) + 7
    parts = out.shape[1] // WINDOW
    for plane in range(out.shape[0]):
        for part in range(parts):
            number = lax.rem(begin + plane, 8) * parts + part
            out[plane, part * WINDOW : (part + 1) * WINDOW, :] = window_mean(number, chunks, ids, places, acc)


def near_kernel(slots, count, chan, *rest):
    chunks = rest[:count]
    far, send_pos, three, one, own, f0, f1, f2, f3, ids, acc, ends, places, planes = rest[count:]
    decode(chunks, ids, ends, places)
    partner = chan[0] ^ 2
    begin = 2 * partner + 7
    parts = far.shape[1] // WINDOW
    planes[0:4] = far[...]
    for plane in range(4, 8):
        for part in range(parts):
            number = lax.rem(begin + plane, 8) * parts + part
            planes[plane, part * WINDOW : (part + 1) * WINDOW, :] = window_mean(number, chunks, ids, places, acc)
    for out, flip in ((three, 3), (one, 1), (own, 0)):
        shift = 2 * ((chan[0] ^ flip) - partner) + 8
        if flip == 3:
            shift = shift + 2 * ((chan[0] ^ 3) & 1)
        for plane in range(out.shape[0]):
            out[plane] = planes[lax.rem(shift + plane, 8)]
    compact = []
    for side in range(2):
        hot = lax.broadcasted_iota(jnp.int32, (REACH, slots), 0) == send_pos[side : side + 1, :]
        compact.append(jnp.where(hot, 1.0, 0.0).astype(BF16))
    last_plane, first_plane = (planes.at[lax.rem(at - begin + 16, 8)] for at in (7, 8))
    for j in range(8):
        rows = slice(j * slots, (j + 1) * slots)
        to_next = mm(compact[0], last_plane[rows, :])
        to_previous = mm(compact[1], first_plane[rows, :])
        for flip, out in enumerate((f0, f1, f2, f3)):
            out[j] = jnp.where(chan[0] == flip, to_next, to_previous).astype(BF16)


def voxel_scratch(chunks, regions):
    total = chunks[0].shape[-3]
    tiles = -(-total // (ID_ROWS + 2))
    return [
        pltpu.VMEM((regions, tiles * ID_ROWS, LANES), jnp.int32),
        pltpu.VMEM((WINDOW, 2 * LANES), F32),
        pltpu.VMEM((2 * regions, LANES), jnp.int32),
        pltpu.SMEM((2 * regions, LANES), jnp.int32),
    ]


def far_voxels(chan, chunks, regions, slots, before):
    return pl.pallas_call(
        functools.partial(far_kernel, len(chunks)),
        out_shape=jax.ShapeDtypeStruct((4, 8 * slots, LANES), BF16),
        in_specs=[SMEM] + [VMEM] * len(chunks) + [pl.BlockSpec(memory_space=pl.ANY)] * len(before),
        out_specs=VMEM,
        scratch_shapes=voxel_scratch(chunks, regions),
        compiler_params=params(),
        cost_estimate=pl.CostEstimate(flops=4_000_000_000, bytes_accessed=1_200_000, transcendentals=0),
        name="far_voxels",
    )(chan, *chunks, *before)


def near_voxels(chan, chunks, regions, far, send_pos, slots):
    return pl.pallas_call(
        functools.partial(near_kernel, slots, len(chunks)),
        out_shape=[jax.ShapeDtypeStruct((planes, 8 * slots, LANES), BF16) for planes in (2, 4, 4)]
        + [jax.ShapeDtypeStruct((8, REACH, LANES), BF16)] * 4,
        in_specs=[SMEM] + [VMEM] * len(chunks) + [VMEM, VMEM],
        out_specs=[VMEM] * 7,
        scratch_shapes=voxel_scratch(chunks, regions) + [pltpu.VMEM((8, 8 * slots, LANES), BF16)],
        compiler_params=params(),
        cost_estimate=pl.CostEstimate(flops=4_000_000_000, bytes_accessed=3_000_000, transcendentals=0),
        name="near_voxels",
    )(chan, *chunks, far, send_pos)


def shared_kernel(chan, planes, out):
    begin = 2 - 2 * (chan[0] & 1)
    for plane in range(2):
        out[plane] = planes[begin + plane]


def shared_planes(chan, planes):
    return pl.pallas_call(
        shared_kernel,
        out_shape=jax.ShapeDtypeStruct((2, *planes.shape[1:]), BF16),
        in_specs=[SMEM, VMEM],
        out_specs=VMEM,
        compiler_params=pltpu.CompilerParams(vmem_limit_bytes=4 * 1024 * 1024),
        name="shared_planes",
    )(chan, planes)


def pack_kernel(conv, down, _, pack):
    for ab in range(9):
        for e in range(3):
            pack[ab, :, e * 64 : (e + 1) * 64] = conv[ab * 3 + e]
    for part in range(8):
        pack[9 + part, :, 0:128] = down[part * 16 : (part + 1) * 16, :]
        pack[9 + part, :, 128:192] = jnp.zeros((16, 64), BF16)


def pack(conv, down, before):
    return pl.pallas_call(
        pack_kernel,
        out_shape=jax.ShapeDtypeStruct((17, 16, 192), BF16),
        in_specs=[VMEM, VMEM, pl.BlockSpec(memory_space=pl.ANY)],
        out_specs=VMEM,
        compiler_params=params(),
        name="pack",
    )(conv, down, before)


def weight_kernel(chan, own, one, two, three, even, odd, down):
    every = (own, one, two, three)
    columns = lax.broadcasted_iota(jnp.int32, (192, 192), 1) ^ (chan[0] * 16)
    turn = jnp.where(lax.broadcasted_iota(jnp.int32, (192, 192), 0) == columns, 1.0, 0.0).astype(BF16)
    for out in (even, odd):
        out[...] = jnp.zeros_like(out)
    for ab in range(9):
        taps = jnp.concatenate([ref[ab] for ref in every], axis=0)
        turned = lax.dot_general(turn, taps, NT, preferred_element_type=F32)
        turned = jnp.concatenate([turned, turned], axis=1).astype(BF16)
        for e in range(3):
            for source in range(4):
                out, place = (even, odd)[source % 2], source // 2
                rows = turned[e * 64 + source * 16 : e * 64 + source * 16 + 16]
                for k in range(4):
                    piece = rows[:, (k % 2) * 64 : (k % 2) * 64 + 64]
                    column = slice(k * 64, (k + 1) * 64)
                    cell = k + e
                    if 1 <= cell <= 4:
                        row = place * 64 + (cell - 1) * 16
                        out[0, ab, row : row + 16, column] = piece
                        out[1, ab, 128 + row : 144 + row, column] = piece
                    else:
                        row = (cell // 5) * 32 + place * 16
                        out[0, ab, 128 + row : 144 + row, column] = piece
                        out[1, ab, 64 + row : 80 + row, column] = piece
    outputs = down.shape[0]
    total = jnp.zeros((outputs, 512), F32)
    rows = lax.broadcasted_iota(jnp.int32, (128, 512), 0)
    place = (rows & 7) * 64 + (rows >> 3)
    for source, ref in enumerate(every):
        part = ref[9:, :, 0:128].reshape(128, outputs)
        move = lax.broadcasted_iota(jnp.int32, (128, 512), 1) == place + source * 16
        move = jnp.where(move, 1.0, 0.0).astype(BF16)
        total += lax.dot_general(part, move, (((0,), (0,)), ((), ())), preferred_element_type=F32)
    down[...] = total.astype(BF16)


def prepare(chan, own, others, outputs):
    return pl.pallas_call(
        weight_kernel,
        out_shape=(
            jax.ShapeDtypeStruct((2, 9, 256, 256), BF16),
            jax.ShapeDtypeStruct((2, 9, 256, 256), BF16),
            jax.ShapeDtypeStruct((outputs, 512), BF16),
        ),
        in_specs=[SMEM] + [VMEM] * 4,
        out_specs=(VMEM, VMEM, VMEM),
        compiler_params=params(),
        cost_estimate=pl.CostEstimate(flops=2_000_000_000, bytes_accessed=3_000_000, transcendentals=0),
        name="prepare",
    )(chan, own, *others)


def halo_matrix():
    pick = np.zeros((256, 128), np.float32)
    for group, cell in enumerate((7, 4, 3, 0)):
        for source in range(2):
            for inner in range(16):
                pick[source * 128 + cell * 16 + inner, group * 32 + source * 16 + inner] = 1
    return pick


def pad_planes(slots, fetch, remote, hot, pick, table, padded):
    total = slots + REACH
    lane = lax.broadcasted_iota(jnp.int32, (slots, LANES), 1)
    for plane in range(4):
        edge = mm(jnp.concatenate([get(plane, slice(None)) for get in fetch], axis=1), pick[...]).astype(BF16)
        for j in range(8):
            rows = slice(j * slots, (j + 1) * slots)
            parts = [get(plane, rows) for get in fetch]
            table[plane, j, 0:slots, 0:128] = jnp.concatenate([part[:, 0:64] for part in parts], axis=1)
            table[plane, j, 0:slots, 128:256] = edge[rows]
            table[plane, j, 0:slots, 256:384] = jnp.concatenate([part[:, 64:128] for part in parts], axis=1)
    for plane in (0, 3):
        for j in range(8):
            parts = [ref[j] for ref in remote]
            table[plane, j, slots:total, 0:128] = jnp.concatenate([part[:, 0:64] for part in parts], axis=1)
            table[plane, j, slots:total, 128:256] = mm(jnp.concatenate(parts, axis=1), pick[...]).astype(BF16)
            table[plane, j, slots:total, 256:384] = jnp.concatenate([part[:, 64:128] for part in parts], axis=1)

    for plane in range(4):
        base = (0, 9, 9, 18)[plane]
        used = total if plane in (0, 3) else slots
        for jj in range(10):
            dy, j = ((-1, 7) if jj == 0 else (1, 0) if jj == 9 else (0, jj - 1))
            at = base + (dy + 1) * 3
            source = table[plane, j, 0:used, :]
            if plane in (1, 2) and dy == 0:
                own = source
            else:
                own = mm(hot[at + 1, :, 0:used], source).astype(BF16)
            below = mm(hot[at, :, 0:used], source[:, 128:256]).astype(BF16)
            above = mm(hot[at + 2, :, 0:used], source[:, 128:256]).astype(BF16)
            padded[plane, jj, :, 0:128] = own[:, 0:128]
            padded[plane, jj, :, 128:256] = jnp.where(lane < 32, below, jnp.where(lane < 96, own[:, 128:256], above))
            padded[plane, jj, :, 256:384] = own[:, 256:384]


def products(padded, weights, half, a_out, start):
    slots = padded.shape[2]
    for ab in range(9):
        left = padded[a_out + ab // 3, ab % 3 : ab % 3 + 8, :, half * 128 : half * 128 + 256]
        term = mm(left.reshape(8 * slots, 256), weights[half, ab])
        start = term if start is None else start + term
    return start


def even_kernel(slots, own, two, r0, r2, hot, pick, weights, sums, table, padded):
    fetch = [lambda plane, rows, ref=ref: ref[plane, rows, :] for ref in (own, two)]
    pad_planes(slots, fetch, (r0, r2), hot, pick, table, padded)
    for half in range(2):
        for a_out in range(2):
            sums[half, a_out] = products(padded, weights, half, a_out, None)


def odd_kernel(slots, chan, active, one, direct, passed, r1, r3, hot, pick, weights, down, sums, *rest):
    table, padded, stacked, answer = rest[4:]
    is_odd = (chan[0] & 1) == 1

    def three(plane, rows):
        first, second = direct[plane % 2, rows, :], passed[plane % 2, rows, :]
        return jnp.where(is_odd, second, first) if plane < 2 else jnp.where(is_odd, first, second)

    fetch = (lambda plane, rows: one[plane, rows, :], three)
    pad_planes(slots, fetch, (r1, r3), hot, pick, table, padded)
    alive = lax.broadcasted_iota(jnp.int32, (slots, 256), 0) < active[0]
    for half in range(2):
        for a_out in range(2):
            total_sum = products(padded, weights, half, a_out, sums[half, a_out])
            for j in range(8):
                block = jnp.where(alive, jnp.maximum(total_sum[j * slots : (j + 1) * slots], 0.0), 0.0).astype(BF16)
                for kk in range(2):
                    begin = ((j // 2) * 4 + half * 2 + kk) * slots
                    place = (a_out * 2 + j % 2) * 128
                    stacked[begin : begin + slots, place : place + 128] = block[:, kk * 128 : kk * 128 + 128]

    result = lax.dot_general(down[...], stacked[...], NT, preferred_element_type=F32)
    answer[...] = jnp.maximum(result, 0.0).astype(BF16)
    width = rest[0].shape[0]
    for flip in range(4):
        rest[flip][...] = answer[pl.ds(pl.multiple_of((chan[0] ^ flip) * width, width), width), :]


def even_sums(own, two, remote, hot, weights):
    slots = own.shape[1] // 8
    return pl.pallas_call(
        functools.partial(even_kernel, slots),
        out_shape=jax.ShapeDtypeStruct((2, 2, 8 * slots, 256), F32),
        in_specs=[VMEM] * 7,
        out_specs=VMEM,
        scratch_shapes=[
            pltpu.VMEM((4, 8, slots + REACH, 384), BF16),
            pltpu.VMEM((4, 10, slots, 384), BF16),
        ],
        compiler_params=params(),
        cost_estimate=pl.CostEstimate(flops=4_000_000_000, bytes_accessed=5_000_000, transcendentals=0),
        name="even_sums",
    )(own, two, *remote, hot, jnp.asarray(halo_matrix(), BF16), weights)


def convolve(chan, active, one, direct, passed, remote, hot, weights, down, sums):
    devices = 4
    slots = one.shape[1] // 8
    outputs = down.shape[0]
    return pl.pallas_call(
        functools.partial(odd_kernel, slots),
        out_shape=[jax.ShapeDtypeStruct((outputs // devices, 16 * slots), BF16)] * devices,
        in_specs=[SMEM] * 2 + [VMEM] * 10,
        out_specs=[VMEM] * devices,
        scratch_shapes=[
            pltpu.VMEM((4, 8, slots + REACH, 384), BF16),
            pltpu.VMEM((4, 10, slots, 384), BF16),
            pltpu.VMEM((16 * slots, 512), BF16),
            pltpu.VMEM((outputs, 16 * slots), BF16),
        ],
        compiler_params=params(),
        cost_estimate=pl.CostEstimate(flops=4_000_000_000, bytes_accessed=5_000_000, transcendentals=0),
        name="convolve",
    )(chan, active, one, direct, passed, *remote, hot, jnp.asarray(halo_matrix(), BF16), weights, down, sums)


def final_kernel(slots, chan, own, one, two, three, out, turned):
    outputs = own.shape[0]
    for flip, ref in enumerate((own, one, two, three)):
        plane = chan[0] ^ flip
        for cell in range(16):
            turned[pl.ds(plane * 16 + cell, outputs, stride=64), :] = ref[
                :, cell * slots : (cell + 1) * slots
            ].astype(F32)
    for tile in range(out.shape[1] // LANES):
        out[:, tile * LANES : (tile + 1) * LANES] = turned[tile * LANES : (tile + 1) * LANES, :].T.astype(BF16)


def finish(chan, coarse, others, slots):
    outputs = coarse.shape[0]
    return pl.pallas_call(
        functools.partial(final_kernel, slots),
        out_shape=jax.ShapeDtypeStruct((slots, outputs * 64), BF16),
        in_specs=[SMEM] + [VMEM] * 4,
        out_specs=VMEM,
        scratch_shapes=[pltpu.VMEM((outputs * 64, slots), F32)],
        compiler_params=params(),
        name="finish",
    )(chan, coarse, *others)


def links(adjacency, region, regions, chan, devices):
    slots = adjacency.shape[0]
    named = adjacency.T
    linked = named < slots * regions
    owner = jnp.where(linked, named // slots, regions + 7)
    slot = named % slots
    every = jnp.arange(slots, dtype=jnp.int32)
    steps = np.array([offset[0] for offset in OFFSETS])
    send_pos = []
    place = {}
    for step in (1, -1):
        rows = np.nonzero(steps == step)[0]
        owns = owner[rows[0] : rows[-1] + 1] == region + step
        sends = jnp.any(owns, axis=0)
        rank = jnp.sum((sends[None, :] & (every[None, :] < every[:, None])).astype(jnp.int32), axis=1)
        send_pos.append(jnp.where(sends, rank, -1))
        there = slot[rows[0] : rows[-1] + 1]
        member = jnp.any(owns[:, :, None] & (there[:, :, None] == every), axis=(0, 1))
        below = jnp.sum(
            (member[None, None, :] & (every < there[:, :, None])).astype(jnp.int32), axis=2
        )
        place[step] = jnp.where(owns, slots + below, -1)
    own = jnp.where(owner == region, slot, -1)
    same = jnp.concatenate([own[9:13], every[None, :], own[13:17]], axis=0)
    left = jnp.where(owner[0:9] == region, slot[0:9], place[-1])
    right = jnp.where(owner[17:26] == region, slot[17:26], place[1])
    first = jnp.where(chan == 0, left, same)
    last = jnp.where(chan == devices - 1, right, same)
    pos = jnp.concatenate([first, same, last], axis=0)
    hot = (pos[:, :, None] == jnp.arange(slots + REACH, dtype=jnp.int32)).astype(BF16)
    return jnp.stack(send_pos), hot


def send_faces(faces, regions, devices):
    got = []
    for flip in range(devices):
        other = (devices - 1) ^ flip
        pairs = [(r * devices + flip, (r + 1) * devices) for r in range(regions - 1)]
        pairs += [(r * devices + other, r * devices - 1) for r in range(1, regions)]
        got.append(lax.ppermute(faces[flip], ("region", "chan"), pairs))
    return got


def swap(value, flip, devices):
    return lax.ppermute(value, "chan", [(source, source ^ flip) for source in range(devices)])


def body(point_feats, destination, voxel_slot, adjacency, active_count, conv_weight, down_weight):
    regions = lax.axis_size("region")
    region = lax.axis_index("region")
    devices = lax.axis_size("chan")
    chan = lax.axis_index("chan")
    me = chan.reshape(1)
    slots = adjacency.shape[0]
    points = point_feats.shape[1]
    cells = slots * 512

    slot = voxel_slot // 512
    inside = voxel_slot % 512
    code = ((inside // 8) * slots + slot) * 8 + inside % 8
    keys, order = lax.sort(
        (destination * cells + code, jnp.arange(points, dtype=jnp.int32)), num_keys=1, is_stable=False
    )
    square = (points // LANES, LANES)
    taps = conv_weight.transpose(2, 3, 4, 0, 1).reshape(27, conv_weight.shape[0], -1)
    down = down_weight.transpose(1, 2, 3, 4, 0).reshape(-1, down_weight.shape[0])
    chunks, middle = exchange(
        point_feats, order.reshape(square), keys.reshape(square), region, regions, cells
    )
    mine = pack(taps, down, middle)
    late = mine[16, 0, 128] != 0
    theirs = [swap(mine, flip, devices) for flip in (1, 2, 3)]
    even, odd, down = prepare(me, mine, theirs, down_weight.shape[0])
    adjacency = jnp.where(late, 0, adjacency)

    send_pos, hot = links(adjacency, region, regions, chan, devices)
    far = far_voxels(me, chunks, regions, slots, (down, hot, send_pos))
    from_two = swap(far, 2, devices)
    near_three, near_one, near, *faces = near_voxels(me, chunks, regions, far, send_pos, slots)
    from_three = swap(near_three, 3, devices)
    from_one = swap(near_one, 1, devices)
    passed = swap(shared_planes(me, from_two), 1, devices)
    remote = send_faces(faces, regions, devices)
    sums = even_sums(near, from_two, remote[0::2], hot, even)
    coarse = convolve(me, active_count, from_one, from_three, passed, remote[1::2], hot, odd, down, sums)
    back = [swap(coarse[flip], flip, devices) for flip in (1, 2, 3)]
    return finish(me, coarse[0], back, slots)


def solution(mesh):
    return jax.shard_map(
        body,
        mesh=mesh,
        in_specs=(
            P("chan", "region"),
            P("region"),
            P("region"),
            P("region", None),
            P("region"),
            P("chan", None, None, None, None),
            P(None, "chan", None, None, None),
        ),
        out_specs=P("region", "chan"),
        check_vma=False,
    )
```

```python
import functools

import jax
import jax.numpy as jnp
import numpy as np
from jax import lax
from jax.experimental import pallas as pl
from jax.experimental.pallas import tpu as pltpu
from jax.sharding import PartitionSpec as P

OFFSETS = [
    (first, second, third)
    for first in (-1, 0, 1)
    for second in (-1, 0, 1)
    for third in (-1, 0, 1)
    if (first, second, third) != (0, 0, 0)
]
LANES = 128
REACH = 16
F32 = jnp.float32
BF16 = jnp.bfloat16
NT = (((1,), (1,)), ((), ()))
VMEM = pl.BlockSpec(memory_space=pltpu.VMEM)
SMEM = pl.BlockSpec(memory_space=pltpu.SMEM)


def mm(a, b):
    return jnp.dot(a, b, preferred_element_type=F32)


def params():
    return pltpu.CompilerParams(vmem_limit_bytes=24 * 1024 * 1024)


ID_ROWS = 16
GROUP = 8


def one_hot_columns(depth, stack, wanted, channels=16):
    count = wanted.shape[0]
    width = count * LANES
    wanted = jnp.concatenate([wanted[i : i + 1] for i in range(count)], axis=1)
    low = (wanted & (depth - 1)).astype(jnp.int16)
    top = wanted // depth
    hot = lax.broadcasted_iota(jnp.int16, (depth, width), 0) == low
    hot = jnp.where(hot, jnp.ones((), BF16), jnp.zeros((), BF16))
    found = mm(stack[...], hot)
    picked = jnp.zeros((channels, width), F32)
    for part in range(stack.shape[0] // channels):
        picked = jnp.where(top == part, found[part * channels : (part + 1) * channels], picked)
    return picked.astype(BF16)


def fill_stack(depth, feats, stack):
    channels, points = feats.shape
    for part in range(points // depth):
        stack[part * channels : (part + 1) * channels, :] = feats[:, part * depth : (part + 1) * depth]


def put_codes(out, blocks, tiles, tile, rows):
    if rows.shape[0] < ID_ROWS:
        rows = jnp.concatenate([rows, jnp.zeros((ID_ROWS - rows.shape[0], LANES), jnp.int32)], axis=0)
    out[blocks + tile] = (rows >> 8).astype(F32).astype(BF16)
    out[blocks + tiles + tile] = (rows & 255).astype(F32).astype(BF16)


def permute_kernel(depth, width, cells, feats, order, keys, out, stack):
    channels, points = feats.shape
    fill_stack(depth, feats, stack)
    regions = out.shape[0]
    blocks = points // regions // LANES
    tiles = (out.shape[1] - blocks) // 2
    count = width // LANES

    def step(at, _):
        picked = one_hot_columns(depth, stack, order[pl.ds(at * count, count), :])
        for part in range(count):
            tile = at * count + part
            out[tile // blocks, tile % blocks] = picked[:, part * LANES : (part + 1) * LANES]
        return 0

    lax.fori_loop(0, points // width, step, 0)
    for target in range(regions):
        for tile in range(tiles):
            begin = target * blocks + tile * ID_ROWS
            rows = min(ID_ROWS, blocks - tile * ID_ROWS)
            put_codes(out.at[target], blocks, tiles, tile, lax.rem(keys[begin : begin + rows, :], cells))


def permute(feats, order, keys, regions, cells):
    channels, points = feats.shape
    depth, width = 512, 1024
    blocks = points // regions // LANES
    tiles = -(-blocks // ID_ROWS)
    return pl.pallas_call(
        functools.partial(permute_kernel, depth, width, cells),
        out_shape=jax.ShapeDtypeStruct((regions, blocks + 2 * tiles, channels, LANES), BF16),
        in_specs=[VMEM] * 3,
        out_specs=VMEM,
        scratch_shapes=[pltpu.VMEM((points // depth * channels, depth), BF16)],
        compiler_params=params(),
        name="permute",
    )(feats, order, keys)


def rotated(rows):
    before = jnp.concatenate([rows[-1:], rows[:-1]], axis=0)
    return jnp.concatenate([before[:, LANES // 2 :], rows[:, : LANES // 2]], axis=1)


def piece_kernel(depth, cells, flips, region, feats, order, keys, *rest):
    outs = rest[-1 - len(flips) : -1]
    stack = rest[-1]
    fill_stack(depth, feats, stack)
    tiles = 1
    blocks = outs[0].shape[0] - 2 * tiles
    count = 8
    for flip, out in zip(flips, outs):
        begin = pl.multiple_of((region[0] ^ flip) * blocks, 8)
        wanted = rotated(order[pl.ds(begin, blocks), :])
        for step in range(blocks // count):
            picked = one_hot_columns(depth, stack, wanted[step * count : (step + 1) * count])
            for part in range(count):
                out[step * count + part] = picked[:, part * LANES : (part + 1) * LANES]
        put_codes(out, blocks, tiles, 0, rotated(lax.rem(keys[pl.ds(begin, blocks), :], cells)))


def permute_piece(flips, region, feats, order, keys, regions, cells, before=()):
    channels, points = feats.shape
    depth = 512
    blocks = points // regions // LANES
    return pl.pallas_call(
        functools.partial(piece_kernel, depth, cells, flips),
        out_shape=[jax.ShapeDtypeStruct((blocks + 2, channels, LANES), BF16)] * len(flips),
        in_specs=[SMEM] + [VMEM] * 3 + [pl.BlockSpec(memory_space=pl.ANY)] * len(before),
        out_specs=[VMEM] * len(flips),
        scratch_shapes=[pltpu.VMEM((points // depth * channels, depth), BF16)],
        compiler_params=params(),
        cost_estimate=pl.CostEstimate(flops=2_000_000_000, bytes_accessed=1_000_000, transcendentals=0),
        name="permute_piece",
    )(region, feats, order, keys, *before)


def exchange(feats, order, keys, region, regions, cells):
    blocks = feats.shape[1] // regions // LANES
    if regions != GROUP or blocks != ID_ROWS:
        moved = permute(feats, order, keys, regions, cells)
        return [lax.all_to_all(moved, "region", 0, 0, tiled=True)], moved

    def send(values, flips):
        pairs = [[(source, source ^ flip) for source in range(regions)] for flip in flips]
        return [lax.ppermute(value, "region", pair) for value, pair in zip(values, pairs)]

    at = region.reshape(1)
    made = []
    got = []
    for number, flips in enumerate(((6, 7), (4, 5), (2, 3, 1, 0))):
        before = [values[0] for values in made[-1:]] + (got[number - 2] if number >= 2 else [])
        values = permute_piece(flips, at, feats, order, keys, regions, cells, before)
        made.append(values)
        sent = sum(flip != 0 for flip in flips)
        got.append(send(values[:sent], flips[:sent]) + list(values[sent:]))
    return [chunk for some in got for chunk in some], made[1][0]


WINDOW = 256


def chunk_of(chunks, number):
    return chunks[0].at[number] if len(chunks) == 1 else chunks[number]


def decode(chunks, ids, ends, places):
    count, padded_blocks, _ = ids.shape
    tiles = padded_blocks // ID_ROWS
    blocks = chunk_of(chunks, 0).shape[0] - 2 * tiles
    bounds = lax.broadcasted_iota(jnp.int32, (ID_ROWS, LANES), 1) * (WINDOW * 8)
    row = lax.broadcasted_iota(jnp.int32, (ID_ROWS, LANES), 0)
    for chunk in range(count):
        first = jnp.zeros((1, LANES), jnp.int32)
        last = jnp.zeros((1, LANES), jnp.int32)
        for tile in range(tiles):
            upper = chunk_of(chunks, chunk)[blocks + tile].astype(F32)
            lower = chunk_of(chunks, chunk)[blocks + tiles + tile].astype(F32)
            code = (upper * 256.0 + lower).astype(jnp.int32)
            ids[chunk, tile * ID_ROWS : (tile + 1) * ID_ROWS, :] = code
            real = row + tile * ID_ROWS < blocks
            passed = real & (code[:, LANES - 1 :] < bounds)
            head = code[:, 0:1]
            if len(chunks) > 1:
                last += jnp.where(head[0:1] < bounds[0:1] + WINDOW * 8, 1, 0)
                head = jnp.where(row[:, 0:1] == 0, code[:, LANES // 2 : LANES // 2 + 1], head)
            begun = real & (head < bounds + WINDOW * 8)
            first += jnp.sum(jnp.where(passed, 1, 0), axis=0, keepdims=True)
            last += jnp.sum(jnp.where(begun, 1, 0), axis=0, keepdims=True)
        ends[chunk : chunk + 1, :] = first
        ends[count + chunk : count + chunk + 1, :] = last
    pltpu.sync_copy(ends, places)


def window_mean(number, chunks, ids, places, acc):
    count, padded_blocks, _ = ids.shape
    channels = chunk_of(chunks, 0).shape[1]
    groups = count // GROUP
    blocks = chunk_of(chunks, 0).shape[0] - 2 * (padded_blocks // ID_ROWS)

    lane = lax.broadcasted_iota(jnp.int32, (1, LANES), 1)

    def product(group, steps, static=False):
        sides = []
        rows = []
        for at in steps:
            for member in range(GROUP):
                chunk = group * GROUP + member
                if static:
                    block = number + at
                else:
                    block = places[chunk, number] + at
                    valid = block < places[count + chunk, number]
                if len(chunks) == 1:
                    block = jnp.minimum(block, blocks - 1)
                else:
                    begin = jnp.where(block == 0, LANES // 2, 0)
                    end = jnp.where(block == blocks, LANES // 2, LANES)
                    if not static:
                        end = jnp.where(valid & ((block < number) | (block > number + 1)), end, 0)
                    valid = (lane >= begin) & (lane < end)
                    block = block & (blocks - 1)
                code = ids[chunk, pl.ds(block, 1), :]
                cell = code & 7
                rows.append(jnp.where(valid, (code >> 3) - number * WINDOW, -1))
                values = chunk_of(chunks, chunk)[block].astype(F32)
                mask = [cell == k for k in range(8)]
                side = [jnp.where(m, values, 0.0).astype(BF16) for m in mask]
                side += [jnp.broadcast_to(jnp.where(m, 1.0, 0.0), (channels, LANES)).astype(BF16) for m in mask]
                sides.append(jnp.concatenate(side, axis=0))
        side = jnp.concatenate(sides, axis=1)
        row = jnp.concatenate(rows, axis=1).astype(jnp.int16)
        hot = lax.broadcasted_iota(jnp.int16, (WINDOW, len(steps) * GROUP * LANES), 0) == row
        hot = jnp.where(hot, jnp.ones((), BF16), jnp.zeros((), BF16))
        return lax.dot_general(hot, side, NT, preferred_element_type=F32)

    def one_group(group, start):
        def step(at, _):
            acc[...] += product(group, [at])
            return 0

        hops = 0
        for member in range(GROUP):
            chunk = group * GROUP + member
            first, last = places[chunk, number], places[count + chunk, number]
            need = last - first
            if len(chunks) > 1:
                need = jnp.where((first < number) | (last > number + 2), need, 0)
            hops = jnp.maximum(hops, need)
        lax.fori_loop(start, hops, step, 0)

    if len(chunks) > 1:
        acc[...] = product(0, [0, 1], static=True)
        one_group(0, 0)
    else:
        acc[...] = jnp.zeros_like(acc)

        def each(group, _):
            one_group(group, 0)
            return 0

        lax.fori_loop(0, groups, each, 0)
    return (acc[:, :LANES] / jnp.maximum(acc[:, LANES:], 1.0)).astype(BF16)


def far_kernel(count, chan, *rest):
    chunks = rest[:count]
    out, ids, acc, ends, places = rest[-5:]
    decode(chunks, ids, ends, places)
    begin = 2 * (chan[0] ^ 2) + 7
    parts = out.shape[1] // WINDOW
    for plane in range(out.shape[0]):
        for part in range(parts):
            number = lax.rem(begin + plane, 8) * parts + part
            out[plane, part * WINDOW : (part + 1) * WINDOW, :] = window_mean(number, chunks, ids, places, acc)


def near_kernel(slots, count, chan, *rest):
    chunks = rest[:count]
    far, send_pos, three, one, own, f0, f1, f2, f3, ids, acc, ends, places, planes = rest[count:]
    decode(chunks, ids, ends, places)
    partner = chan[0] ^ 2
    begin = 2 * partner + 7
    parts = far.shape[1] // WINDOW
    planes[0:4] = far[...]
    for plane in range(4, 8):
        for part in range(parts):
            number = lax.rem(begin + plane, 8) * parts + part
            planes[plane, part * WINDOW : (part + 1) * WINDOW, :] = window_mean(number, chunks, ids, places, acc)
    for out, flip in ((three, 3), (one, 1), (own, 0)):
        shift = 2 * ((chan[0] ^ flip) - partner) + 8
        if flip == 3:
            shift = shift + 2 * ((chan[0] ^ 3) & 1)
        for plane in range(out.shape[0]):
            out[plane] = planes[lax.rem(shift + plane, 8)]
    compact = []
    for side in range(2):
        hot = lax.broadcasted_iota(jnp.int32, (REACH, slots), 0) == send_pos[side : side + 1, :]
        compact.append(jnp.where(hot, 1.0, 0.0).astype(BF16))
    last_plane, first_plane = (planes.at[lax.rem(at - begin + 16, 8)] for at in (7, 8))
    for j in range(8):
        rows = slice(j * slots, (j + 1) * slots)
        to_next = mm(compact[0], last_plane[rows, :])
        to_previous = mm(compact[1], first_plane[rows, :])
        for flip, out in enumerate((f0, f1, f2, f3)):
            out[j] = jnp.where(chan[0] == flip, to_next, to_previous).astype(BF16)


def voxel_scratch(chunks, regions):
    total = chunks[0].shape[-3]
    tiles = -(-total // (ID_ROWS + 2))
    return [
        pltpu.VMEM((regions, tiles * ID_ROWS, LANES), jnp.int32),
        pltpu.VMEM((WINDOW, 2 * LANES), F32),
        pltpu.VMEM((2 * regions, LANES), jnp.int32),
        pltpu.SMEM((2 * regions, LANES), jnp.int32),
    ]


def far_voxels(chan, chunks, regions, slots, before):
    return pl.pallas_call(
        functools.partial(far_kernel, len(chunks)),
        out_shape=jax.ShapeDtypeStruct((4, 8 * slots, LANES), BF16),
        in_specs=[SMEM] + [VMEM] * len(chunks) + [pl.BlockSpec(memory_space=pl.ANY)] * len(before),
        out_specs=VMEM,
        scratch_shapes=voxel_scratch(chunks, regions),
        compiler_params=params(),
        cost_estimate=pl.CostEstimate(flops=4_000_000_000, bytes_accessed=1_200_000, transcendentals=0),
        name="far_voxels",
    )(chan, *chunks, *before)


def near_voxels(chan, chunks, regions, far, send_pos, slots):
    return pl.pallas_call(
        functools.partial(near_kernel, slots, len(chunks)),
        out_shape=[jax.ShapeDtypeStruct((planes, 8 * slots, LANES), BF16) for planes in (2, 4, 4)]
        + [jax.ShapeDtypeStruct((8, REACH, LANES), BF16)] * 4,
        in_specs=[SMEM] + [VMEM] * len(chunks) + [VMEM, VMEM],
        out_specs=[VMEM] * 7,
        scratch_shapes=voxel_scratch(chunks, regions) + [pltpu.VMEM((8, 8 * slots, LANES), BF16)],
        compiler_params=params(),
        cost_estimate=pl.CostEstimate(flops=4_000_000_000, bytes_accessed=3_000_000, transcendentals=0),
        name="near_voxels",
    )(chan, *chunks, far, send_pos)


def shared_kernel(chan, planes, out):
    begin = 2 - 2 * (chan[0] & 1)
    for plane in range(2):
        out[plane] = planes[begin + plane]


def shared_planes(chan, planes):
    return pl.pallas_call(
        shared_kernel,
        out_shape=jax.ShapeDtypeStruct((2, *planes.shape[1:]), BF16),
        in_specs=[SMEM, VMEM],
        out_specs=VMEM,
        compiler_params=pltpu.CompilerParams(vmem_limit_bytes=4 * 1024 * 1024),
        name="shared_planes",
    )(chan, planes)


def pack_kernel(conv, down, _, pack):
    for ab in range(9):
        for e in range(3):
            pack[ab, :, e * 64 : (e + 1) * 64] = conv[ab * 3 + e]
    for part in range(8):
        pack[9 + part, :, 0:128] = down[part * 16 : (part + 1) * 16, :]
        pack[9 + part, :, 128:192] = jnp.zeros((16, 64), BF16)


def pack(conv, down, before):
    return pl.pallas_call(
        pack_kernel,
        out_shape=jax.ShapeDtypeStruct((17, 16, 192), BF16),
        in_specs=[VMEM, VMEM, pl.BlockSpec(memory_space=pl.ANY)],
        out_specs=VMEM,
        compiler_params=params(),
        name="pack",
    )(conv, down, before)


def weight_kernel(chan, own, one, two, three, even, odd, down):
    every = (own, one, two, three)
    columns = lax.broadcasted_iota(jnp.int32, (192, 192), 1) ^ (chan[0] * 16)
    turn = jnp.where(lax.broadcasted_iota(jnp.int32, (192, 192), 0) == columns, 1.0, 0.0).astype(BF16)
    for out in (even, odd):
        out[...] = jnp.zeros_like(out)
    for ab in range(9):
        taps = jnp.concatenate([ref[ab] for ref in every], axis=0)
        turned = lax.dot_general(turn, taps, NT, preferred_element_type=F32)
        turned = jnp.concatenate([turned, turned], axis=1).astype(BF16)
        for e in range(3):
            for source in range(4):
                out, place = (even, odd)[source % 2], source // 2
                rows = turned[e * 64 + source * 16 : e * 64 + source * 16 + 16]
                for k in range(4):
                    piece = rows[:, (k % 2) * 64 : (k % 2) * 64 + 64]
                    column = slice(k * 64, (k + 1) * 64)
                    cell = k + e
                    if 1 <= cell <= 4:
                        row = place * 64 + (cell - 1) * 16
                        out[0, ab, row : row + 16, column] = piece
                        out[1, ab, 128 + row : 144 + row, column] = piece
                    else:
                        row = (cell // 5) * 32 + place * 16
                        out[0, ab, 128 + row : 144 + row, column] = piece
                        out[1, ab, 64 + row : 80 + row, column] = piece
    outputs = down.shape[0]
    total = jnp.zeros((outputs, 512), F32)
    rows = lax.broadcasted_iota(jnp.int32, (128, 512), 0)
    place = (rows & 7) * 64 + (rows >> 3)
    for source, ref in enumerate(every):
        part = ref[9:, :, 0:128].reshape(128, outputs)
        move = lax.broadcasted_iota(jnp.int32, (128, 512), 1) == place + source * 16
        move = jnp.where(move, 1.0, 0.0).astype(BF16)
        total += lax.dot_general(part, move, (((0,), (0,)), ((), ())), preferred_element_type=F32)
    down[...] = total.astype(BF16)


def prepare(chan, own, others, outputs):
    return pl.pallas_call(
        weight_kernel,
        out_shape=(
            jax.ShapeDtypeStruct((2, 9, 256, 256), BF16),
            jax.ShapeDtypeStruct((2, 9, 256, 256), BF16),
            jax.ShapeDtypeStruct((outputs, 512), BF16),
        ),
        in_specs=[SMEM] + [VMEM] * 4,
        out_specs=(VMEM, VMEM, VMEM),
        compiler_params=params(),
        cost_estimate=pl.CostEstimate(flops=2_000_000_000, bytes_accessed=3_000_000, transcendentals=0),
        name="prepare",
    )(chan, own, *others)


def halo_matrix():
    pick = np.zeros((256, 128), np.float32)
    for group, cell in enumerate((7, 4, 3, 0)):
        for source in range(2):
            for inner in range(16):
                pick[source * 128 + cell * 16 + inner, group * 32 + source * 16 + inner] = 1
    return pick


def pad_planes(slots, fetch, remote, hot, pick, table, padded):
    total = slots + REACH
    lane = lax.broadcasted_iota(jnp.int32, (slots, LANES), 1)
    for plane in range(4):
        edge = mm(jnp.concatenate([get(plane, slice(None)) for get in fetch], axis=1), pick[...]).astype(BF16)
        for j in range(8):
            rows = slice(j * slots, (j + 1) * slots)
            parts = [get(plane, rows) for get in fetch]
            table[plane, j, 0:slots, 0:128] = jnp.concatenate([part[:, 0:64] for part in parts], axis=1)
            table[plane, j, 0:slots, 128:256] = edge[rows]
            table[plane, j, 0:slots, 256:384] = jnp.concatenate([part[:, 64:128] for part in parts], axis=1)
    for plane in (0, 3):
        for j in range(8):
            parts = [ref[j] for ref in remote]
            table[plane, j, slots:total, 0:128] = jnp.concatenate([part[:, 0:64] for part in parts], axis=1)
            table[plane, j, slots:total, 128:256] = mm(jnp.concatenate(parts, axis=1), pick[...]).astype(BF16)
            table[plane, j, slots:total, 256:384] = jnp.concatenate([part[:, 64:128] for part in parts], axis=1)

    for plane in range(4):
        base = (0, 9, 9, 18)[plane]
        used = total if plane in (0, 3) else slots
        for jj in range(10):
            dy, j = ((-1, 7) if jj == 0 else (1, 0) if jj == 9 else (0, jj - 1))
            at = base + (dy + 1) * 3
            source = table[plane, j, 0:used, :]
            if plane in (1, 2) and dy == 0:
                own = source
            else:
                own = mm(hot[at + 1, :, 0:used], source).astype(BF16)
            below = mm(hot[at, :, 0:used], source[:, 128:256]).astype(BF16)
            above = mm(hot[at + 2, :, 0:used], source[:, 128:256]).astype(BF16)
            padded[plane, jj, :, 0:128] = own[:, 0:128]
            padded[plane, jj, :, 128:256] = jnp.where(lane < 32, below, jnp.where(lane < 96, own[:, 128:256], above))
            padded[plane, jj, :, 256:384] = own[:, 256:384]


def products(padded, weights, half, a_out, start):
    slots = padded.shape[2]
    for ab in range(9):
        left = padded[a_out + ab // 3, ab % 3 : ab % 3 + 8, :, half * 128 : half * 128 + 256]
        term = mm(left.reshape(8 * slots, 256), weights[half, ab])
        start = term if start is None else start + term
    return start


def even_kernel(slots, own, two, r0, r2, hot, pick, weights, sums, table, padded):
    fetch = [lambda plane, rows, ref=ref: ref[plane, rows, :] for ref in (own, two)]
    pad_planes(slots, fetch, (r0, r2), hot, pick, table, padded)
    for half in range(2):
        for a_out in range(2):
            sums[half, a_out] = products(padded, weights, half, a_out, None)


def odd_kernel(slots, chan, active, one, direct, passed, r1, r3, hot, pick, weights, down, sums, *rest):
    table, padded, stacked, answer = rest[4:]
    is_odd = (chan[0] & 1) == 1

    def three(plane, rows):
        first, second = direct[plane % 2, rows, :], passed[plane % 2, rows, :]
        return jnp.where(is_odd, second, first) if plane < 2 else jnp.where(is_odd, first, second)

    fetch = (lambda plane, rows: one[plane, rows, :], three)
    pad_planes(slots, fetch, (r1, r3), hot, pick, table, padded)
    alive = lax.broadcasted_iota(jnp.int32, (slots, 256), 0) < active[0]
    for half in range(2):
        for a_out in range(2):
            total_sum = products(padded, weights, half, a_out, sums[half, a_out])
            for j in range(8):
                block = jnp.where(alive, jnp.maximum(total_sum[j * slots : (j + 1) * slots], 0.0), 0.0).astype(BF16)
                for kk in range(2):
                    begin = ((j // 2) * 4 + half * 2 + kk) * slots
                    place = (a_out * 2 + j % 2) * 128
                    stacked[begin : begin + slots, place : place + 128] = block[:, kk * 128 : kk * 128 + 128]

    result = lax.dot_general(down[...], stacked[...], NT, preferred_element_type=F32)
    answer[...] = jnp.maximum(result, 0.0).astype(BF16)
    width = rest[0].shape[0]
    for flip in range(4):
        rest[flip][...] = answer[pl.ds(pl.multiple_of((chan[0] ^ flip) * width, width), width), :]


def even_sums(own, two, remote, hot, weights):
    slots = own.shape[1] // 8
    return pl.pallas_call(
        functools.partial(even_kernel, slots),
        out_shape=jax.ShapeDtypeStruct((2, 2, 8 * slots, 256), F32),
        in_specs=[VMEM] * 7,
        out_specs=VMEM,
        scratch_shapes=[
            pltpu.VMEM((4, 8, slots + REACH, 384), BF16),
            pltpu.VMEM((4, 10, slots, 384), BF16),
        ],
        compiler_params=params(),
        cost_estimate=pl.CostEstimate(flops=4_000_000_000, bytes_accessed=5_000_000, transcendentals=0),
        name="even_sums",
    )(own, two, *remote, hot, jnp.asarray(halo_matrix(), BF16), weights)


def convolve(chan, active, one, direct, passed, remote, hot, weights, down, sums):
    devices = 4
    slots = one.shape[1] // 8
    outputs = down.shape[0]
    return pl.pallas_call(
        functools.partial(odd_kernel, slots),
        out_shape=[jax.ShapeDtypeStruct((outputs // devices, 16 * slots), BF16)] * devices,
        in_specs=[SMEM] * 2 + [VMEM] * 10,
        out_specs=[VMEM] * devices,
        scratch_shapes=[
            pltpu.VMEM((4, 8, slots + REACH, 384), BF16),
            pltpu.VMEM((4, 10, slots, 384), BF16),
            pltpu.VMEM((16 * slots, 512), BF16),
            pltpu.VMEM((outputs, 16 * slots), BF16),
        ],
        compiler_params=params(),
        cost_estimate=pl.CostEstimate(flops=4_000_000_000, bytes_accessed=5_000_000, transcendentals=0),
        name="convolve",
    )(chan, active, one, direct, passed, *remote, hot, jnp.asarray(halo_matrix(), BF16), weights, down, sums)


def final_kernel(slots, chan, own, one, two, three, out, turned):
    outputs = own.shape[0]
    for flip, ref in enumerate((own, one, two, three)):
        plane = chan[0] ^ flip
        for cell in range(16):
            turned[pl.ds(plane * 16 + cell, outputs, stride=64), :] = ref[
                :, cell * slots : (cell + 1) * slots
            ].astype(F32)
    for tile in range(out.shape[1] // LANES):
        out[:, tile * LANES : (tile + 1) * LANES] = turned[tile * LANES : (tile + 1) * LANES, :].T.astype(BF16)


def finish(chan, coarse, others, slots):
    outputs = coarse.shape[0]
    return pl.pallas_call(
        functools.partial(final_kernel, slots),
        out_shape=jax.ShapeDtypeStruct((slots, outputs * 64), BF16),
        in_specs=[SMEM] + [VMEM] * 4,
        out_specs=VMEM,
        scratch_shapes=[pltpu.VMEM((outputs * 64, slots), F32)],
        compiler_params=params(),
        name="finish",
    )(chan, coarse, *others)


def link_kernel(regions, place_of, named, _, send_pos, hot):
    slots = named.shape[1]
    region, chan = place_of[0], place_of[1]
    names = named[...]
    owner = jnp.where(names < slots * regions, names >> (slots.bit_length() - 1), regions + 7)
    slot = names & (slots - 1)
    row = lax.broadcasted_iota(jnp.int32, (slots, slots), 0)
    earlier = jnp.where(row < lax.broadcasted_iota(jnp.int32, (slots, slots), 1), 1.0, 0.0).astype(BF16)
    far = {}
    for number, (step, begin) in enumerate(((1, 17), (-1, 0))):
        numbers = range(begin, begin + 9)
        owns = {n: jnp.where(owner[n : n + 1] == region + step, 1.0, 0.0) for n in numbers}
        sends = functools.reduce(jnp.maximum, owns.values())
        rank = mm(jnp.broadcast_to(sends, (16, slots)).astype(BF16), earlier)[0:1]
        send_pos[number : number + 1, :] = jnp.where(sends > 0.0, rank, -1.0).astype(jnp.int32)
        member = jnp.zeros((slots, 1), F32)
        for n in numbers:
            hit = jnp.where(row == slot[n : n + 1], owns[n], 0.0)
            member = jnp.maximum(member, jnp.max(hit, axis=1, keepdims=True))
        for n in numbers:
            below = jnp.sum(jnp.where(row < slot[n : n + 1], member, 0.0), axis=0, keepdims=True)
            far[n] = jnp.where(owns[n] > 0.0, slots + below, -1.0).astype(jnp.int32)
    every = lax.broadcasted_iota(jnp.int32, (1, slots), 1)
    own = {n: jnp.where(owner[n : n + 1] == region, slot[n : n + 1], -1) for n in range(26)}
    same = [own[n] for n in range(9, 13)] + [every] + [own[n] for n in range(13, 17)]
    left = [jnp.maximum(own[n], far[n]) for n in range(0, 9)]
    right = [jnp.maximum(own[n], far[n]) for n in range(17, 26)]
    first = [jnp.where(chan == 0, *both) for both in zip(left, same)]
    last = [jnp.where(chan == 3, *both) for both in zip(right, same)]
    entry = lax.broadcasted_iota(jnp.int32, (LANES, slots), 0)
    for number, pos in enumerate(first + same + last):
        turned = jnp.where(entry == pos, 1.0, 0.0).T.astype(BF16)
        hot[number] = turned[:, : slots + REACH]


def links(adjacency, region, regions, chan, before):
    slots = adjacency.shape[0]
    return pl.pallas_call(
        functools.partial(link_kernel, regions),
        out_shape=(
            jax.ShapeDtypeStruct((2, slots), jnp.int32),
            jax.ShapeDtypeStruct((27, slots, slots + REACH), BF16),
        ),
        in_specs=[SMEM, VMEM, pl.BlockSpec(memory_space=pl.ANY)],
        out_specs=(VMEM, VMEM),
        compiler_params=params(),
        name="links",
    )(jnp.stack([region, chan]), adjacency.T, before)


def send_faces(faces, regions, devices):
    got = []
    for flip in range(devices):
        other = (devices - 1) ^ flip
        pairs = [(r * devices + flip, (r + 1) * devices) for r in range(regions - 1)]
        pairs += [(r * devices + other, r * devices - 1) for r in range(1, regions)]
        got.append(lax.ppermute(faces[flip], ("region", "chan"), pairs))
    return got


def swap(value, flip, devices):
    return lax.ppermute(value, "chan", [(source, source ^ flip) for source in range(devices)])


def body(point_feats, destination, voxel_slot, adjacency, active_count, conv_weight, down_weight):
    regions = lax.axis_size("region")
    region = lax.axis_index("region")
    devices = lax.axis_size("chan")
    chan = lax.axis_index("chan")
    me = chan.reshape(1)
    slots = adjacency.shape[0]
    points = point_feats.shape[1]
    cells = slots * 512

    slot = voxel_slot // 512
    inside = voxel_slot % 512
    code = ((inside // 8) * slots + slot) * 8 + inside % 8
    keys, order = lax.sort(
        (destination * cells + code, jnp.arange(points, dtype=jnp.int32)), num_keys=1, is_stable=False
    )
    square = (points // LANES, LANES)
    taps = conv_weight.transpose(2, 3, 4, 0, 1).reshape(27, conv_weight.shape[0], -1)
    down = down_weight.transpose(1, 2, 3, 4, 0).reshape(-1, down_weight.shape[0])
    chunks, middle = exchange(
        point_feats, order.reshape(square), keys.reshape(square), region, regions, cells
    )
    mine = pack(taps, down, middle)
    theirs = [swap(mine, flip, devices) for flip in (1, 2, 3)]
    even, odd, down = prepare(me, mine, theirs, down_weight.shape[0])
    send_pos, hot = links(adjacency, region, regions, chan, middle)
    far = far_voxels(me, chunks, regions, slots, (down, hot, send_pos))
    from_two = swap(far, 2, devices)
    near_three, near_one, near, *faces = near_voxels(me, chunks, regions, far, send_pos, slots)
    from_three = swap(near_three, 3, devices)
    from_one = swap(near_one, 1, devices)
    passed = swap(shared_planes(me, from_two), 1, devices)
    remote = send_faces(faces, regions, devices)
    sums = even_sums(near, from_two, remote[0::2], hot, even)
    coarse = convolve(me, active_count, from_one, from_three, passed, remote[1::2], hot, odd, down, sums)
    back = [swap(coarse[flip], flip, devices) for flip in (1, 2, 3)]
    return finish(me, coarse[0], back, slots)


def solution(mesh):
    return jax.shard_map(
        body,
        mesh=mesh,
        in_specs=(
            P("chan", "region"),
            P("region"),
            P("region"),
            P("region", None),
            P("region"),
            P("chan", None, None, None, None),
            P(None, "chan", None, None, None),
        ),
        out_specs=P("region", "chan"),
        check_vma=False,
    )
```

```python
import functools

import jax
import jax.numpy as jnp
import numpy as np
from jax import lax
from jax.experimental import pallas as pl
from jax.experimental.pallas import tpu as pltpu
from jax.sharding import PartitionSpec as P

OFFSETS = [
    (first, second, third)
    for first in (-1, 0, 1)
    for second in (-1, 0, 1)
    for third in (-1, 0, 1)
    if (first, second, third) != (0, 0, 0)
]
LANES = 128
REACH = 16
F32 = jnp.float32
BF16 = jnp.bfloat16
NT = (((1,), (1,)), ((), ()))
VMEM = pl.BlockSpec(memory_space=pltpu.VMEM)
SMEM = pl.BlockSpec(memory_space=pltpu.SMEM)


def mm(a, b):
    return jnp.dot(a, b, preferred_element_type=F32)


def params():
    return pltpu.CompilerParams(vmem_limit_bytes=24 * 1024 * 1024)


ID_ROWS = 16
GROUP = 8


def one_hot_columns(depth, stack, wanted, channels=16):
    count = wanted.shape[0]
    width = count * LANES
    wanted = jnp.concatenate([wanted[i : i + 1] for i in range(count)], axis=1)
    low = (wanted & (depth - 1)).astype(jnp.int16)
    top = wanted // depth
    hot = lax.broadcasted_iota(jnp.int16, (depth, width), 0) == low
    hot = jnp.where(hot, jnp.ones((), BF16), jnp.zeros((), BF16))
    found = mm(stack[...], hot)
    picked = jnp.zeros((channels, width), F32)
    for part in range(stack.shape[0] // channels):
        picked = jnp.where(top == part, found[part * channels : (part + 1) * channels], picked)
    return picked.astype(BF16)


def fill_stack(depth, feats, stack):
    channels, points = feats.shape
    for part in range(points // depth):
        stack[part * channels : (part + 1) * channels, :] = feats[:, part * depth : (part + 1) * depth]


def put_codes(out, blocks, tiles, tile, rows):
    if rows.shape[0] < ID_ROWS:
        rows = jnp.concatenate([rows, jnp.zeros((ID_ROWS - rows.shape[0], LANES), jnp.int32)], axis=0)
    out[blocks + tile] = (rows >> 8).astype(F32).astype(BF16)
    out[blocks + tiles + tile] = (rows & 255).astype(F32).astype(BF16)


def permute_kernel(depth, width, cells, feats, order, keys, out, stack):
    channels, points = feats.shape
    fill_stack(depth, feats, stack)
    regions = out.shape[0]
    blocks = points // regions // LANES
    tiles = (out.shape[1] - blocks) // 2
    count = width // LANES

    def step(at, _):
        picked = one_hot_columns(depth, stack, order[pl.ds(at * count, count), :])
        for part in range(count):
            tile = at * count + part
            out[tile // blocks, tile % blocks] = picked[:, part * LANES : (part + 1) * LANES]
        return 0

    lax.fori_loop(0, points // width, step, 0)
    for target in range(regions):
        for tile in range(tiles):
            begin = target * blocks + tile * ID_ROWS
            rows = min(ID_ROWS, blocks - tile * ID_ROWS)
            put_codes(out.at[target], blocks, tiles, tile, lax.rem(keys[begin : begin + rows, :], cells))


def permute(feats, order, keys, regions, cells):
    channels, points = feats.shape
    depth, width = 512, 1024
    blocks = points // regions // LANES
    tiles = -(-blocks // ID_ROWS)
    return pl.pallas_call(
        functools.partial(permute_kernel, depth, width, cells),
        out_shape=jax.ShapeDtypeStruct((regions, blocks + 2 * tiles, channels, LANES), BF16),
        in_specs=[VMEM] * 3,
        out_specs=VMEM,
        scratch_shapes=[pltpu.VMEM((points // depth * channels, depth), BF16)],
        compiler_params=params(),
        name="permute",
    )(feats, order, keys)


def rotated(rows):
    before = jnp.concatenate([rows[-1:], rows[:-1]], axis=0)
    return jnp.concatenate([before[:, LANES // 2 :], rows[:, : LANES // 2]], axis=1)


def piece_kernel(depth, cells, flips, region, feats, order, keys, *rest):
    outs = rest[-1 - len(flips) : -1]
    stack = rest[-1]
    fill_stack(depth, feats, stack)
    tiles = 1
    blocks = outs[0].shape[0] - 2 * tiles
    count = 8
    for flip, out in zip(flips, outs):
        begin = pl.multiple_of((region[0] ^ flip) * blocks, 8)
        wanted = rotated(order[pl.ds(begin, blocks), :])
        for step in range(blocks // count):
            picked = one_hot_columns(depth, stack, wanted[step * count : (step + 1) * count])
            for part in range(count):
                out[step * count + part] = picked[:, part * LANES : (part + 1) * LANES]
        put_codes(out, blocks, tiles, 0, rotated(lax.rem(keys[pl.ds(begin, blocks), :], cells)))


def permute_piece(flips, region, feats, order, keys, regions, cells, before=()):
    channels, points = feats.shape
    depth = 512
    blocks = points // regions // LANES
    return pl.pallas_call(
        functools.partial(piece_kernel, depth, cells, flips),
        out_shape=[jax.ShapeDtypeStruct((blocks + 2, channels, LANES), BF16)] * len(flips),
        in_specs=[SMEM] + [VMEM] * 3 + [pl.BlockSpec(memory_space=pl.ANY)] * len(before),
        out_specs=[VMEM] * len(flips),
        scratch_shapes=[pltpu.VMEM((points // depth * channels, depth), BF16)],
        compiler_params=params(),
        cost_estimate=pl.CostEstimate(flops=2_000_000_000, bytes_accessed=1_000_000, transcendentals=0),
        name="permute_piece",
    )(region, feats, order, keys, *before)


def exchange(feats, order, keys, region, regions, cells):
    blocks = feats.shape[1] // regions // LANES
    if regions != GROUP or blocks != ID_ROWS:
        moved = permute(feats, order, keys, regions, cells)
        return [lax.all_to_all(moved, "region", 0, 0, tiled=True)], moved

    def send(values, flips):
        pairs = [[(source, source ^ flip) for source in range(regions)] for flip in flips]
        return [lax.ppermute(value, "region", pair) for value, pair in zip(values, pairs)]

    at = region.reshape(1)
    made = []
    got = []
    for number, flips in enumerate(((6, 7), (4, 5), (2, 3, 1, 0))):
        before = [values[0] for values in made[-1:]] + (got[number - 2] if number >= 2 else [])
        values = permute_piece(flips, at, feats, order, keys, regions, cells, before)
        made.append(values)
        sent = sum(flip != 0 for flip in flips)
        got.append(send(values[:sent], flips[:sent]) + list(values[sent:]))
    return [chunk for some in got for chunk in some], made[1][0]


WINDOW = 256


def chunk_of(chunks, number):
    return chunks[0].at[number] if len(chunks) == 1 else chunks[number]


def decode(chunks, ids, ends, places):
    count, padded_blocks, _ = ids.shape
    tiles = padded_blocks // ID_ROWS
    blocks = chunk_of(chunks, 0).shape[0] - 2 * tiles
    bounds = lax.broadcasted_iota(jnp.int32, (ID_ROWS, LANES), 1) * (WINDOW * 8)
    row = lax.broadcasted_iota(jnp.int32, (ID_ROWS, LANES), 0)
    for chunk in range(count):
        first = jnp.zeros((1, LANES), jnp.int32)
        last = jnp.zeros((1, LANES), jnp.int32)
        for tile in range(tiles):
            upper = chunk_of(chunks, chunk)[blocks + tile].astype(F32)
            lower = chunk_of(chunks, chunk)[blocks + tiles + tile].astype(F32)
            code = (upper * 256.0 + lower).astype(jnp.int32)
            ids[chunk, tile * ID_ROWS : (tile + 1) * ID_ROWS, :] = code
            real = row + tile * ID_ROWS < blocks
            passed = real & (code[:, LANES - 1 :] < bounds)
            head = code[:, 0:1]
            if len(chunks) > 1:
                last += jnp.where(head[0:1] < bounds[0:1] + WINDOW * 8, 1, 0)
                head = jnp.where(row[:, 0:1] == 0, code[:, LANES // 2 : LANES // 2 + 1], head)
            begun = real & (head < bounds + WINDOW * 8)
            first += jnp.sum(jnp.where(passed, 1, 0), axis=0, keepdims=True)
            last += jnp.sum(jnp.where(begun, 1, 0), axis=0, keepdims=True)
        ends[chunk : chunk + 1, :] = first
        ends[count + chunk : count + chunk + 1, :] = last
    pltpu.sync_copy(ends, places)


def window_mean(number, chunks, ids, places, acc):
    count, padded_blocks, _ = ids.shape
    channels = chunk_of(chunks, 0).shape[1]
    groups = count // GROUP
    blocks = chunk_of(chunks, 0).shape[0] - 2 * (padded_blocks // ID_ROWS)

    lane = lax.broadcasted_iota(jnp.int32, (1, LANES), 1)

    def product(group, steps, static=False):
        sides = []
        rows = []
        for at in steps:
            for member in range(GROUP):
                chunk = group * GROUP + member
                if static:
                    block = number + at
                else:
                    block = places[chunk, number] + at
                    valid = block < places[count + chunk, number]
                if len(chunks) == 1:
                    block = jnp.minimum(block, blocks - 1)
                else:
                    begin = jnp.where(block == 0, LANES // 2, 0)
                    end = jnp.where(block == blocks, LANES // 2, LANES)
                    if not static:
                        end = jnp.where(valid & ((block < number) | (block > number + 1)), end, 0)
                    valid = (lane >= begin) & (lane < end)
                    block = block & (blocks - 1)
                code = ids[chunk, pl.ds(block, 1), :]
                cell = code & 7
                rows.append(jnp.where(valid, (code >> 3) - number * WINDOW, -1))
                values = chunk_of(chunks, chunk)[block].astype(F32)
                mask = [cell == k for k in range(8)]
                side = [jnp.where(m, values, 0.0).astype(BF16) for m in mask]
                side += [jnp.broadcast_to(jnp.where(m, 1.0, 0.0), (channels, LANES)).astype(BF16) for m in mask]
                sides.append(jnp.concatenate(side, axis=0))
        side = jnp.concatenate(sides, axis=1)
        row = jnp.concatenate(rows, axis=1).astype(jnp.int16)
        hot = lax.broadcasted_iota(jnp.int16, (WINDOW, len(steps) * GROUP * LANES), 0) == row
        hot = jnp.where(hot, jnp.ones((), BF16), jnp.zeros((), BF16))
        return lax.dot_general(hot, side, NT, preferred_element_type=F32)

    def one_group(group, start):
        def step(at, _):
            acc[...] += product(group, [at])
            return 0

        hops = 0
        for member in range(GROUP):
            chunk = group * GROUP + member
            first, last = places[chunk, number], places[count + chunk, number]
            need = last - first
            if len(chunks) > 1:
                need = jnp.where((first < number) | (last > number + 2), need, 0)
            hops = jnp.maximum(hops, need)
        lax.fori_loop(start, hops, step, 0)

    if len(chunks) > 1:
        acc[...] = product(0, [0, 1], static=True)
        one_group(0, 0)
    else:
        acc[...] = jnp.zeros_like(acc)

        def each(group, _):
            one_group(group, 0)
            return 0

        lax.fori_loop(0, groups, each, 0)
    return (acc[:, :LANES] / jnp.maximum(acc[:, LANES:], 1.0)).astype(BF16)


def far_kernel(count, chan, *rest):
    chunks = rest[:count]
    out, ids, acc, ends, places = rest[-5:]
    decode(chunks, ids, ends, places)
    begin = 2 * (chan[0] ^ 2) + 7
    parts = out.shape[1] // WINDOW
    for plane in range(out.shape[0]):
        for part in range(parts):
            number = lax.rem(begin + plane, 8) * parts + part
            out[plane, part * WINDOW : (part + 1) * WINDOW, :] = window_mean(number, chunks, ids, places, acc)


def near_kernel(slots, count, chan, *rest):
    chunks = rest[:count]
    far, send_pos, three, one, own, f0, f1, f2, f3, ids, acc, ends, places, planes = rest[count:]
    decode(chunks, ids, ends, places)
    partner = chan[0] ^ 2
    begin = 2 * partner + 7
    parts = far.shape[1] // WINDOW
    planes[0:4] = far[...]
    for plane in range(4, 8):
        for part in range(parts):
            number = lax.rem(begin + plane, 8) * parts + part
            planes[plane, part * WINDOW : (part + 1) * WINDOW, :] = window_mean(number, chunks, ids, places, acc)
    for out, flip in ((three, 3), (one, 1), (own, 0)):
        shift = 2 * ((chan[0] ^ flip) - partner) + 8
        if flip == 3:
            shift = shift + 2 * ((chan[0] ^ 3) & 1)
        for plane in range(out.shape[0]):
            out[plane] = planes[lax.rem(shift + plane, 8)]
    compact = []
    for side in range(2):
        hot = lax.broadcasted_iota(jnp.int32, (REACH, slots), 0) == send_pos[side : side + 1, :]
        compact.append(jnp.where(hot, 1.0, 0.0).astype(BF16))
    last_plane, first_plane = (planes.at[lax.rem(at - begin + 16, 8)] for at in (7, 8))
    for j in range(8):
        rows = slice(j * slots, (j + 1) * slots)
        to_next = mm(compact[0], last_plane[rows, :])
        to_previous = mm(compact[1], first_plane[rows, :])
        for flip, out in enumerate((f0, f1, f2, f3)):
            out[j] = jnp.where(chan[0] == flip, to_next, to_previous).astype(BF16)


def voxel_scratch(chunks, regions):
    total = chunks[0].shape[-3]
    tiles = -(-total // (ID_ROWS + 2))
    return [
        pltpu.VMEM((regions, tiles * ID_ROWS, LANES), jnp.int32),
        pltpu.VMEM((WINDOW, 2 * LANES), F32),
        pltpu.VMEM((2 * regions, LANES), jnp.int32),
        pltpu.SMEM((2 * regions, LANES), jnp.int32),
    ]


def far_voxels(chan, chunks, regions, slots, before):
    return pl.pallas_call(
        functools.partial(far_kernel, len(chunks)),
        out_shape=jax.ShapeDtypeStruct((4, 8 * slots, LANES), BF16),
        in_specs=[SMEM] + [VMEM] * len(chunks) + [pl.BlockSpec(memory_space=pl.ANY)] * len(before),
        out_specs=VMEM,
        scratch_shapes=voxel_scratch(chunks, regions),
        compiler_params=params(),
        cost_estimate=pl.CostEstimate(flops=4_000_000_000, bytes_accessed=1_200_000, transcendentals=0),
        name="far_voxels",
    )(chan, *chunks, *before)


def near_voxels(chan, chunks, regions, far, send_pos, slots):
    return pl.pallas_call(
        functools.partial(near_kernel, slots, len(chunks)),
        out_shape=[jax.ShapeDtypeStruct((planes, 8 * slots, LANES), BF16) for planes in (2, 4, 4)]
        + [jax.ShapeDtypeStruct((8, REACH, LANES), BF16)] * 4,
        in_specs=[SMEM] + [VMEM] * len(chunks) + [VMEM, VMEM],
        out_specs=[VMEM] * 7,
        scratch_shapes=voxel_scratch(chunks, regions) + [pltpu.VMEM((8, 8 * slots, LANES), BF16)],
        compiler_params=params(),
        cost_estimate=pl.CostEstimate(flops=4_000_000_000, bytes_accessed=3_000_000, transcendentals=0),
        name="near_voxels",
    )(chan, *chunks, far, send_pos)


def shared_kernel(chan, planes, out):
    begin = 2 - 2 * (chan[0] & 1)
    for plane in range(2):
        out[plane] = planes[begin + plane]


def shared_planes(chan, planes):
    return pl.pallas_call(
        shared_kernel,
        out_shape=jax.ShapeDtypeStruct((2, *planes.shape[1:]), BF16),
        in_specs=[SMEM, VMEM],
        out_specs=VMEM,
        compiler_params=pltpu.CompilerParams(vmem_limit_bytes=4 * 1024 * 1024),
        name="shared_planes",
    )(chan, planes)


def pack_kernel(conv, down, _, pack):
    for ab in range(9):
        for e in range(3):
            pack[ab, :, e * 64 : (e + 1) * 64] = conv[ab * 3 + e]
    for part in range(8):
        pack[9 + part, :, 0:128] = down[part * 16 : (part + 1) * 16, :]
        pack[9 + part, :, 128:192] = jnp.zeros((16, 64), BF16)


def pack(conv, down, before):
    return pl.pallas_call(
        pack_kernel,
        out_shape=jax.ShapeDtypeStruct((17, 16, 192), BF16),
        in_specs=[VMEM, VMEM, pl.BlockSpec(memory_space=pl.ANY)],
        out_specs=VMEM,
        compiler_params=params(),
        name="pack",
    )(conv, down, before)


def weight_kernel(chan, own, one, two, three, even, odd, down):
    every = (own, one, two, three)
    columns = lax.broadcasted_iota(jnp.int32, (192, 192), 1) ^ (chan[0] * 16)
    turn = jnp.where(lax.broadcasted_iota(jnp.int32, (192, 192), 0) == columns, 1.0, 0.0).astype(BF16)
    for out in (even, odd):
        out[...] = jnp.zeros_like(out)
    for ab in range(9):
        taps = jnp.concatenate([ref[ab] for ref in every], axis=0)
        turned = lax.dot_general(turn, taps, NT, preferred_element_type=F32)
        turned = jnp.concatenate([turned, turned], axis=1).astype(BF16)
        for e in range(3):
            for source in range(4):
                out, place = (even, odd)[source % 2], source // 2
                rows = turned[e * 64 + source * 16 : e * 64 + source * 16 + 16]
                for k in range(4):
                    piece = rows[:, (k % 2) * 64 : (k % 2) * 64 + 64]
                    column = slice(k * 64, (k + 1) * 64)
                    cell = k + e
                    if 1 <= cell <= 4:
                        row = place * 64 + (cell - 1) * 16
                        out[0, ab, row : row + 16, column] = piece
                        out[1, ab, 128 + row : 144 + row, column] = piece
                    else:
                        row = (cell // 5) * 32 + place * 16
                        out[0, ab, 128 + row : 144 + row, column] = piece
                        out[1, ab, 64 + row : 80 + row, column] = piece
    outputs = down.shape[0]
    total = jnp.zeros((outputs, 512), F32)
    rows = lax.broadcasted_iota(jnp.int32, (128, 512), 0)
    place = (rows & 7) * 64 + (rows >> 3)
    for source, ref in enumerate(every):
        part = ref[9:, :, 0:128].reshape(128, outputs)
        move = lax.broadcasted_iota(jnp.int32, (128, 512), 1) == place + source * 16
        move = jnp.where(move, 1.0, 0.0).astype(BF16)
        total += lax.dot_general(part, move, (((0,), (0,)), ((), ())), preferred_element_type=F32)
    down[...] = total.astype(BF16)


def prepare(chan, own, others, outputs):
    return pl.pallas_call(
        weight_kernel,
        out_shape=(
            jax.ShapeDtypeStruct((2, 9, 256, 256), BF16),
            jax.ShapeDtypeStruct((2, 9, 256, 256), BF16),
            jax.ShapeDtypeStruct((outputs, 512), BF16),
        ),
        in_specs=[SMEM] + [VMEM] * 4,
        out_specs=(VMEM, VMEM, VMEM),
        compiler_params=params(),
        cost_estimate=pl.CostEstimate(flops=2_000_000_000, bytes_accessed=3_000_000, transcendentals=0),
        name="prepare",
    )(chan, own, *others)


def halo_matrix():
    pick = np.zeros((256, 128), np.float32)
    for group, cell in enumerate((7, 4, 3, 0)):
        for source in range(2):
            for inner in range(16):
                pick[source * 128 + cell * 16 + inner, group * 32 + source * 16 + inner] = 1
    return pick


def pad_planes(slots, fetch, remote, hot, pick, table, padded):
    total = slots + REACH
    lane = lax.broadcasted_iota(jnp.int32, (slots, LANES), 1)
    for plane in range(4):
        edge = mm(jnp.concatenate([get(plane, slice(None)) for get in fetch], axis=1), pick[...]).astype(BF16)
        for j in range(8):
            rows = slice(j * slots, (j + 1) * slots)
            parts = [get(plane, rows) for get in fetch]
            table[plane, j, 0:slots, 0:128] = jnp.concatenate([part[:, 0:64] for part in parts], axis=1)
            table[plane, j, 0:slots, 128:256] = edge[rows]
            table[plane, j, 0:slots, 256:384] = jnp.concatenate([part[:, 64:128] for part in parts], axis=1)
    for plane in (0, 3):
        for j in range(8):
            parts = [ref[j] for ref in remote]
            table[plane, j, slots:total, 0:128] = jnp.concatenate([part[:, 0:64] for part in parts], axis=1)
            table[plane, j, slots:total, 128:256] = mm(jnp.concatenate(parts, axis=1), pick[...]).astype(BF16)
            table[plane, j, slots:total, 256:384] = jnp.concatenate([part[:, 64:128] for part in parts], axis=1)

    for plane in range(4):
        base = (0, 9, 9, 18)[plane]
        used = total if plane in (0, 3) else slots
        for jj in range(10):
            dy, j = ((-1, 7) if jj == 0 else (1, 0) if jj == 9 else (0, jj - 1))
            at = base + (dy + 1) * 3
            source = table[plane, j, 0:used, :]
            if plane in (1, 2) and dy == 0:
                own = source
            else:
                own = mm(hot[at + 1, :, 0:used], source).astype(BF16)
            below = mm(hot[at, :, 0:used], source[:, 128:256]).astype(BF16)
            above = mm(hot[at + 2, :, 0:used], source[:, 128:256]).astype(BF16)
            padded[plane, jj, :, 0:128] = own[:, 0:128]
            padded[plane, jj, :, 128:256] = jnp.where(lane < 32, below, jnp.where(lane < 96, own[:, 128:256], above))
            padded[plane, jj, :, 256:384] = own[:, 256:384]


def products(padded, weights, half, a_out, start):
    slots = padded.shape[2]
    for ab in range(9):
        left = padded[a_out + ab // 3, ab % 3 : ab % 3 + 8, :, half * 128 : half * 128 + 256]
        term = mm(left.reshape(8 * slots, 256), weights[half, ab])
        start = term if start is None else start + term
    return start


def even_kernel(slots, own, two, r0, r2, hot, pick, weights, sums, table, padded):
    fetch = [lambda plane, rows, ref=ref: ref[plane, rows, :] for ref in (own, two)]
    pad_planes(slots, fetch, (r0, r2), hot, pick, table, padded)
    for half in range(2):
        for a_out in range(2):
            sums[half, a_out] = products(padded, weights, half, a_out, None)


def odd_kernel(slots, chan, active, one, direct, passed, r1, r3, hot, pick, weights, down, sums, *rest):
    table, padded, stacked, answer = rest[4:]
    is_odd = (chan[0] & 1) == 1

    def three(plane, rows):
        first, second = direct[plane % 2, rows, :], passed[plane % 2, rows, :]
        return jnp.where(is_odd, second, first) if plane < 2 else jnp.where(is_odd, first, second)

    fetch = (lambda plane, rows: one[plane, rows, :], three)
    pad_planes(slots, fetch, (r1, r3), hot, pick, table, padded)
    alive = lax.broadcasted_iota(jnp.int32, (slots, 256), 0) < active[0]
    for half in range(2):
        for a_out in range(2):
            total_sum = products(padded, weights, half, a_out, sums[half, a_out])
            for j in range(8):
                block = jnp.where(alive, jnp.maximum(total_sum[j * slots : (j + 1) * slots], 0.0), 0.0).astype(BF16)
                for kk in range(2):
                    begin = ((j // 2) * 4 + half * 2 + kk) * slots
                    place = (a_out * 2 + j % 2) * 128
                    stacked[begin : begin + slots, place : place + 128] = block[:, kk * 128 : kk * 128 + 128]

    result = lax.dot_general(down[...], stacked[...], NT, preferred_element_type=F32)
    answer[...] = jnp.maximum(result, 0.0).astype(BF16)
    width = rest[0].shape[0]
    for flip in range(4):
        rest[flip][...] = answer[pl.ds(pl.multiple_of((chan[0] ^ flip) * width, width), width), :]


def even_sums(own, two, remote, hot, weights):
    slots = own.shape[1] // 8
    return pl.pallas_call(
        functools.partial(even_kernel, slots),
        out_shape=jax.ShapeDtypeStruct((2, 2, 8 * slots, 256), F32),
        in_specs=[VMEM] * 7,
        out_specs=VMEM,
        scratch_shapes=[
            pltpu.VMEM((4, 8, slots + REACH, 384), BF16),
            pltpu.VMEM((4, 10, slots, 384), BF16),
        ],
        compiler_params=params(),
        cost_estimate=pl.CostEstimate(flops=4_000_000_000, bytes_accessed=5_000_000, transcendentals=0),
        name="even_sums",
    )(own, two, *remote, hot, jnp.asarray(halo_matrix(), BF16), weights)


def convolve(chan, active, one, direct, passed, remote, hot, weights, down, sums):
    devices = 4
    slots = one.shape[1] // 8
    outputs = down.shape[0]
    return pl.pallas_call(
        functools.partial(odd_kernel, slots),
        out_shape=[jax.ShapeDtypeStruct((outputs // devices, 16 * slots), BF16)] * devices,
        in_specs=[SMEM] * 2 + [VMEM] * 10,
        out_specs=[VMEM] * devices,
        scratch_shapes=[
            pltpu.VMEM((4, 8, slots + REACH, 384), BF16),
            pltpu.VMEM((4, 10, slots, 384), BF16),
            pltpu.VMEM((16 * slots, 512), BF16),
            pltpu.VMEM((outputs, 16 * slots), BF16),
        ],
        compiler_params=params(),
        cost_estimate=pl.CostEstimate(flops=4_000_000_000, bytes_accessed=5_000_000, transcendentals=0),
        name="convolve",
    )(chan, active, one, direct, passed, *remote, hot, jnp.asarray(halo_matrix(), BF16), weights, down, sums)


def final_kernel(slots, chan, own, one, two, three, out, turned):
    outputs = own.shape[0]
    for flip, ref in enumerate((own, one, two, three)):
        plane = chan[0] ^ flip
        for cell in range(16):
            turned[pl.ds(plane * 16 + cell, outputs, stride=64), :] = ref[
                :, cell * slots : (cell + 1) * slots
            ].astype(F32)
    for tile in range(out.shape[1] // LANES):
        out[:, tile * LANES : (tile + 1) * LANES] = turned[tile * LANES : (tile + 1) * LANES, :].T.astype(BF16)


def finish(chan, coarse, others, slots):
    outputs = coarse.shape[0]
    return pl.pallas_call(
        functools.partial(final_kernel, slots),
        out_shape=jax.ShapeDtypeStruct((slots, outputs * 64), BF16),
        in_specs=[SMEM] + [VMEM] * 4,
        out_specs=VMEM,
        scratch_shapes=[pltpu.VMEM((outputs * 64, slots), F32)],
        compiler_params=params(),
        name="finish",
    )(chan, coarse, *others)


def link_kernel(regions, place_of, named, _, send_pos, hot):
    slots = named.shape[1]
    region, chan = place_of[0], place_of[1]
    names = named[...]
    owner = jnp.where(names < slots * regions, names >> (slots.bit_length() - 1), regions + 7)
    slot = names & (slots - 1)
    row = lax.broadcasted_iota(jnp.int32, (slots, slots), 0)
    earlier = jnp.where(row < lax.broadcasted_iota(jnp.int32, (slots, slots), 1), 1.0, 0.0).astype(BF16)
    far = {}
    for number, (step, begin) in enumerate(((1, 17), (-1, 0))):
        numbers = range(begin, begin + 9)
        owns = {n: jnp.where(owner[n : n + 1] == region + step, 1.0, 0.0) for n in numbers}
        sends = functools.reduce(jnp.maximum, owns.values())
        rank = mm(jnp.broadcast_to(sends, (16, slots)).astype(BF16), earlier)[0:1]
        send_pos[number : number + 1, :] = jnp.where(sends > 0.0, rank, -1.0).astype(jnp.int32)
        member = jnp.zeros((slots, 1), F32)
        for n in numbers:
            hit = jnp.where(row == slot[n : n + 1], owns[n], 0.0)
            member = jnp.maximum(member, jnp.max(hit, axis=1, keepdims=True))
        for n in numbers:
            below = jnp.sum(jnp.where(row < slot[n : n + 1], member, 0.0), axis=0, keepdims=True)
            far[n] = jnp.where(owns[n] > 0.0, slots + below, -1.0).astype(jnp.int32)
    every = lax.broadcasted_iota(jnp.int32, (1, slots), 1)
    own = {n: jnp.where(owner[n : n + 1] == region, slot[n : n + 1], -1) for n in range(26)}
    same = [own[n] for n in range(9, 13)] + [every] + [own[n] for n in range(13, 17)]
    left = [jnp.maximum(own[n], far[n]) for n in range(0, 9)]
    right = [jnp.maximum(own[n], far[n]) for n in range(17, 26)]
    first = [jnp.where(chan == 0, *both) for both in zip(left, same)]
    last = [jnp.where(chan == 3, *both) for both in zip(right, same)]
    entry = lax.broadcasted_iota(jnp.int32, (LANES, slots), 0)
    for number, pos in enumerate(first + same + last):
        turned = jnp.where(entry == pos, 1.0, 0.0).T.astype(BF16)
        hot[number] = turned[:, : slots + REACH]


def links(adjacency, region, regions, chan, before):
    slots = adjacency.shape[0]
    return pl.pallas_call(
        functools.partial(link_kernel, regions),
        out_shape=(
            jax.ShapeDtypeStruct((2, slots), jnp.int32),
            jax.ShapeDtypeStruct((27, slots, slots + REACH), BF16),
        ),
        in_specs=[SMEM, VMEM, pl.BlockSpec(memory_space=pl.ANY)],
        out_specs=(VMEM, VMEM),
        compiler_params=params(),
        name="links",
    )(jnp.stack([region, chan]), adjacency.T, before)


def send_faces(faces, regions, devices):
    got = []
    for flip in range(devices):
        other = (devices - 1) ^ flip
        pairs = [(r * devices + flip, (r + 1) * devices) for r in range(regions - 1)]
        pairs += [(r * devices + other, r * devices - 1) for r in range(1, regions)]
        got.append(lax.ppermute(faces[flip], ("region", "chan"), pairs))
    return got


def swap(value, flip, devices):
    return lax.ppermute(value, "chan", [(source, source ^ flip) for source in range(devices)])


def body(point_feats, destination, voxel_slot, adjacency, active_count, conv_weight, down_weight):
    regions = lax.axis_size("region")
    region = lax.axis_index("region")
    devices = lax.axis_size("chan")
    chan = lax.axis_index("chan")
    me = chan.reshape(1)
    slots = adjacency.shape[0]
    points = point_feats.shape[1]
    cells = slots * 512

    slot = voxel_slot // 512
    inside = voxel_slot % 512
    code = ((inside // 8) * slots + slot) * 8 + inside % 8
    keys, order = lax.sort(
        (destination * cells + code, jnp.arange(points, dtype=jnp.int32)), num_keys=1, is_stable=False
    )
    square = (points // LANES, LANES)
    taps = conv_weight.transpose(2, 3, 4, 0, 1).reshape(27, conv_weight.shape[0], -1)
    down = down_weight.transpose(1, 2, 3, 4, 0).reshape(-1, down_weight.shape[0])
    chunks, middle = exchange(
        point_feats, order.reshape(square), keys.reshape(square), region, regions, cells
    )
    mine = pack(taps, down, middle)
    theirs = [swap(mine, flip, devices) for flip in (1, 2, 3)]
    even, odd, down = prepare(me, mine, theirs, down_weight.shape[0])
    send_pos, hot = links(adjacency, region, regions, chan, middle)
    far = far_voxels(me, chunks, regions, slots, (hot, send_pos, *theirs))
    from_two = swap(far, 2, devices)
    near_three, near_one, near, *faces = near_voxels(me, chunks, regions, far, send_pos, slots)
    from_three = swap(near_three, 3, devices)
    from_one = swap(near_one, 1, devices)
    passed = swap(shared_planes(me, from_two), 1, devices)
    remote = send_faces(faces, regions, devices)
    sums = even_sums(near, from_two, remote[0::2], hot, even)
    coarse = convolve(me, active_count, from_one, from_three, passed, remote[1::2], hot, odd, down, sums)
    back = [swap(coarse[flip], flip, devices) for flip in (1, 2, 3)]
    return finish(me, coarse[0], back, slots)


def solution(mesh):
    return jax.shard_map(
        body,
        mesh=mesh,
        in_specs=(
            P("chan", "region"),
            P("region"),
            P("region"),
            P("region", None),
            P("region"),
            P("chan", None, None, None, None),
            P(None, "chan", None, None, None),
        ),
        out_specs=P("region", "chan"),
        check_vma=False,
    )
```
